256 devices in a mesh: dp: 2 (over core), expert: 128 (over z, x, y).
Axes of the slice: x: 4, y: 4, z: 8, core: 2. Of those that a mesh axis runs over, the one named last changes fastest.
Arguments:
- tokens: bfloat16 [32768, 1024], P(('dp', 'expert')), may hold values from -6 to 6
- cotangent: bfloat16 [32768, 1024], P(('dp', 'expert')), may hold values from -6 to 6
- route: int32 [32768, 8], P(('dp', 'expert')), may hold values from 0 to 127, as said below
- numer: int32 [32768, 8], P(('dp', 'expert')), may hold values from 1 to 64
- w_gate: bfloat16 [128, 1024, 384], P('expert'), may hold values from -0.1875 to 0.1875
- w_up: bfloat16 [128, 1024, 384], P('expert'), may hold values from -0.1875 to 0.1875
- w_down: bfloat16 [128, 384, 1024], P('expert'), may hold values from -0.3125 to 0.3125
Outputs:
- output: bfloat16 [32768, 1024], P(('dp', 'expert'))
- grad_tokens: bfloat16 [32768, 1024], P(('dp', 'expert'))
- grad_gate: float32 [128, 1024, 384], P('expert', 'dp')
- grad_up: float32 [128, 1024, 384], P('expert', 'dp')
- grad_down: float32 [128, 384, 1024], P('expert', None, 'dp')
The draws below stay inside these ranges and needn't reach their ends.
Inputs may be any that keep to these rules, and one draw needn't show every extreme that they name: `route`: each row names 8 different experts. Two experts, the same on every device, are each named by exactly 16 of the 128 rows of every device; every other expert is named by at most 8 rows of one device, and some expert reaches 8 on every device.
All inputs are finite; a program needn't handle non-finite values.
Results may differ from the reference program's by a relative error of at most 0.015.
Values may be sent and summed in bfloat16 or wider, within the bound.
No kernel may reach another device: no remote copies, remote signals or barrier semaphores. Data moves between devices by JAX's collectives and lax.ppermute only.
A program may use at most 128 MiB of HBM per device.

```python
import jax
import jax.numpy as jnp
from jax import lax

D = 1024
FF = 384
TOP = 8
TOK_DEV = 128
E = 128
TOKENS = 32768
HOT_ROWS = 16
COLD = 8
N_DP = 2
N_EXPERT = 128


def draw_route(key, part):
    key = jax.random.fold_in(key, 11)
    key_perm, key_blocks = jax.random.split(key)
    perm = jax.random.permutation(key_perm, E).astype(jnp.int32)
    hot_a = perm[0]
    hot_b = perm[1]
    cold = perm[2:]
    column = jnp.arange(TOP, dtype=jnp.int32)

    def block(block_key):
        key_a, key_b, key_c = jax.random.split(block_key, 3)
        cold_order = cold[jax.random.permutation(key_a, E - 2)]
        shuffled = jax.random.permutation(key_b, TOK_DEV).astype(jnp.int32)
        place = jnp.zeros((TOK_DEV,), jnp.int32).at[shuffled].set(jnp.arange(TOK_DEV, dtype=jnp.int32))
        has_a = place < HOT_ROWS
        has_b = place >= TOK_DEV - HOT_ROWS
        nhot = has_a.astype(jnp.int32) + has_b.astype(jnp.int32)
        ncold = TOP - nhot
        start = jnp.cumsum(ncold) - ncold
        cold_ids = cold_order[(start[:, None] + column[None, :] - nhot[:, None]) % (E - 2)]
        hot_first = jnp.where(has_a, hot_a, hot_b)
        row = jnp.where(column[None, :] == 0, hot_first[:, None], hot_b)
        row = jnp.where(column[None, :] < nhot[:, None], row, cold_ids)
        shift = jax.random.randint(key_c, (TOK_DEV,), 0, TOP)
        cols = (column[None, :] + shift[:, None]) % TOP
        return jnp.take_along_axis(row, cols, axis=1)
    keys = jax.random.split(key_blocks, TOKENS // TOK_DEV)
    return jax.vmap(block)(keys).reshape(TOKENS, TOP).astype(jnp.int32)


def with_ends(values, own_key, least, high):
    longest = values.shape.index(max(values.shape))
    spots = []
    for shift in (0, 1):
        where = [jax.random.randint(jax.random.fold_in(own_key, axis), (), 0, length) for axis, length in enumerate(values.shape)]
        where[longest] = (where[longest] + shift) % values.shape[longest]
        spots.append(tuple(where))
    return values.at[spots[0]].set(least).at[spots[1]].set(high)


def levels(stream_key, extent, cuts, smallest, largest):
    level, own = 1.0, jax.random.fold_in(stream_key, 6)
    for dim, blocks in cuts:
        heights = jnp.exp(jax.random.uniform(jax.random.fold_in(own, dim), (blocks,), jnp.float32, smallest / len(cuts), largest / len(cuts)))
        level = level * jnp.repeat(heights, extent[dim] // blocks).reshape([-1 if axis == dim else 1 for axis in range(len(extent))])
    return level


def bell_draw(key, shape, spread, most, pieces=(), held_as=jnp.bfloat16):
    entries = spread * jax.random.normal(key, shape, jnp.float32)
    if pieces:
        entries = entries * levels(key, shape, pieces, -0.22, 0.18)
    return jnp.clip(entries, -most, most).astype(held_as)


def setup_inputs(seed: int = 0) -> dict:
    key_list = jax.random.split(jax.random.key(seed), 8)
    return {
        "tokens": bell_draw(key_list[0], (TOKENS, D), 1.0, 6.0, ((0, 256),)),
        "cotangent": bell_draw(key_list[1], (TOKENS, D), 1.0, 6.0, ((0, 256),)),
        "route": draw_route(jax.random.fold_in(key_list[7], 71), 0),
        "numer": with_ends(jax.random.randint(key_list[3], (TOKENS, TOP), 1, 65), jax.random.fold_in(key_list[3], 1), 1, 64).astype(jnp.int32),
        "w_gate": bell_draw(key_list[4], (E, D, FF), D ** -0.5, 0.1875, ((0, 128),)),
        "w_up": bell_draw(key_list[5], (E, D, FF), D ** -0.5, 0.1875, ((0, 128),)),
        "w_down": bell_draw(key_list[6], (E, FF, D), FF ** -0.5, 0.3125, ((0, 128),)),
    }


def silu_slope(pre):
    sig = jax.nn.sigmoid(pre)
    return sig * (1.0 + pre * (1.0 - sig))


def expert_pass(rows_in, rows_cot, gate_w, up_w, down_w):
    pre_gate = jnp.dot(rows_in, gate_w, preferred_element_type=jnp.float32)
    pre_up = jnp.dot(rows_in, up_w, preferred_element_type=jnp.float32)
    active = jax.nn.silu(pre_gate)
    hidden = (active * pre_up).astype(jnp.bfloat16)
    result = jnp.dot(hidden, down_w, preferred_element_type=jnp.float32).astype(jnp.bfloat16)
    grad_hidden = jnp.dot(rows_cot, down_w.T, preferred_element_type=jnp.float32)
    grad_pg = (grad_hidden * pre_up * silu_slope(pre_gate)).astype(jnp.bfloat16)
    grad_pu = (grad_hidden * active).astype(jnp.bfloat16)
    back = jnp.dot(grad_pg, gate_w.T, preferred_element_type=jnp.float32)
    back = (back + jnp.dot(grad_pu, up_w.T, preferred_element_type=jnp.float32)).astype(jnp.bfloat16)
    g_gate = jnp.dot(rows_in.T, grad_pg, preferred_element_type=jnp.float32)
    g_up = jnp.dot(rows_in.T, grad_pu, preferred_element_type=jnp.float32)
    g_down = jnp.dot(hidden.T, rows_cot, preferred_element_type=jnp.float32)
    return result, back, g_gate, g_up, g_down


def reference(tokens, cotangent, route, numer, w_gate, w_up, w_down):
    num = numer.astype(jnp.float32)
    gates = (num / jnp.sum(num, axis=1, keepdims=True)).reshape(-1)
    flat = route.reshape(-1).astype(jnp.int32)
    counts = jnp.sum((flat[:, None] == jnp.arange(E, dtype=jnp.int32)[None, :]).astype(jnp.int32), axis=0)
    starts = (jnp.cumsum(counts) - counts).astype(jnp.int32)
    first = jnp.argmax(counts).astype(jnp.int32)
    second = jnp.argmax(jnp.where(jnp.arange(E) == first, -1, counts)).astype(jnp.int32)
    order = jnp.argsort(flat, stable=True).astype(jnp.int32)
    cold_width = N_DP * N_EXPERT * COLD
    hot_width = N_DP * N_EXPERT * HOT_ROWS
    padded = jnp.concatenate([order, jnp.zeros((hot_width,), jnp.int32)])

    def run(expert, width, allowed, accum):
        idx = lax.dynamic_slice(padded, (starts[expert].astype(jnp.int32),), (width,))
        valid = (jnp.arange(width) < counts[expert]) & allowed
        tok = (idx // TOP).astype(jnp.int32)
        rows_in = jnp.where(valid[:, None], tokens[tok], jnp.zeros((), jnp.bfloat16))
        weight = jnp.where(valid, gates[idx], jnp.zeros((), jnp.float32))
        rows_cot = (weight[:, None] * cotangent[tok].astype(jnp.float32)).astype(jnp.bfloat16)
        result, back, g_gate, g_up, g_down = expert_pass(rows_in, rows_cot, w_gate[expert], w_up[expert], w_down[expert])
        out_acc, back_acc = accum
        out_acc = out_acc.at[tok].add(weight[:, None] * result.astype(jnp.float32))
        back_acc = back_acc.at[tok].add(back.astype(jnp.float32))
        return (out_acc, back_acc), (g_gate, g_up, g_down)

    def cold_step(accum, expert):
        allowed = (expert != first) & (expert != second)
        return run(expert, cold_width, allowed, accum)

    zero = jnp.zeros((TOKENS, D), jnp.float32)
    accum, grads = lax.scan(cold_step, (zero, zero), jnp.arange(E, dtype=jnp.int32))
    grad_gate, grad_up, grad_down = grads
    for hot in (first, second):
        accum, extra = run(hot, hot_width, jnp.array(True), accum)
        grad_gate = grad_gate.at[hot].add(extra[0])
        grad_up = grad_up.at[hot].add(extra[1])
        grad_down = grad_down.at[hot].add(extra[2])
    output = accum[0].astype(jnp.bfloat16)
    grad_tokens = accum[1].astype(jnp.bfloat16)
    return output, grad_tokens, grad_gate, grad_up, grad_down
```

```python
import jax
import jax.numpy as jnp
from jax import lax
from jax.experimental import pallas as pl
from jax.experimental.pallas import tpu as pltpu
from jax.sharding import Mesh, PartitionSpec as P

BF = jnp.bfloat16
F32 = jnp.float32
D = 1024
FF = 384
T = 128
CAP = 8
HOT = 16
NZ = 8
SLICE = FF // NZ
PAY = T + 2 * HOT + 16
VMEM = pltpu.CompilerParams(vmem_limit_bytes=48 * 1024 * 1024)


def iota(shape, dim):
    return lax.broadcasted_iota(jnp.int32, shape, dim).astype(F32)


def before():
    return (iota((T, T), 0) < iota((T, T), 1)).astype(BF)


def dot(a, b):
    return jnp.dot(a, b, preferred_element_type=F32)


def dot_t(a, b):
    return lax.dot_general(a, b, (((1,), (1,)), ((), ())), preferred_element_type=F32)


def members(route, gates, expert):
    hit = jnp.zeros(expert.shape, F32)
    gate = jnp.zeros(expert.shape, F32)
    for k in range(8):
        same = route[k : k + 1, :] == expert
        hit = hit + jnp.where(same, 1.0, 0.0)
        if gates is not None:
            gate = gate + jnp.where(same, gates[k : k + 1, :], 0.0)
    return hit, gate


def places(hit):
    return jnp.where(hit > 0.5, dot(hit.astype(BF), before()), -1.0)


def cold_pick(place):
    n = place.shape[0]
    return jnp.where(place[:, None, :] == iota((n, CAP, T), 1), 1.0, 0.0)


def hot_pick(place2):
    want = iota((HOT, T), 0)
    return jnp.concatenate(
        [jnp.where(place2[h : h + 1, :] == want, 1.0, 0.0) for h in range(2)], axis=0
    )


def send_kernel(tok, cot, route, numer, slots, pay, place_out, info):
    r = route[...].astype(F32)
    expert = iota((T, T), 0)
    hit, _ = members(r, None, expert)
    place = places(hit)
    hot = jnp.sum(hit, axis=1, keepdims=True) > CAP + 0.5
    ids = iota((T, 1), 0)
    first = jnp.min(jnp.where(hot, ids, 1000.0), axis=0, keepdims=True)
    second = jnp.max(jnp.where(hot, ids, -1.0), axis=0, keepdims=True)
    row = iota((8, T), 0)
    info[...] = jnp.where(row == 0.0, first, second).astype(jnp.int32)
    hot_hit, _ = members(r, None, jnp.where(row == 0.0, first, second))
    place2 = places(hot_hit)
    cold = jnp.where(hot, -1.0, place)
    place_out[0:T, :] = cold
    place_out[T : T + 8, :] = place2
    tokens = tok[...]
    for i in range(4):
        pick = cold_pick(cold[32 * i : 32 * i + 32]).reshape(256, T).astype(BF)
        slots[256 * i : 256 * i + 256, :] = dot(pick, tokens).astype(BF)
    pay[0:T, :] = cot[...]
    pay[T : T + 2 * HOT, :] = dot(hot_pick(place2).astype(BF), tokens).astype(BF)
    pay[T + 2 * HOT : PAY, :] = jnp.zeros((16, D), BF)
    meta = jnp.concatenate([r, numer[...].astype(F32)], axis=0)
    pay[T + 2 * HOT : PAY, 0:T] = meta.astype(BF)


def column_parts(meta, scal):
    meta = meta.astype(F32)
    route, numer = meta[0:8], meta[8:16]
    gates = numer / jnp.sum(numer, axis=0, keepdims=True)
    first = scal[0].astype(F32)
    second = scal[1].astype(F32)
    expert = iota((16, T), 0) + scal[2].astype(F32)
    hit, gate = members(route, gates, expert)
    place = places(hit)
    place = jnp.where((expert == first) | (expert == second), -1.0, place)
    hot_expert = jnp.where(iota((8, T), 0) == 0.0, first, second)
    hot_hit, hot_gate = members(route, gates, hot_expert)
    pick = cold_pick(place)
    weight = pick * gate[:, None, :]
    hpick = hot_pick(places(hot_hit))
    hgate = jnp.concatenate(
        [jnp.broadcast_to(hot_gate[h : h + 1, :], (HOT, T)) for h in range(2)], axis=0
    )
    hweight = hpick * hgate
    return pick, weight, hpick, hweight


def column_kernel(scal, pay, slots, hot_cot):
    parts = []
    for z in range(2):
        pick, weight, hpick, hweight = column_parts(pay[z, T + 2 * HOT : PAY, 0:T], scal)
        cot = pay[z, 0:T, :]
        rows = dot(pick.reshape(16 * CAP, T).astype(BF), cot).reshape(16, CAP, D)
        parts.append(rows * jnp.sum(weight, axis=2, keepdims=True))
        hot_rows = dot(hpick.astype(BF), cot) * jnp.sum(hweight, axis=1, keepdims=True)
        hot_cot[z] = hot_rows.astype(BF)
    slots[...] = jnp.concatenate(parts, axis=1).astype(BF)


def column_send(scal, pay):
    return pl.pallas_call(
        column_kernel,
        grid=(4,),
        in_specs=[
            pl.BlockSpec(memory_space=pltpu.SMEM),
            pl.BlockSpec((2, PAY, D), lambda g: (g, 0, 0)),
        ],
        out_specs=[
            pl.BlockSpec((16, 16, D), lambda g: (0, g, 0)),
            pl.BlockSpec((2, 2 * HOT, D), lambda g: (g, 0, 0)),
        ],
        out_shape=[
            jax.ShapeDtypeStruct((16, 64, D), BF),
            jax.ShapeDtypeStruct((NZ, 2 * HOT, D), BF),
        ],
        cost_estimate=pl.CostEstimate(flops=600_000_000, bytes_accessed=7_000_000, transcendentals=0),
        compiler_params=VMEM,
        name="column_send",
    )(scal, pay)


def merge_kernel(scal, meta, rows, hot_out, hot_back, total):
    block = rows[...].astype(F32)
    for z in range(2):
        _, weight, hpick, hweight = column_parts(meta[z], scal)
        mine = block[:, CAP * z : CAP * z + CAP, :].reshape(16 * CAP, D).astype(BF)
        weight = weight.reshape(16 * CAP, T).T
        high = weight.astype(BF)
        low = (weight - high.astype(F32)).astype(BF)
        hot_rows = hot_out[z] * jnp.sum(hweight, axis=1, keepdims=True)
        hot_sum = dot(hpick.T.astype(BF), hot_rows.astype(BF))
        total[z, 0:T, :] = (dot(high, mine) + dot(low, mine) + hot_sum).astype(BF)
        total[z, T : T + 2 * HOT, :] = hot_back[z].astype(BF)


def column_merge(scal, pay, rows, hot_out, hot_back):
    return pl.pallas_call(
        merge_kernel,
        grid=(4,),
        in_specs=[
            pl.BlockSpec(memory_space=pltpu.SMEM),
            pl.BlockSpec((2, 16, T), lambda g: (g, (T + 2 * HOT) // 16, 0)),
            pl.BlockSpec((16, 16, D), lambda g: (0, g, 0)),
            pl.BlockSpec((2, 2 * HOT, D), lambda g: (g, 0, 0)),
            pl.BlockSpec((2, 2 * HOT, D), lambda g: (g, 0, 0)),
        ],
        out_specs=pl.BlockSpec((2, T + 2 * HOT, D), lambda g: (g, 0, 0)),
        out_shape=jax.ShapeDtypeStruct((NZ, T + 2 * HOT, D), BF),
        cost_estimate=pl.CostEstimate(flops=900_000_000, bytes_accessed=7_000_000, transcendentals=0),
        compiler_params=VMEM,
        name="column_merge",
    )(scal, pay, rows, hot_out, hot_back)


def silu_slope(pre):
    sig = jax.nn.sigmoid(pre)
    return sig * (1.0 + pre * (1.0 - sig))


def hot_kernel(rows_in, rows_cot, weights, out, back, grads):
    x = rows_in[...].reshape(NZ * HOT, D)
    c = rows_cot[...].reshape(NZ * HOT, D)
    gate_w = weights[0, 0:SLICE, :]
    up_w = weights[0, SLICE : 2 * SLICE, :]
    down_w = weights[0, 2 * SLICE : 3 * SLICE, :]
    pre_gate = dot_t(x, gate_w)
    pre_up = dot_t(x, up_w)
    sig = 1.0 / (1.0 + jnp.exp(-pre_gate))
    active = pre_gate * sig
    hidden = active * pre_up
    out[...] = dot(hidden.astype(BF), down_w).reshape(NZ, HOT, D)
    grad_hidden = dot_t(c, down_w)
    grad_pg = grad_hidden * pre_up * (sig * (1.0 + pre_gate * (1.0 - sig)))
    grad_pu = grad_hidden * active
    back[...] = (dot(grad_pg.astype(BF), gate_w) + dot(grad_pu.astype(BF), up_w)).reshape(NZ, HOT, D)
    grads[0, 0:SLICE, :] = dot(grad_pg.T.astype(BF), x)
    grads[0, SLICE : 2 * SLICE, :] = dot(grad_pu.T.astype(BF), x)
    grads[0, 2 * SLICE : 3 * SLICE, :] = dot(hidden.T.astype(BF), c)


def hot_pass(pay, hot_cot, weights):
    rows = jax.ShapeDtypeStruct((NZ, 2 * HOT, D), F32)
    return pl.pallas_call(
        hot_kernel,
        grid=(2,),
        in_specs=[
            pl.BlockSpec((NZ, HOT, D), lambda h: (0, T // HOT + h, 0)),
            pl.BlockSpec((NZ, HOT, D), lambda h: (0, h, 0)),
            pl.BlockSpec((1, 3 * SLICE, D), lambda h: (h, 0, 0)),
        ],
        out_specs=[
            pl.BlockSpec((NZ, HOT, D), lambda h: (0, h, 0)),
            pl.BlockSpec((NZ, HOT, D), lambda h: (0, h, 0)),
            pl.BlockSpec((1, 3 * SLICE, D), lambda h: (h, 0, 0)),
        ],
        out_shape=[rows, rows, jax.ShapeDtypeStruct((2, 3 * SLICE, D), F32)],
        cost_estimate=pl.CostEstimate(flops=600_000_000, bytes_accessed=6_000_000, transcendentals=20_000),
        compiler_params=VMEM,
        name="hot_pass",
    )(pay, hot_cot, weights)


def last_kernel(place, rows, hot_back, out):
    total = dot(hot_pick(place[T : T + 8, :]).T.astype(BF), hot_back[...])
    for i in range(4):
        pick = cold_pick(place[32 * i : 32 * i + 32, :]).reshape(256, T).T.astype(BF)
        total = total + dot(pick, rows[256 * i : 256 * i + 256, :])
    out[...] = total.astype(BF)


def spread_sum(v, axis):
    n = lax.axis_size(axis)
    moved = [
        lax.ppermute(v, axis, [(i, (i + s) % n) for i in range(n)]) for s in range(1, n)
    ]
    total = v.astype(F32)
    for m in moved:
        total = total + m.astype(F32)
    return total.astype(v.dtype)


def ring_gather(v, z):
    up = [(i, (i + 1) % NZ) for i in range(NZ)]
    down = [((i + 1) % NZ, i) for i in range(NZ)]
    below, above = [v], [v]
    for step in range(4):
        below.append(lax.ppermute(below[-1], "z", up))
        if step < 3:
            above.append(lax.ppermute(above[-1], "z", down))
    return jnp.roll(jnp.stack(below[:0:-1] + above), z - 4, axis=0)


def swap(v):
    return lax.ppermute(v, "dp", [(0, 1), (1, 0)])


def half_sum(v, dp, dim):
    size = v.shape[dim] // 2
    mine = lax.dynamic_slice_in_dim(v, dp * size, size, dim)
    other = lax.dynamic_slice_in_dim(v, (1 - dp) * size, size, dim)
    return mine + swap(other)


def exchange(v, axes):
    return lax.all_to_all(v, axes, split_axis=0, concat_axis=0, tiled=True)


def shards(tokens, cotangent, route, numer, w_gate, w_up, w_down):
    dp = lax.axis_index("dp")
    z = lax.axis_index("z")
    me = z * 16 + lax.axis_index("x") * 4 + lax.axis_index("y")
    gate_w, up_w, down_w = w_gate[0], w_up[0], w_down[0]

    sent_in, pay, place, info = pl.pallas_call(
        send_kernel,
        out_shape=[
            jax.ShapeDtypeStruct((T * CAP, D), BF),
            jax.ShapeDtypeStruct((PAY, D), BF),
            jax.ShapeDtypeStruct((T + 8, T), F32),
            jax.ShapeDtypeStruct((8, T), jnp.int32),
        ],
        cost_estimate=pl.CostEstimate(flops=300_000_000, bytes_accessed=3_500_000, transcendentals=0),
        compiler_params=VMEM,
        name="send",
    )(tokens, cotangent, route.T, numer.T)
    first, second = info[0, 0], info[1, 0]
    scal = jnp.stack([first, second, z * 16]).astype(jnp.int32)

    pay_all = lax.all_gather(pay, "z")
    recv_in = exchange(sent_in.reshape(T, CAP, D), ("z", "x", "y"))

    wcat = jnp.concatenate(
        [w.reshape(NZ, SLICE, D) for w in (gate_w.T, up_w.T, down_w)], axis=1
    )
    named = jnp.where(me == jnp.where(dp == 0, first, second), wcat, jnp.zeros((), BF))
    named, _ = lax.optimization_barrier((named, pay_all))
    hot_w = lax.psum_scatter(
        named.reshape(NZ * 3 * SLICE, D), "z", scatter_dimension=0, tiled=True
    )
    hot_w = spread_sum(spread_sum(hot_w, "x"), "y")
    other_w = swap(hot_w)
    hot_w = jnp.where(dp == 0, jnp.stack([hot_w, other_w]), jnp.stack([other_w, hot_w]))

    sent_cot, hot_cot = column_send(scal, pay_all)
    recv_cot = exchange(sent_cot, ("x", "y"))

    rows_in = recv_in.reshape(NZ, 16, CAP, D).transpose(1, 0, 2, 3).reshape(T * CAP, D)
    pre_gate = dot(rows_in, gate_w)
    pre_up = dot(rows_in, up_w)
    active = jax.nn.silu(pre_gate)
    hidden = (active * pre_up).astype(BF)
    result = dot(hidden, down_w).astype(BF)
    back_out = exchange(result.reshape(16, 64, D), ("x", "y"))

    rows_cot = recv_cot.reshape(T * CAP, D)
    grad_hidden = dot_t(rows_cot, down_w)
    grad_pg = (grad_hidden * pre_up * silu_slope(pre_gate)).astype(BF)
    grad_pu = (grad_hidden * active).astype(BF)
    back = (dot_t(grad_pg, gate_w) + dot_t(grad_pu, up_w)).astype(BF)
    back = back.reshape(16, NZ, CAP, D).transpose(1, 0, 2, 3).reshape(T, CAP, D)
    back_grad = exchange(back, ("z", "x", "y"))

    hot_out, hot_back, hot_grads = hot_pass(pay_all, hot_cot, hot_w)
    total = column_merge(scal, pay_all, back_out, hot_out, hot_back)
    summed = lax.psum_scatter(
        total.reshape(NZ * (T + 2 * HOT), D), "z", scatter_dimension=0, tiled=True
    )
    output = summed[:T]

    hot_g = half_sum(hot_grads.reshape(2 * 3 * SLICE, D), dp, 1).astype(BF)
    hot_g = spread_sum(spread_sum(hot_g, "x"), "y")
    hot_g = ring_gather(hot_g, z).reshape(NZ, 2, 3, SLICE, D // 2)
    hot_g = jnp.where(me == first, hot_g[:, 0], hot_g[:, 1]).astype(F32)
    is_hot = (me == first) | (me == second)

    def pieces(i):
        return hot_g[:, i].reshape(FF, D // 2)

    def grad(a, b):
        return lax.dot_general(a, b, (((0,), (0,)), ((), ())), preferred_element_type=F32)

    cold_gate = half_sum(grad(rows_in, grad_pg), dp, 0)
    cold_up = half_sum(grad(rows_in, grad_pu), dp, 0)
    cold_down = half_sum(grad(hidden, rows_cot), dp, 1)
    grad_gate = jnp.where(is_hot, pieces(0).T, cold_gate)
    grad_up = jnp.where(is_hot, pieces(1).T, cold_up)
    grad_down = jnp.where(is_hot, pieces(2), cold_down)

    grad_tokens = pl.pallas_call(
        last_kernel,
        out_shape=jax.ShapeDtypeStruct((T, D), BF),
        cost_estimate=pl.CostEstimate(flops=300_000_000, bytes_accessed=3_000_000, transcendentals=0),
        compiler_params=VMEM,
        name="last",
    )(place, back_grad.reshape(T * CAP, D), summed[T:])
    return (output, grad_tokens, grad_gate[None], grad_up[None], grad_down[None])


def solution(mesh):
    cube = Mesh(mesh.devices.reshape(2, 8, 4, 4), ("dp", "z", "x", "y"))
    owner = ("z", "x", "y")
    rows = P(("dp", "z", "x", "y"), None)
    weights = P(owner, None, None)
    return jax.shard_map(
        shards,
        mesh=cube,
        in_specs=(rows, rows, rows, rows, weights, weights, weights),
        out_specs=(
            rows,
            rows,
            P(owner, "dp", None),
            P(owner, "dp", None),
            P(owner, None, "dp"),
        ),
        check_vma=False,
    )
```

```python
import jax
import jax.numpy as jnp
from jax import lax
from jax.experimental import pallas as pl
from jax.experimental.pallas import tpu as pltpu
from jax.sharding import Mesh, PartitionSpec as P

BF = jnp.bfloat16
F32 = jnp.float32
D = 1024
FF = 384
T = 128
CAP = 8
HOT = 16
NZ = 8
SLICE = FF // NZ
PAY = T + 16
VMEM = pltpu.CompilerParams(vmem_limit_bytes=48 * 1024 * 1024)


def iota(shape, dim):
    return lax.broadcasted_iota(jnp.int32, shape, dim).astype(F32)


def before():
    return (iota((T, T), 0) < iota((T, T), 1)).astype(BF)


def dot(a, b):
    return jnp.dot(a, b, preferred_element_type=F32)


def dot_t(a, b):
    return lax.dot_general(a, b, (((1,), (1,)), ((), ())), preferred_element_type=F32)


def members(route, gates, expert):
    hit = jnp.zeros(expert.shape, F32)
    gate = jnp.zeros(expert.shape, F32)
    for k in range(8):
        same = route[k : k + 1, :] == expert
        hit = hit + jnp.where(same, 1.0, 0.0)
        if gates is not None:
            gate = gate + jnp.where(same, gates[k : k + 1, :], 0.0)
    return hit, gate


def places(hit):
    return jnp.where(hit > 0.5, dot(hit.astype(BF), before()), -1.0)


def cold_pick(place):
    n = place.shape[0]
    return jnp.where(place[:, None, :] == iota((n, CAP, T), 1), 1.0, 0.0)


def hot_pick(place2):
    want = iota((HOT, T), 0)
    return jnp.concatenate(
        [jnp.where(place2[h : h + 1, :] == want, 1.0, 0.0) for h in range(2)], axis=0
    )


def send_kernel(tok, route, numer, pay, info):
    r = route[...].astype(F32)
    hit, _ = members(r, None, iota((T, T), 0))
    hot = jnp.sum(hit, axis=1, keepdims=True) > CAP + 0.5
    ids = iota((T, 1), 0)
    first = jnp.min(jnp.where(hot, ids, 1000.0), axis=0, keepdims=True)
    second = jnp.max(jnp.where(hot, ids, -1.0), axis=0, keepdims=True)
    info[...] = jnp.where(iota((8, T), 0) == 0.0, first, second).astype(jnp.int32)
    pay[0:T, :] = tok[...]
    pay[T:PAY, :] = jnp.zeros((16, D), BF)
    pay[T:PAY, 0:T] = jnp.concatenate([r, numer[...].astype(F32)], axis=0).astype(BF)


def column_parts(meta, scal):
    meta = meta.astype(F32)
    route, numer = meta[0:8], meta[8:16]
    gates = numer / jnp.sum(numer, axis=0, keepdims=True)
    first = scal[0].astype(F32)
    second = scal[1].astype(F32)
    expert = iota((16, T), 0) + scal[2].astype(F32)
    hit, gate = members(route, gates, expert)
    place = places(hit)
    place = jnp.where((expert == first) | (expert == second), -1.0, place)
    hot_expert = jnp.where(iota((8, T), 0) == 0.0, first, second)
    hot_hit, hot_gate = members(route, gates, hot_expert)
    pick = cold_pick(place)
    weight = pick * gate[:, None, :]
    hpick = hot_pick(places(hot_hit))
    hgate = jnp.concatenate(
        [jnp.broadcast_to(hot_gate[h : h + 1, :], (HOT, T)) for h in range(2)], axis=0
    )
    hweight = hpick * hgate
    return pick, weight, hpick, hweight


def ring_kernel(scal, *refs):
    pays, (slots, hot_in, meta) = refs[:NZ], refs[NZ:]
    for g in range(NZ // 2):
        parts = []
        for o in (2 * g, 2 * g + 1):
            small = pays[o][T:PAY, 0:T]
            meta[o] = small
            pick, _, hpick, _ = column_parts(small, scal)
            tok = pays[o][0:T, :]
            parts.append(dot(pick.reshape(16 * CAP, T).astype(BF), tok).reshape(16, CAP, D))
            hot_in[o] = dot(hpick.astype(BF), tok).astype(BF)
        slots[:, 16 * g : 16 * g + 16, :] = jnp.concatenate(parts, axis=1).astype(BF)


def ring_send(scal, pays):
    return pl.pallas_call(
        ring_kernel,
        in_specs=[pl.BlockSpec(memory_space=pltpu.SMEM)]
        + [pl.BlockSpec(memory_space=pltpu.VMEM)] * NZ,
        out_shape=[
            jax.ShapeDtypeStruct((16, 64, D), BF),
            jax.ShapeDtypeStruct((NZ, 2 * HOT, D), BF),
            jax.ShapeDtypeStruct((NZ, 16, T), BF),
        ],
        cost_estimate=pl.CostEstimate(flops=600_000_000, bytes_accessed=7_000_000, transcendentals=0),
        compiler_params=VMEM,
        name="ring_send",
    )(scal, *pays)


def column_kernel(scal, meta, cot_a, cot_b, slots, hot_cot):
    parts = []
    for o, ref in enumerate((cot_a, cot_b)):
        pick, weight, hpick, hweight = column_parts(meta[o], scal)
        cot = ref[0]
        rows = dot(pick.reshape(16 * CAP, T).astype(BF), cot).reshape(16, CAP, D)
        parts.append(rows * jnp.sum(weight, axis=2, keepdims=True))
        hot_rows = dot(hpick.astype(BF), cot) * jnp.sum(hweight, axis=1, keepdims=True)
        hot_cot[o] = hot_rows.astype(BF)
    slots[...] = jnp.concatenate(parts, axis=1).astype(BF)


def column_send(scal, meta, cots):
    def at(shift):
        return pl.BlockSpec((1, T, D), lambda g, s: (lax.rem(s[3] + 2 * g + shift, NZ), 0, 0))

    return pl.pallas_call(
        column_kernel,
        grid_spec=pltpu.PrefetchScalarGridSpec(
            num_scalar_prefetch=1,
            grid=(4,),
            in_specs=[pl.BlockSpec((2, 16, T), lambda g, s: (g, 0, 0)), at(4), at(5)],
            out_specs=[
                pl.BlockSpec((16, 16, D), lambda g, s: (0, g, 0)),
                pl.BlockSpec((2, 2 * HOT, D), lambda g, s: (g, 0, 0)),
            ],
        ),
        out_shape=[
            jax.ShapeDtypeStruct((16, 64, D), BF),
            jax.ShapeDtypeStruct((NZ, 2 * HOT, D), BF),
        ],
        cost_estimate=pl.CostEstimate(flops=600_000_000, bytes_accessed=7_000_000, transcendentals=0),
        compiler_params=VMEM,
        name="column_send",
    )(scal, meta, cots, cots)


def merge_kernel(gated, scal, meta, rows, hot_rows, total):
    odd = lax.rem(pl.program_id(0), 2) == 1
    pick, weight, hpick, hweight = column_parts(meta[0], scal)
    block = rows[...].astype(F32)
    mine = jnp.where(odd, block[:, CAP:, :], block[:, :CAP, :])
    mine = mine.reshape(16 * CAP, D).astype(BF)
    hot = hot_rows[0]
    if gated:
        hot = hot * jnp.sum(hweight, axis=1, keepdims=True)
    out = dot(hpick.T.astype(BF), hot.astype(BF))
    if gated:
        weight = weight.reshape(16 * CAP, T).T
        high = weight.astype(BF)
        low = (weight - high.astype(F32)).astype(BF)
        out = out + dot(high, mine) + dot(low, mine)
    else:
        out = out + dot(pick.reshape(16 * CAP, T).T.astype(BF), mine)
    total[0] = out.astype(BF)


def column_merge(scal, meta, rows, hot_rows, gated):
    def place(g, s):
        return (lax.rem(s[3] + g + 4, NZ) if gated else g, 0, 0)

    def kernel(*refs):
        merge_kernel(gated, *refs)

    return pl.pallas_call(
        kernel,
        grid_spec=pltpu.PrefetchScalarGridSpec(
            num_scalar_prefetch=1,
            grid=(NZ,),
            in_specs=[
                pl.BlockSpec((1, 16, T), lambda g, s: (g, 0, 0)),
                pl.BlockSpec((16, 16, D), lambda g, s: (0, g // 2, 0)),
                pl.BlockSpec((1, 2 * HOT, D), lambda g, s: (g, 0, 0)),
            ],
            out_specs=pl.BlockSpec((1, T, D), place),
        ),
        out_shape=jax.ShapeDtypeStruct((NZ, T, D), BF),
        cost_estimate=pl.CostEstimate(flops=900_000_000, bytes_accessed=7_000_000, transcendentals=0),
        compiler_params=VMEM,
        name="merge_gated" if gated else "merge_plain",
    )(scal, meta, rows, hot_rows)


def silu_slope(pre):
    sig = jax.nn.sigmoid(pre)
    return sig * (1.0 + pre * (1.0 - sig))


def hot_kernel(rows_in, rows_cot, weights, out, back, grads):
    x = rows_in[...].reshape(NZ * HOT, D)
    c = rows_cot[...].reshape(NZ * HOT, D)
    gate_w = weights[0, 0:SLICE, :]
    up_w = weights[0, SLICE : 2 * SLICE, :]
    down_w = weights[0, 2 * SLICE : 3 * SLICE, :]
    pre_gate = dot_t(x, gate_w)
    pre_up = dot_t(x, up_w)
    sig = 1.0 / (1.0 + jnp.exp(-pre_gate))
    active = pre_gate * sig
    hidden = active * pre_up
    out[...] = dot(hidden.astype(BF), down_w).reshape(NZ, HOT, D)
    grad_hidden = dot_t(c, down_w)
    grad_pg = grad_hidden * pre_up * (sig * (1.0 + pre_gate * (1.0 - sig)))
    grad_pu = grad_hidden * active
    back[...] = (dot(grad_pg.astype(BF), gate_w) + dot(grad_pu.astype(BF), up_w)).reshape(NZ, HOT, D)
    grads[0, 0:SLICE, :] = dot(grad_pg.T.astype(BF), x)
    grads[0, SLICE : 2 * SLICE, :] = dot(grad_pu.T.astype(BF), x)
    grads[0, 2 * SLICE : 3 * SLICE, :] = dot(hidden.T.astype(BF), c)


def hot_pass(hot_in, hot_cot, weights):
    rows = jax.ShapeDtypeStruct((NZ, 2 * HOT, D), F32)
    return pl.pallas_call(
        hot_kernel,
        grid=(2,),
        in_specs=[
            pl.BlockSpec((NZ, HOT, D), lambda h: (0, h, 0)),
            pl.BlockSpec((NZ, HOT, D), lambda h: (0, h, 0)),
            pl.BlockSpec((1, 3 * SLICE, D), lambda h: (h, 0, 0)),
        ],
        out_specs=[
            pl.BlockSpec((NZ, HOT, D), lambda h: (0, h, 0)),
            pl.BlockSpec((NZ, HOT, D), lambda h: (0, h, 0)),
            pl.BlockSpec((1, 3 * SLICE, D), lambda h: (h, 0, 0)),
        ],
        out_shape=[rows, rows, jax.ShapeDtypeStruct((2, 3 * SLICE, D), F32)],
        cost_estimate=pl.CostEstimate(flops=600_000_000, bytes_accessed=6_000_000, transcendentals=20_000),
        compiler_params=VMEM,
        name="hot_pass",
    )(hot_in, hot_cot, weights)


def spread_sum(v, axis):
    n = lax.axis_size(axis)
    moved = [
        lax.ppermute(v, axis, [(i, (i + s) % n) for i in range(n)]) for s in range(1, n)
    ]
    total = v.astype(F32)
    for m in moved:
        total = total + m.astype(F32)
    return total.astype(v.dtype)


def up(v):
    return lax.ppermute(v, "z", [(i, (i + 1) % NZ) for i in range(NZ)])


def down(v):
    return lax.ppermute(v, "z", [((i + 1) % NZ, i) for i in range(NZ)])


def ring_gather(v):
    below, above = [v], [v]
    for step in range(4):
        below.append(up(below[-1]))
        if step < 3:
            above.append(down(above[-1]))
    return below[:0:-1] + above


def add(a, b):
    return (a.astype(F32) + b.astype(F32)).astype(BF)


def ring_sum(parts):
    rising, falling = up(parts[0]), down(parts[1])
    for step in range(3):
        rising = up(add(rising, parts[7 - step]))
        if step < 2:
            falling = down(add(falling, parts[2 + step]))
    return (parts[4].astype(F32) + rising.astype(F32) + falling.astype(F32)).astype(BF)


def swap(v):
    return lax.ppermute(v, "dp", [(0, 1), (1, 0)])


def half_sum(v, dp, dim):
    size = v.shape[dim] // 2
    mine = lax.dynamic_slice_in_dim(v, dp * size, size, dim)
    other = lax.dynamic_slice_in_dim(v, (1 - dp) * size, size, dim)
    return mine + swap(other)


def exchange(v, axes):
    return lax.all_to_all(v, axes, split_axis=0, concat_axis=0, tiled=True)


def shards(tokens, cotangent, route, numer, w_gate, w_up, w_down):
    dp = lax.axis_index("dp")
    z = lax.axis_index("z")
    me = z * 16 + lax.axis_index("x") * 4 + lax.axis_index("y")
    gate_w, up_w, down_w = w_gate[0], w_up[0], w_down[0]
    plane = ("x", "y")

    cots = lax.all_gather(cotangent, "z")
    pay, info = pl.pallas_call(
        send_kernel,
        out_shape=[
            jax.ShapeDtypeStruct((PAY, D), BF),
            jax.ShapeDtypeStruct((8, T), jnp.int32),
        ],
        cost_estimate=pl.CostEstimate(flops=10_000_000, bytes_accessed=700_000, transcendentals=0),
        compiler_params=VMEM,
        name="send",
    )(tokens, route.T, numer.T)
    first, second = info[0, 0], info[1, 0]
    scal = jnp.stack([first, second, z * 16, z]).astype(jnp.int32)
    sent_in, hot_in, meta = ring_send(scal, ring_gather(pay))
    recv_in = exchange(sent_in, plane)

    sent_cot, hot_cot = column_send(scal, meta, cots)
    sent_cot, recv_in = lax.optimization_barrier((sent_cot, recv_in))
    recv_cot = exchange(sent_cot, plane)

    wcat = jnp.concatenate(
        [w.reshape(NZ, SLICE, D) for w in (gate_w.T, up_w.T, down_w)], axis=1
    )
    named = jnp.where(me == jnp.where(dp == 0, first, second), wcat, jnp.zeros((), BF))
    named, _ = lax.optimization_barrier((named, cots))
    hot_w = lax.psum_scatter(
        named.reshape(NZ * 3 * SLICE, D), "z", scatter_dimension=0, tiled=True
    )
    hot_w = spread_sum(spread_sum(hot_w, "x"), "y")
    other_w = swap(hot_w)
    hot_w = jnp.where(dp == 0, jnp.stack([hot_w, other_w]), jnp.stack([other_w, hot_w]))
    hot_out, hot_back, hot_grads = hot_pass(hot_in, hot_cot, hot_w)

    rows_in = recv_in.reshape(T * CAP, D)
    pre_gate = dot(rows_in, gate_w)
    pre_up = dot(rows_in, up_w)
    active = jax.nn.silu(pre_gate)
    hidden = (active * pre_up).astype(BF)
    result = dot(hidden, down_w).astype(BF)
    result, recv_cot = lax.optimization_barrier((result, recv_cot))
    back_out = exchange(result.reshape(16, 64, D), plane)

    rows_cot = recv_cot.reshape(T * CAP, D)
    grad_hidden = dot_t(rows_cot, down_w)
    grad_pg = (grad_hidden * pre_up * silu_slope(pre_gate)).astype(BF)
    grad_pu = (grad_hidden * active).astype(BF)
    back = (dot_t(grad_pg, gate_w) + dot_t(grad_pu, up_w)).astype(BF)
    back, back_out = lax.optimization_barrier((back, back_out))
    back_grad = exchange(back.reshape(16, 64, D), plane)

    total = column_merge(scal, meta, back_out, hot_out, True)
    output = lax.psum_scatter(
        total.reshape(NZ * T, D), "z", scatter_dimension=0, tiled=True
    )
    parts = column_merge(scal, meta, back_grad, hot_back, False)
    grad_tokens = ring_sum([parts[i] for i in range(NZ)])

    hot_g = half_sum(hot_grads.reshape(2 * 3 * SLICE, D), dp, 1).astype(BF)
    hot_g = spread_sum(spread_sum(hot_g, "x"), "y")
    hot_g = [g.reshape(2, 3, SLICE, D // 2) for g in ring_gather(hot_g)]
    hot_g = jnp.stack([jnp.where(me == first, g[0], g[1]) for g in hot_g])
    hot_g = jnp.roll(hot_g, z - 4, axis=0).astype(F32)
    is_hot = (me == first) | (me == second)

    def pieces(i):
        return hot_g[:, i].reshape(FF, D // 2)

    def grad(a, b):
        return lax.dot_general(a, b, (((0,), (0,)), ((), ())), preferred_element_type=F32)

    cold_gate = half_sum(grad(rows_in, grad_pg), dp, 0)
    cold_up = half_sum(grad(rows_in, grad_pu), dp, 0)
    cold_down = half_sum(grad(hidden, rows_cot), dp, 1)
    grad_gate = jnp.where(is_hot, pieces(0).T, cold_gate)
    grad_up = jnp.where(is_hot, pieces(1).T, cold_up)
    grad_down = jnp.where(is_hot, pieces(2), cold_down)
    return (output, grad_tokens, grad_gate[None], grad_up[None], grad_down[None])


def solution(mesh):
    cube = Mesh(mesh.devices.reshape(2, 8, 4, 4), ("dp", "z", "x", "y"))
    owner = ("z", "x", "y")
    rows = P(("dp", "z", "x", "y"), None)
    weights = P(owner, None, None)
    return jax.shard_map(
        shards,
        mesh=cube,
        in_specs=(rows, rows, rows, rows, weights, weights, weights),
        out_specs=(
            rows,
            rows,
            P(owner, "dp", None),
            P(owner, "dp", None),
            P(owner, None, "dp"),
        ),
        check_vma=False,
    )
```

```python
import jax
import jax.numpy as jnp
from jax import lax
from jax.experimental import pallas as pl
from jax.experimental.pallas import tpu as pltpu
from jax.sharding import Mesh, PartitionSpec as P

BF = jnp.bfloat16
F32 = jnp.float32
D = 1024
FF = 384
T = 128
CAP = 8
HOT = 16
NZ = 8
SLICE = FF // NZ
PAY = T + 16
ORDER = (3, 4, 5, 2, 6, 0, 1, 7)
NEAR = 5
LAST = 3
VMEM = pltpu.CompilerParams(vmem_limit_bytes=48 * 1024 * 1024)


def iota(shape, dim):
    return lax.broadcasted_iota(jnp.int32, shape, dim).astype(F32)


def before():
    return (iota((T, T), 0) < iota((T, T), 1)).astype(BF)


def dot(a, b):
    return jnp.dot(a, b, preferred_element_type=F32)


def dot_t(a, b):
    return lax.dot_general(a, b, (((1,), (1,)), ((), ())), preferred_element_type=F32)


def members(route, gates, expert):
    hit = jnp.zeros(expert.shape, F32)
    gate = jnp.zeros(expert.shape, F32)
    for k in range(8):
        same = route[k : k + 1, :] == expert
        hit = hit + jnp.where(same, 1.0, 0.0)
        if gates is not None:
            gate = gate + jnp.where(same, gates[k : k + 1, :], 0.0)
    return hit, gate


def places(hit):
    return jnp.where(hit > 0.5, dot(hit.astype(BF), before()), -1.0)


def cold_pick(place):
    n = place.shape[0]
    return jnp.where(place[:, None, :] == iota((n, CAP, T), 1), 1.0, 0.0)


def hot_pick(place2):
    want = iota((HOT, T), 0)
    return jnp.concatenate(
        [jnp.where(place2[h : h + 1, :] == want, 1.0, 0.0) for h in range(2)], axis=0
    )


def send_kernel(tok, route, numer, pay, info):
    r = route[...].astype(F32)
    hit, _ = members(r, None, iota((T, T), 0))
    hot = jnp.sum(hit, axis=1, keepdims=True) > CAP + 0.5
    ids = iota((T, 1), 0)
    first = jnp.min(jnp.where(hot, ids, 1000.0), axis=0, keepdims=True)
    second = jnp.max(jnp.where(hot, ids, -1.0), axis=0, keepdims=True)
    info[...] = jnp.where(iota((8, T), 0) == 0.0, first, second).astype(jnp.int32)
    pay[0:T, :] = tok[...]
    pay[T:PAY, :] = jnp.zeros((16, D), BF)
    pay[T:PAY, 0:T] = jnp.concatenate([r, numer[...].astype(F32)], axis=0).astype(BF)


def column_parts(meta, scal):
    meta = meta.astype(F32)
    route, numer = meta[0:8], meta[8:16]
    gates = numer / jnp.sum(numer, axis=0, keepdims=True)
    first = scal[0].astype(F32)
    second = scal[1].astype(F32)
    expert = iota((16, T), 0) + scal[2].astype(F32)
    hit, gate = members(route, gates, expert)
    place = places(hit)
    place = jnp.where((expert == first) | (expert == second), -1.0, place)
    hot_expert = jnp.where(iota((8, T), 0) == 0.0, first, second)
    hot_hit, hot_gate = members(route, gates, hot_expert)
    pick = cold_pick(place)
    weight = pick * gate[:, None, :]
    hpick = hot_pick(places(hot_hit))
    hgate = jnp.concatenate(
        [jnp.broadcast_to(hot_gate[h : h + 1, :], (HOT, T)) for h in range(2)], axis=0
    )
    hweight = hpick * hgate
    return pick, weight, hpick, hweight


def send_part(scal, pays):
    n = len(pays)

    def kernel(scal, *refs):
        slots, hot_in, meta = refs[n:]
        parts = []
        for o in range(n):
            small = refs[o][T:PAY, 0:T]
            meta[o] = small
            pick, _, hpick, _ = column_parts(small, scal)
            tok = refs[o][0:T, :]
            parts.append(dot(pick.reshape(16 * CAP, T).astype(BF), tok).reshape(16, CAP, D))
            hot_in[o] = dot(hpick.astype(BF), tok).astype(BF)
        slots[...] = jnp.concatenate(parts, axis=1).astype(BF)

    return pl.pallas_call(
        kernel,
        in_specs=[pl.BlockSpec(memory_space=pltpu.SMEM)]
        + [pl.BlockSpec(memory_space=pltpu.VMEM)] * n,
        out_shape=[
            jax.ShapeDtypeStruct((16, CAP * n, D), BF),
            jax.ShapeDtypeStruct((n, 2 * HOT, D), BF),
            jax.ShapeDtypeStruct((n, 16, T), BF),
        ],
        cost_estimate=pl.CostEstimate(
            flops=75_000_000 * n, bytes_accessed=800_000 * n, transcendentals=0
        ),
        compiler_params=VMEM,
        name=f"send_part_{n}",
    )(scal, *pays)


def send_cots(scal, meta, cots):
    n = len(cots)

    def kernel(scal, meta, *refs):
        slots, hot_cot = refs[n:]
        parts = []
        for o in range(n):
            pick, weight, hpick, hweight = column_parts(meta[o], scal)
            cot = refs[o][...]
            rows = dot(pick.reshape(16 * CAP, T).astype(BF), cot).reshape(16, CAP, D)
            parts.append(rows * jnp.sum(weight, axis=2, keepdims=True))
            hot_rows = dot(hpick.astype(BF), cot) * jnp.sum(hweight, axis=1, keepdims=True)
            hot_cot[o] = hot_rows.astype(BF)
            if o % 2:
                pair = jnp.concatenate(parts[-2:], axis=1).astype(BF)
                slots[:, 8 * o - 8 : 8 * o + 8, :] = pair

    return pl.pallas_call(
        kernel,
        in_specs=[pl.BlockSpec(memory_space=pltpu.SMEM)]
        + [pl.BlockSpec(memory_space=pltpu.VMEM)] * (n + 1),
        out_shape=[
            jax.ShapeDtypeStruct((16, CAP * n, D), BF),
            jax.ShapeDtypeStruct((n, 2 * HOT, D), BF),
        ],
        cost_estimate=pl.CostEstimate(flops=600_000_000, bytes_accessed=6_000_000, transcendentals=0),
        compiler_params=VMEM,
        name="send_cots",
    )(scal, meta, *cots)


def merge_kernel(scal, meta, rows, hot_rows, total):
    odd = lax.rem(pl.program_id(0), 2) == 1
    _, weight, hpick, hweight = column_parts(meta[0], scal)
    block = rows[...].astype(F32)
    mine = jnp.where(odd, block[:, CAP:, :], block[:, :CAP, :])
    mine = mine.reshape(16 * CAP, D).astype(BF)
    hot = hot_rows[0] * jnp.sum(hweight, axis=1, keepdims=True)
    weight = weight.reshape(16 * CAP, T).T
    high = weight.astype(BF)
    low = (weight - high.astype(F32)).astype(BF)
    out = dot(hpick.T.astype(BF), hot.astype(BF)) + dot(high, mine) + dot(low, mine)
    total[0] = out.astype(BF)


def merge_gated(scal, meta, rows, hot_rows):
    return pl.pallas_call(
        merge_kernel,
        grid_spec=pltpu.PrefetchScalarGridSpec(
            num_scalar_prefetch=1,
            grid=(NZ,),
            in_specs=[
                pl.BlockSpec((1, 16, T), lambda g, s: (g, 0, 0)),
                pl.BlockSpec((16, 16, D), lambda g, s: (0, g // 2, 0)),
                pl.BlockSpec((1, 2 * HOT, D), lambda g, s: (g, 0, 0)),
            ],
            out_specs=pl.BlockSpec((1, T, D), lambda g, s: (s[3 + g], 0, 0)),
        ),
        out_shape=jax.ShapeDtypeStruct((NZ, T, D), BF),
        cost_estimate=pl.CostEstimate(flops=900_000_000, bytes_accessed=7_000_000, transcendentals=0),
        compiler_params=VMEM,
        name="merge_gated",
    )(scal, meta, rows, hot_rows)


def merge_plain(scal, meta, rows, hot_rows, start):
    n = rows.shape[1] // CAP

    def kernel(scal, meta, rows, hot_rows, *outs):
        block = rows[...].astype(F32)
        for o in range(n):
            pick, _, hpick, _ = column_parts(meta[start + o], scal)
            mine = block[:, CAP * o : CAP * o + CAP, :].reshape(16 * CAP, D).astype(BF)
            out = dot(pick.reshape(16 * CAP, T).T.astype(BF), mine)
            out = out + dot(hpick.T.astype(BF), hot_rows[start + o].astype(BF))
            outs[o][...] = out.astype(BF)

    return pl.pallas_call(
        kernel,
        in_specs=[pl.BlockSpec(memory_space=pltpu.SMEM)]
        + [pl.BlockSpec(memory_space=pltpu.VMEM)] * 3,
        out_shape=[jax.ShapeDtypeStruct((T, D), BF)] * n,
        cost_estimate=pl.CostEstimate(
            flops=75_000_000 * n, bytes_accessed=1_000_000 * n, transcendentals=0
        ),
        compiler_params=VMEM,
        name=f"merge_plain_{n}",
    )(scal, meta, rows, hot_rows)


def silu_slope(pre):
    sig = jax.nn.sigmoid(pre)
    return sig * (1.0 + pre * (1.0 - sig))


def hot_kernel(rows_in, rows_cot, weights, out, back, grads):
    x = rows_in[...].reshape(NZ * HOT, D)
    c = rows_cot[...].reshape(NZ * HOT, D)
    gate_w = weights[0, 0:SLICE, :]
    up_w = weights[0, SLICE : 2 * SLICE, :]
    down_w = weights[0, 2 * SLICE : 3 * SLICE, :]
    pre_gate = dot_t(x, gate_w)
    pre_up = dot_t(x, up_w)
    sig = 1.0 / (1.0 + jnp.exp(-pre_gate))
    active = pre_gate * sig
    hidden = active * pre_up
    out[...] = dot(hidden.astype(BF), down_w).reshape(NZ, HOT, D)
    grad_hidden = dot_t(c, down_w)
    grad_pg = grad_hidden * pre_up * (sig * (1.0 + pre_gate * (1.0 - sig)))
    grad_pu = grad_hidden * active
    back[...] = (dot(grad_pg.astype(BF), gate_w) + dot(grad_pu.astype(BF), up_w)).reshape(NZ, HOT, D)
    grads[0, 0:SLICE, :] = dot(grad_pg.T.astype(BF), x)
    grads[0, SLICE : 2 * SLICE, :] = dot(grad_pu.T.astype(BF), x)
    grads[0, 2 * SLICE : 3 * SLICE, :] = dot(hidden.T.astype(BF), c)


def hot_pass(hot_in, hot_cot, weights):
    rows = jax.ShapeDtypeStruct((NZ, 2 * HOT, D), F32)
    return pl.pallas_call(
        hot_kernel,
        grid=(2,),
        in_specs=[
            pl.BlockSpec((NZ, HOT, D), lambda h: (0, h, 0)),
            pl.BlockSpec((NZ, HOT, D), lambda h: (0, h, 0)),
            pl.BlockSpec((1, 3 * SLICE, D), lambda h: (h, 0, 0)),
        ],
        out_specs=[
            pl.BlockSpec((NZ, HOT, D), lambda h: (0, h, 0)),
            pl.BlockSpec((NZ, HOT, D), lambda h: (0, h, 0)),
            pl.BlockSpec((1, 3 * SLICE, D), lambda h: (h, 0, 0)),
        ],
        out_shape=[rows, rows, jax.ShapeDtypeStruct((2, 3 * SLICE, D), F32)],
        cost_estimate=pl.CostEstimate(flops=600_000_000, bytes_accessed=6_000_000, transcendentals=20_000),
        compiler_params=VMEM,
        name="hot_pass",
    )(hot_in, hot_cot, weights)


def spread_sum(v, axis):
    n = lax.axis_size(axis)
    moved = [
        lax.ppermute(v, axis, [(i, (i + s) % n) for i in range(n)]) for s in range(1, n)
    ]
    total = v.astype(F32)
    for m in moved:
        total = total + m.astype(F32)
    return total.astype(v.dtype)


def up(v):
    return lax.ppermute(v, "z", [(i, (i + 1) % NZ) for i in range(NZ)])


def down(v):
    return lax.ppermute(v, "z", [((i + 1) % NZ, i) for i in range(NZ)])


def tie(v, *others):
    return lax.optimization_barrier((v, *others))[0]


def ring_gather(v, *others):
    below, above = [v], [v]
    for step in range(4):
        last = tie(below[-1], *others) if step == 1 and others else below[-1]
        below.append(up(last))
        if step < 3:
            above.append(down(above[-1]))
    return below[:0:-1] + above


def add(a, b):
    return (a.astype(F32) + b.astype(F32)).astype(BF)


def ring_sum(parts):
    rising, falling = up(parts[0]), down(parts[1])
    for step in range(3):
        rising = up(add(rising, parts[7 - step]))
        if step < 2:
            falling = down(add(falling, parts[2 + step]))
    return (parts[4].astype(F32) + rising.astype(F32) + falling.astype(F32)).astype(BF)


def swap(v):
    return lax.ppermute(v, "dp", [(0, 1), (1, 0)])


def half_sum(v, dp, dim):
    size = v.shape[dim] // 2
    mine = lax.dynamic_slice_in_dim(v, dp * size, size, dim)
    other = lax.dynamic_slice_in_dim(v, (1 - dp) * size, size, dim)
    return mine + swap(other)


def exchange(v, axes):
    return lax.all_to_all(v, axes, split_axis=0, concat_axis=0, tiled=True)


def shards(tokens, cotangent, route, numer, w_gate, w_up, w_down):
    dp = lax.axis_index("dp")
    z = lax.axis_index("z")
    me = z * 16 + lax.axis_index("x") * 4 + lax.axis_index("y")
    gate_w, up_w, down_w = w_gate[0], w_up[0], w_down[0]
    plane = ("x", "y")

    pay, info = pl.pallas_call(
        send_kernel,
        out_shape=[
            jax.ShapeDtypeStruct((PAY, D), BF),
            jax.ShapeDtypeStruct((8, T), jnp.int32),
        ],
        cost_estimate=pl.CostEstimate(flops=10_000_000, bytes_accessed=700_000, transcendentals=0),
        compiler_params=VMEM,
        name="send",
    )(tokens, route.T, numer.T)
    first, second = info[0, 0], info[1, 0]
    places_z = [lax.rem(z + g + 4, NZ) for g in ORDER]
    scal = jnp.stack([first, second, z * 16, *places_z]).astype(jnp.int32)

    wcat = jnp.concatenate(
        [w.reshape(NZ, SLICE, D) for w in (gate_w.T, up_w.T, down_w)], axis=1
    )
    named = jnp.where(me == jnp.where(dp == 0, first, second), wcat, jnp.zeros((), BF))
    hot_w = lax.psum_scatter(
        named.reshape(NZ * 3 * SLICE, D), "z", scatter_dimension=0, tiled=True
    )

    ring = ring_gather(pay, named)
    near = send_part(scal, [ring[g] for g in ORDER[:NEAR]])
    recv_near = exchange(near[0], plane)
    far = send_part(scal, [ring[g] for g in ORDER[NEAR:]])
    recv_far = exchange(tie(far[0], recv_near), plane)
    hot_in = jnp.concatenate([near[1], far[1]])
    meta = jnp.concatenate([near[2], far[2]])

    cots = ring_gather(tie(cotangent, ring[1], ring[7]))
    sent_cot, hot_cot = send_cots(scal, meta, [cots[g] for g in ORDER])
    hot_w = spread_sum(hot_w, "x")
    sent_cot, recv_far, hot_w = lax.optimization_barrier((sent_cot, recv_far, hot_w))
    recv_cot = exchange(sent_cot, plane)

    hot_w = spread_sum(hot_w, "y")
    other_w = swap(hot_w)
    hot_w = jnp.where(dp == 0, jnp.stack([hot_w, other_w]), jnp.stack([other_w, hot_w]))
    hot_out, hot_back, hot_grads = hot_pass(hot_in, hot_cot, hot_w)
    hot_g = half_sum(hot_grads.reshape(2 * 3 * SLICE, D), dp, 1).astype(BF)

    rows_in = jnp.concatenate([recv_near, recv_far], axis=1).reshape(T * CAP, D)
    pre_gate = dot(rows_in, gate_w)
    pre_up = dot(rows_in, up_w)
    active = jax.nn.silu(pre_gate)
    hidden = (active * pre_up).astype(BF)
    result = dot(hidden, down_w).astype(BF)
    result, recv_cot, hot_g = lax.optimization_barrier((result, recv_cot, hot_g))
    back_out = exchange(result.reshape(16, 64, D), plane)
    hot_g = spread_sum(hot_g, "x")

    rows_cot = recv_cot.reshape(T * CAP, D)
    grad_hidden = dot_t(rows_cot, down_w)
    grad_pg = (grad_hidden * pre_up * silu_slope(pre_gate)).astype(BF)
    grad_pu = (grad_hidden * active).astype(BF)
    back = (dot_t(grad_pg, gate_w) + dot_t(grad_pu, up_w)).astype(BF)
    back, back_out, hot_g = lax.optimization_barrier((back, back_out, hot_g))
    back = back.reshape(16, 64, D)
    back_far = exchange(back[:, CAP * LAST :], plane)
    hot_g = spread_sum(hot_g, "y")
    total = merge_gated(scal, meta, back_out, hot_out)
    output = lax.psum_scatter(
        total.reshape(NZ * T, D), "z", scatter_dimension=0, tiled=True
    )
    back_near = exchange(tie(back[:, : CAP * LAST], back_far), plane)
    merged = merge_plain(scal, meta, back_far, hot_back, LAST)
    merged = merge_plain(scal, meta, back_near, hot_back, 0) + merged
    grad_tokens = ring_sum([merged[ORDER.index(g)] for g in range(NZ)])

    hot_g = [g.reshape(2, 3, SLICE, D // 2) for g in ring_gather(hot_g)]
    hot_g = jnp.stack([jnp.where(me == first, g[0], g[1]) for g in hot_g])
    hot_g = jnp.roll(hot_g, z - 4, axis=0).astype(F32)
    is_hot = (me == first) | (me == second)

    def pieces(i):
        return hot_g[:, i].reshape(FF, D // 2)

    def grad(a, b):
        return lax.dot_general(a, b, (((0,), (0,)), ((), ())), preferred_element_type=F32)

    cold_gate = half_sum(grad(rows_in, grad_pg), dp, 0)
    cold_up = half_sum(grad(rows_in, grad_pu), dp, 0)
    cold_down = half_sum(grad(hidden, rows_cot), dp, 1)
    grad_gate = jnp.where(is_hot, pieces(0).T, cold_gate)
    grad_up = jnp.where(is_hot, pieces(1).T, cold_up)
    grad_down = jnp.where(is_hot, pieces(2), cold_down)
    return (output, grad_tokens, grad_gate[None], grad_up[None], grad_down[None])


def solution(mesh):
    cube = Mesh(mesh.devices.reshape(2, 8, 4, 4), ("dp", "z", "x", "y"))
    owner = ("z", "x", "y")
    rows = P(("dp", "z", "x", "y"), None)
    weights = P(owner, None, None)
    return jax.shard_map(
        shards,
        mesh=cube,
        in_specs=(rows, rows, rows, rows, weights, weights, weights),
        out_specs=(
            rows,
            rows,
            P(owner, "dp", None),
            P(owner, "dp", None),
            P(owner, None, "dp"),
        ),
        check_vma=False,
    )
```

```python
import jax
import jax.numpy as jnp
from jax import lax
from jax.experimental import pallas as pl
from jax.experimental.pallas import tpu as pltpu
from jax.sharding import Mesh, PartitionSpec as P

BF = jnp.bfloat16
F32 = jnp.float32
D = 1024
FF = 384
T = 128
CAP = 8
HOT = 16
NZ = 8
SLICE = FF // NZ
PAY = T + 16
ORDER = (3, 4, 5, 2, 6, 0, 1, 7)
LAST = 3
VMEM = pltpu.CompilerParams(vmem_limit_bytes=48 * 1024 * 1024)


def iota(shape, dim):
    return lax.broadcasted_iota(jnp.int32, shape, dim).astype(F32)


def before():
    return (iota((T, T), 0) < iota((T, T), 1)).astype(BF)


def dot(a, b):
    return jnp.dot(a, b, preferred_element_type=F32)


def dot_t(a, b):
    return lax.dot_general(a, b, (((1,), (1,)), ((), ())), preferred_element_type=F32)


def members(route, gates, expert):
    hit = jnp.zeros(expert.shape, F32)
    gate = jnp.zeros(expert.shape, F32)
    for k in range(8):
        same = route[k : k + 1, :] == expert
        hit = hit + jnp.where(same, 1.0, 0.0)
        if gates is not None:
            gate = gate + jnp.where(same, gates[k : k + 1, :], 0.0)
    return hit, gate


def places(hit):
    return jnp.where(hit > 0.5, dot(hit.astype(BF), before()), -1.0)


def cold_pick(place):
    n = place.shape[0]
    return jnp.where(place[:, None, :] == iota((n, CAP, T), 1), 1.0, 0.0)


def hot_pick(place2):
    want = iota((HOT, T), 0)
    return jnp.concatenate(
        [jnp.where(place2[h : h + 1, :] == want, 1.0, 0.0) for h in range(2)], axis=0
    )


def send_kernel(tok, route, numer, pay, info):
    r = route[...].astype(F32)
    hit, _ = members(r, None, iota((T, T), 0))
    hot = jnp.sum(hit, axis=1, keepdims=True) > CAP + 0.5
    ids = iota((T, 1), 0)
    first = jnp.min(jnp.where(hot, ids, 1000.0), axis=0, keepdims=True)
    second = jnp.max(jnp.where(hot, ids, -1.0), axis=0, keepdims=True)
    info[...] = jnp.where(iota((8, T), 0) == 0.0, first, second).astype(jnp.int32)
    pay[0:T, :] = tok[...]
    pay[T:PAY, :] = jnp.zeros((16, D), BF)
    pay[T:PAY, 0:T] = jnp.concatenate([r, numer[...].astype(F32)], axis=0).astype(BF)


def column_parts(meta, scal):
    meta = meta.astype(F32)
    route, numer = meta[0:8], meta[8:16]
    gates = numer / jnp.sum(numer, axis=0, keepdims=True)
    first = scal[0].astype(F32)
    second = scal[1].astype(F32)
    expert = iota((16, T), 0) + scal[2].astype(F32)
    hit, gate = members(route, gates, expert)
    place = places(hit)
    place = jnp.where((expert == first) | (expert == second), -1.0, place)
    hot_expert = jnp.where(iota((8, T), 0) == 0.0, first, second)
    hot_hit, hot_gate = members(route, gates, hot_expert)
    pick = cold_pick(place)
    weight = pick * gate[:, None, :]
    hpick = hot_pick(places(hot_hit))
    hgate = jnp.concatenate(
        [jnp.broadcast_to(hot_gate[h : h + 1, :], (HOT, T)) for h in range(2)], axis=0
    )
    hweight = hpick * hgate
    return pick, weight, hpick, hweight


def send_part(scal, pays):
    n = len(pays)

    def kernel(scal, *refs):
        slots, hot_in, meta = refs[n:]
        parts = []
        for o in range(n):
            small = refs[o][T:PAY, 0:T]
            meta[o] = small
            pick, _, hpick, _ = column_parts(small, scal)
            tok = refs[o][0:T, :]
            parts.append(dot(pick.reshape(16 * CAP, T).astype(BF), tok).reshape(16, CAP, D))
            hot_in[o] = dot(hpick.astype(BF), tok).astype(BF)
        slots[...] = jnp.concatenate(parts, axis=1).astype(BF)

    return pl.pallas_call(
        kernel,
        in_specs=[pl.BlockSpec(memory_space=pltpu.SMEM)]
        + [pl.BlockSpec(memory_space=pltpu.VMEM)] * n,
        out_shape=[
            jax.ShapeDtypeStruct((16, CAP * n, D), BF),
            jax.ShapeDtypeStruct((n, 2 * HOT, D), BF),
            jax.ShapeDtypeStruct((n, 16, T), BF),
        ],
        cost_estimate=pl.CostEstimate(
            flops=75_000_000 * n, bytes_accessed=800_000 * n, transcendentals=0
        ),
        compiler_params=VMEM,
        name=f"send_part_{n}",
    )(scal, *pays)


def cots_kernel(scal, meta, cot_a, cot_b, slots, hot_cot):
    parts = []
    for o, ref in enumerate((cot_a, cot_b)):
        pick, weight, hpick, hweight = column_parts(meta[o], scal)
        cot = ref[0]
        rows = dot(pick.reshape(16 * CAP, T).astype(BF), cot).reshape(16, CAP, D)
        parts.append(rows * jnp.sum(weight, axis=2, keepdims=True))
        hot_rows = dot(hpick.astype(BF), cot) * jnp.sum(hweight, axis=1, keepdims=True)
        hot_cot[o] = hot_rows.astype(BF)
    slots[...] = jnp.concatenate(parts, axis=1).astype(BF)


def send_cots(scal, meta, cots):
    def at(odd):
        return pl.BlockSpec((1, T, D), lambda g, s: (s[3 + 2 * g + odd], 0, 0))

    return pl.pallas_call(
        cots_kernel,
        grid_spec=pltpu.PrefetchScalarGridSpec(
            num_scalar_prefetch=1,
            grid=(4,),
            in_specs=[pl.BlockSpec((2, 16, T), lambda g, s: (g, 0, 0)), at(0), at(1)],
            out_specs=[
                pl.BlockSpec((16, 16, D), lambda g, s: (0, g, 0)),
                pl.BlockSpec((2, 2 * HOT, D), lambda g, s: (g, 0, 0)),
            ],
        ),
        out_shape=[
            jax.ShapeDtypeStruct((16, 64, D), BF),
            jax.ShapeDtypeStruct((NZ, 2 * HOT, D), BF),
        ],
        cost_estimate=pl.CostEstimate(flops=600_000_000, bytes_accessed=7_000_000, transcendentals=0),
        compiler_params=VMEM,
        name="send_cots",
    )(scal, meta, cots, cots)


def merge_kernel(scal, meta, rows, hot_rows, total):
    odd = lax.rem(pl.program_id(0), 2) == 1
    _, weight, hpick, hweight = column_parts(meta[0], scal)
    block = rows[...].astype(F32)
    mine = jnp.where(odd, block[:, CAP:, :], block[:, :CAP, :])
    mine = mine.reshape(16 * CAP, D).astype(BF)
    hot = hot_rows[0] * jnp.sum(hweight, axis=1, keepdims=True)
    weight = weight.reshape(16 * CAP, T).T
    high = weight.astype(BF)
    low = (weight - high.astype(F32)).astype(BF)
    out = dot(hpick.T.astype(BF), hot.astype(BF)) + dot(high, mine) + dot(low, mine)
    total[0] = out.astype(BF)


def merge_gated(scal, meta, rows, hot_rows):
    return pl.pallas_call(
        merge_kernel,
        grid_spec=pltpu.PrefetchScalarGridSpec(
            num_scalar_prefetch=1,
            grid=(NZ,),
            in_specs=[
                pl.BlockSpec((1, 16, T), lambda g, s: (g, 0, 0)),
                pl.BlockSpec((16, 16, D), lambda g, s: (0, g // 2, 0)),
                pl.BlockSpec((1, 2 * HOT, D), lambda g, s: (g, 0, 0)),
            ],
            out_specs=pl.BlockSpec((1, T, D), lambda g, s: (s[3 + g], 0, 0)),
        ),
        out_shape=jax.ShapeDtypeStruct((NZ, T, D), BF),
        cost_estimate=pl.CostEstimate(flops=900_000_000, bytes_accessed=7_000_000, transcendentals=0),
        compiler_params=VMEM,
        name="merge_gated",
    )(scal, meta, rows, hot_rows)


def merge_plain(scal, meta, rows, hot_rows, start):
    n = rows.shape[1] // CAP

    def kernel(scal, meta, rows, hot_rows, *outs):
        block = rows[...].astype(F32)
        for o in range(n):
            pick, _, hpick, _ = column_parts(meta[start + o], scal)
            mine = block[:, CAP * o : CAP * o + CAP, :].reshape(16 * CAP, D).astype(BF)
            out = dot(pick.reshape(16 * CAP, T).T.astype(BF), mine)
            out = out + dot(hpick.T.astype(BF), hot_rows[start + o].astype(BF))
            outs[o][...] = out.astype(BF)

    return pl.pallas_call(
        kernel,
        in_specs=[pl.BlockSpec(memory_space=pltpu.SMEM)]
        + [pl.BlockSpec(memory_space=pltpu.VMEM)] * 3,
        out_shape=[jax.ShapeDtypeStruct((T, D), BF)] * n,
        cost_estimate=pl.CostEstimate(
            flops=75_000_000 * n, bytes_accessed=1_000_000 * n, transcendentals=0
        ),
        compiler_params=VMEM,
        name=f"merge_plain_{n}",
    )(scal, meta, rows, hot_rows)


def silu_slope(pre):
    sig = jax.nn.sigmoid(pre)
    return sig * (1.0 + pre * (1.0 - sig))


def hot_kernel(rows_in, rows_cot, weights, out, back, grads):
    x = rows_in[...].reshape(NZ * HOT, D)
    c = rows_cot[...].reshape(NZ * HOT, D)
    gate_w = weights[0, 0:SLICE, :]
    up_w = weights[0, SLICE : 2 * SLICE, :]
    down_w = weights[0, 2 * SLICE : 3 * SLICE, :]
    pre_gate = dot_t(x, gate_w)
    pre_up = dot_t(x, up_w)
    sig = 1.0 / (1.0 + jnp.exp(-pre_gate))
    active = pre_gate * sig
    hidden = active * pre_up
    out[...] = dot(hidden.astype(BF), down_w).reshape(NZ, HOT, D)
    grad_hidden = dot_t(c, down_w)
    grad_pg = grad_hidden * pre_up * (sig * (1.0 + pre_gate * (1.0 - sig)))
    grad_pu = grad_hidden * active
    back[...] = (dot(grad_pg.astype(BF), gate_w) + dot(grad_pu.astype(BF), up_w)).reshape(NZ, HOT, D)
    grads[0, 0:SLICE, :] = dot(grad_pg.T.astype(BF), x)
    grads[0, SLICE : 2 * SLICE, :] = dot(grad_pu.T.astype(BF), x)
    grads[0, 2 * SLICE : 3 * SLICE, :] = dot(hidden.T.astype(BF), c)


def hot_pass(hot_in, hot_cot, weights):
    rows = jax.ShapeDtypeStruct((NZ, 2 * HOT, D), F32)
    return pl.pallas_call(
        hot_kernel,
        grid=(2,),
        in_specs=[
            pl.BlockSpec((NZ, HOT, D), lambda h: (0, h, 0)),
            pl.BlockSpec((NZ, HOT, D), lambda h: (0, h, 0)),
            pl.BlockSpec((1, 3 * SLICE, D), lambda h: (h, 0, 0)),
        ],
        out_specs=[
            pl.BlockSpec((NZ, HOT, D), lambda h: (0, h, 0)),
            pl.BlockSpec((NZ, HOT, D), lambda h: (0, h, 0)),
            pl.BlockSpec((1, 3 * SLICE, D), lambda h: (h, 0, 0)),
        ],
        out_shape=[rows, rows, jax.ShapeDtypeStruct((2, 3 * SLICE, D), F32)],
        cost_estimate=pl.CostEstimate(flops=600_000_000, bytes_accessed=6_000_000, transcendentals=20_000),
        compiler_params=VMEM,
        name="hot_pass",
    )(hot_in, hot_cot, weights)


def spread_sum(v, axis):
    n = lax.axis_size(axis)
    moved = [
        lax.ppermute(v, axis, [(i, (i + s) % n) for i in range(n)]) for s in range(1, n)
    ]
    total = v.astype(F32)
    for m in moved:
        total = total + m.astype(F32)
    return total.astype(v.dtype)


def up(v):
    return lax.ppermute(v, "z", [(i, (i + 1) % NZ) for i in range(NZ)])


def down(v):
    return lax.ppermute(v, "z", [((i + 1) % NZ, i) for i in range(NZ)])


def tie(v, *others):
    return lax.optimization_barrier((v, *others))[0]


def ring_gather(v, *others):
    below, above = [v], [v]
    for step in range(4):
        last = tie(below[-1], *others) if step == 1 and others else below[-1]
        below.append(up(last))
        if step < 3:
            above.append(down(above[-1]))
    return below[:0:-1] + above


def add(a, b):
    return (a.astype(F32) + b.astype(F32)).astype(BF)


def ring_sum(parts):
    rising, falling = up(parts[0]), down(parts[1])
    for step in range(3):
        rising = up(add(rising, parts[7 - step]))
        if step < 2:
            falling = down(add(falling, parts[2 + step]))
    return (parts[4].astype(F32) + rising.astype(F32) + falling.astype(F32)).astype(BF)


def swap(v):
    return lax.ppermute(v, "dp", [(0, 1), (1, 0)])


def half_sum(v, dp, dim):
    size = v.shape[dim] // 2
    mine = lax.dynamic_slice_in_dim(v, dp * size, size, dim)
    other = lax.dynamic_slice_in_dim(v, (1 - dp) * size, size, dim)
    return mine + swap(other)


def exchange(v, axes):
    return lax.all_to_all(v, axes, split_axis=0, concat_axis=0, tiled=True)


def shards(tokens, cotangent, route, numer, w_gate, w_up, w_down):
    dp = lax.axis_index("dp")
    z = lax.axis_index("z")
    me = z * 16 + lax.axis_index("x") * 4 + lax.axis_index("y")
    gate_w, up_w, down_w = w_gate[0], w_up[0], w_down[0]
    plane = ("x", "y")

    pay, info = pl.pallas_call(
        send_kernel,
        out_shape=[
            jax.ShapeDtypeStruct((PAY, D), BF),
            jax.ShapeDtypeStruct((8, T), jnp.int32),
        ],
        cost_estimate=pl.CostEstimate(flops=10_000_000, bytes_accessed=700_000, transcendentals=0),
        compiler_params=VMEM,
        name="send",
    )(tokens, route.T, numer.T)
    first, second = info[0, 0], info[1, 0]
    places_z = [lax.rem(z + g + 4, NZ) for g in ORDER]
    scal = jnp.stack([first, second, z * 16, *places_z]).astype(jnp.int32)

    wcat = jnp.concatenate(
        [w.reshape(NZ, SLICE, D) for w in (gate_w.T, up_w.T, down_w)], axis=1
    )
    named = jnp.where(me == jnp.where(dp == 0, first, second), wcat, jnp.zeros((), BF))
    hot_w = lax.psum_scatter(
        named.reshape(NZ * 3 * SLICE, D), "z", scatter_dimension=0, tiled=True
    )

    cots = lax.all_gather(tie(cotangent, hot_w), "z")

    ring = ring_gather(pay, named)
    sent_in, hot_in, meta = send_part(scal, [ring[g] for g in ORDER])
    recv_in = exchange(sent_in, plane)

    hot_w = spread_sum(spread_sum(hot_w, "x"), "y")
    other_w = swap(hot_w)
    hot_w = jnp.where(dp == 0, jnp.stack([hot_w, other_w]), jnp.stack([other_w, hot_w]))
    sent_cot, hot_cot = send_cots(scal, meta, cots)
    sent_cot, recv_in, hot_w = lax.optimization_barrier((sent_cot, recv_in, hot_w))
    recv_cot = exchange(sent_cot, plane)

    hot_out, hot_back, hot_grads = hot_pass(hot_in, hot_cot, hot_w)
    hot_g = half_sum(hot_grads.reshape(2 * 3 * SLICE, D), dp, 1).astype(BF)

    hot_g = spread_sum(hot_g, "x")
    rows_in = recv_in.reshape(T * CAP, D)
    pre_gate = dot(rows_in, gate_w)
    pre_up = dot(rows_in, up_w)
    active = jax.nn.silu(pre_gate)
    hidden = (active * pre_up).astype(BF)
    result = dot(hidden, down_w).astype(BF)
    result, recv_cot, hot_g = lax.optimization_barrier((result, recv_cot, hot_g))
    back_out = exchange(result.reshape(16, 64, D), plane)
    hot_g = spread_sum(hot_g, "y")

    rows_cot = recv_cot.reshape(T * CAP, D)
    grad_hidden = dot_t(rows_cot, down_w)
    grad_pg = (grad_hidden * pre_up * silu_slope(pre_gate)).astype(BF)
    grad_pu = (grad_hidden * active).astype(BF)
    back = (dot_t(grad_pg, gate_w) + dot_t(grad_pu, up_w)).astype(BF)
    back, back_out, hot_g = lax.optimization_barrier((back, back_out, hot_g))
    back = back.reshape(16, 64, D)
    back_far = exchange(back[:, CAP * LAST :], plane)
    total = merge_gated(scal, meta, back_out, hot_out)
    hot_g, total = lax.optimization_barrier((hot_g, total))
    output = lax.psum_scatter(
        total.reshape(NZ * T, D), "z", scatter_dimension=0, tiled=True
    )
    back_near = exchange(tie(back[:, : CAP * LAST], back_far), plane)
    merged = merge_plain(scal, meta, back_far, hot_back, LAST)
    merged = merge_plain(scal, meta, back_near, hot_back, 0) + merged
    grad_tokens = ring_sum([merged[ORDER.index(g)] for g in range(NZ)])

    hot_g = [g.reshape(2, 3, SLICE, D // 2) for g in ring_gather(hot_g)]
    hot_g = jnp.stack([jnp.where(me == first, g[0], g[1]) for g in hot_g])
    hot_g = jnp.roll(hot_g, z - 4, axis=0).astype(F32)
    is_hot = (me == first) | (me == second)

    def pieces(i):
        return hot_g[:, i].reshape(FF, D // 2)

    def grad(a, b):
        return lax.dot_general(a, b, (((0,), (0,)), ((), ())), preferred_element_type=F32)

    cold_gate = half_sum(grad(rows_in, grad_pg), dp, 0)
    cold_up = half_sum(grad(rows_in, grad_pu), dp, 0)
    cold_down = half_sum(grad(hidden, rows_cot), dp, 1)
    grad_gate = jnp.where(is_hot, pieces(0).T, cold_gate)
    grad_up = jnp.where(is_hot, pieces(1).T, cold_up)
    grad_down = jnp.where(is_hot, pieces(2), cold_down)
    return (output, grad_tokens, grad_gate[None], grad_up[None], grad_down[None])


def solution(mesh):
    cube = Mesh(mesh.devices.reshape(2, 8, 4, 4), ("dp", "z", "x", "y"))
    owner = ("z", "x", "y")
    rows = P(("dp", "z", "x", "y"), None)
    weights = P(owner, None, None)
    return jax.shard_map(
        shards,
        mesh=cube,
        in_specs=(rows, rows, rows, rows, weights, weights, weights),
        out_specs=(
            rows,
            rows,
            P(owner, "dp", None),
            P(owner, "dp", None),
            P(owner, None, "dp"),
        ),
        check_vma=False,
    )
```

```python
import jax
import jax.numpy as jnp
from jax import lax
from jax.experimental import pallas as pl
from jax.experimental.pallas import tpu as pltpu
from jax.sharding import Mesh, PartitionSpec as P

BF = jnp.bfloat16
F32 = jnp.float32
D = 1024
FF = 384
T = 128
CAP = 8
HOT = 16
NZ = 8
SLICE = FF // NZ
PAY = T + 16
ORDER = (3, 4, 5, 2, 6, 0, 1, 7)
EXTRA = 16
PIECE = 72
VMEM = pltpu.CompilerParams(vmem_limit_bytes=48 * 1024 * 1024)


def iota(shape, dim):
    return lax.broadcasted_iota(jnp.int32, shape, dim).astype(F32)


def before():
    return (iota((T, T), 0) < iota((T, T), 1)).astype(BF)


def dot(a, b):
    return jnp.dot(a, b, preferred_element_type=F32)


def dot_t(a, b):
    return lax.dot_general(a, b, (((1,), (1,)), ((), ())), preferred_element_type=F32)


def members(route, gates, expert):
    hit = jnp.zeros(expert.shape, F32)
    gate = jnp.zeros(expert.shape, F32)
    for k in range(8):
        same = route[k : k + 1, :] == expert
        hit = hit + jnp.where(same, 1.0, 0.0)
        if gates is not None:
            gate = gate + jnp.where(same, gates[k : k + 1, :], 0.0)
    return hit, gate


def places(hit):
    return jnp.where(hit > 0.5, dot(hit.astype(BF), before()), -1.0)


def cold_pick(place):
    n = place.shape[0]
    return jnp.where(place[:, None, :] == iota((n, CAP, T), 1), 1.0, 0.0)


def hot_pick(place2):
    want = iota((HOT, T), 0)
    return jnp.concatenate(
        [jnp.where(place2[h : h + 1, :] == want, 1.0, 0.0) for h in range(2)], axis=0
    )


def send_kernel(tok, route, numer, pay, info):
    r = route[...].astype(F32)
    hit, _ = members(r, None, iota((T, T), 0))
    hot = jnp.sum(hit, axis=1, keepdims=True) > CAP + 0.5
    ids = iota((T, 1), 0)
    first = jnp.min(jnp.where(hot, ids, 1000.0), axis=0, keepdims=True)
    second = jnp.max(jnp.where(hot, ids, -1.0), axis=0, keepdims=True)
    info[...] = jnp.where(iota((8, T), 0) == 0.0, first, second).astype(jnp.int32)
    pay[0:T, :] = tok[...]
    pay[T:PAY, :] = jnp.zeros((16, D), BF)
    pay[T:PAY, 0:T] = jnp.concatenate([r, numer[...].astype(F32)], axis=0).astype(BF)


def column_parts(meta, scal):
    meta = meta.astype(F32)
    route, numer = meta[0:8], meta[8:16]
    gates = numer / jnp.sum(numer, axis=0, keepdims=True)
    first = scal[0].astype(F32)
    second = scal[1].astype(F32)
    expert = iota((16, T), 0) + scal[2].astype(F32)
    hit, gate = members(route, gates, expert)
    place = places(hit)
    place = jnp.where((expert == first) | (expert == second), -1.0, place)
    hot_expert = jnp.where(iota((8, T), 0) == 0.0, first, second)
    hot_hit, hot_gate = members(route, gates, hot_expert)
    pick = cold_pick(place)
    weight = pick * gate[:, None, :]
    hpick = hot_pick(places(hot_hit))
    hgate = jnp.concatenate(
        [jnp.broadcast_to(hot_gate[h : h + 1, :], (HOT, T)) for h in range(2)], axis=0
    )
    hweight = hpick * hgate
    return pick, weight, hpick, hweight


def send_part(scal, piece, pays):
    n = len(pays)

    def kernel(scal, piece, *refs):
        slots, hot_in, meta = refs[n:]
        parts = []
        for o in range(n):
            small = refs[o][T:PAY, 0:T]
            meta[o] = small
            pick, _, hpick, _ = column_parts(small, scal)
            tok = refs[o][0:T, :]
            parts.append(dot(pick.reshape(16 * CAP, T).astype(BF), tok).reshape(16, CAP, D))
            hot_in[o] = dot(hpick.astype(BF), tok).astype(BF)
        parts.append(jnp.broadcast_to(piece[...].astype(F32)[None], (16, EXTRA, D)))
        slots[...] = jnp.concatenate(parts, axis=1).astype(BF)

    return pl.pallas_call(
        kernel,
        in_specs=[pl.BlockSpec(memory_space=pltpu.SMEM)]
        + [pl.BlockSpec(memory_space=pltpu.VMEM)] * (n + 1),
        out_shape=[
            jax.ShapeDtypeStruct((16, CAP * n + EXTRA, D), BF),
            jax.ShapeDtypeStruct((n, 2 * HOT, D), BF),
            jax.ShapeDtypeStruct((n, 16, T), BF),
        ],
        cost_estimate=pl.CostEstimate(
            flops=75_000_000 * n, bytes_accessed=800_000 * n, transcendentals=0
        ),
        compiler_params=VMEM,
        name=f"send_part_{n}",
    )(scal, piece, *pays)


def cots_kernel(scal, meta, cot_a, cot_b, slots, hot_cot):
    parts = []
    for o, ref in enumerate((cot_a, cot_b)):
        pick, weight, hpick, hweight = column_parts(meta[o], scal)
        cot = ref[0]
        rows = dot(pick.reshape(16 * CAP, T).astype(BF), cot).reshape(16, CAP, D)
        parts.append(rows * jnp.sum(weight, axis=2, keepdims=True))
        hot_rows = dot(hpick.astype(BF), cot) * jnp.sum(hweight, axis=1, keepdims=True)
        hot_cot[o] = hot_rows.astype(BF)
    slots[...] = jnp.concatenate(parts, axis=1).astype(BF)


def send_cots(scal, meta, cots):
    def at(odd):
        return pl.BlockSpec((1, T, D), lambda g, s: (s[3 + 2 * g + odd], 0, 0))

    return pl.pallas_call(
        cots_kernel,
        grid_spec=pltpu.PrefetchScalarGridSpec(
            num_scalar_prefetch=1,
            grid=(4,),
            in_specs=[pl.BlockSpec((2, 16, T), lambda g, s: (g, 0, 0)), at(0), at(1)],
            out_specs=[
                pl.BlockSpec((16, 16, D), lambda g, s: (0, g, 0)),
                pl.BlockSpec((2, 2 * HOT, D), lambda g, s: (g, 0, 0)),
            ],
        ),
        out_shape=[
            jax.ShapeDtypeStruct((16, 64, D), BF),
            jax.ShapeDtypeStruct((NZ, 2 * HOT, D), BF),
        ],
        cost_estimate=pl.CostEstimate(flops=600_000_000, bytes_accessed=7_000_000, transcendentals=0),
        compiler_params=VMEM,
        name="send_cots",
    )(scal, meta, cots, cots)


def merge_kernel(scal, meta, rows, hot_rows, total):
    odd = lax.rem(pl.program_id(0), 2) == 1
    _, weight, hpick, hweight = column_parts(meta[0], scal)
    block = rows[...].astype(F32)
    mine = jnp.where(odd, block[:, CAP:, :], block[:, :CAP, :])
    mine = mine.reshape(16 * CAP, D).astype(BF)
    hot = hot_rows[0] * jnp.sum(hweight, axis=1, keepdims=True)
    weight = weight.reshape(16 * CAP, T).T
    high = weight.astype(BF)
    low = (weight - high.astype(F32)).astype(BF)
    out = dot(hpick.T.astype(BF), hot.astype(BF)) + dot(high, mine) + dot(low, mine)
    total[0] = out.astype(BF)


def merge_gated(scal, meta, rows, hot_rows):
    return pl.pallas_call(
        merge_kernel,
        grid_spec=pltpu.PrefetchScalarGridSpec(
            num_scalar_prefetch=1,
            grid=(NZ,),
            in_specs=[
                pl.BlockSpec((1, 16, T), lambda g, s: (g, 0, 0)),
                pl.BlockSpec((16, 16, D), lambda g, s: (0, g // 2, 0)),
                pl.BlockSpec((1, 2 * HOT, D), lambda g, s: (g, 0, 0)),
            ],
            out_specs=pl.BlockSpec((1, T, D), lambda g, s: (s[3 + g], 0, 0)),
        ),
        out_shape=jax.ShapeDtypeStruct((NZ, T, D), BF),
        cost_estimate=pl.CostEstimate(flops=900_000_000, bytes_accessed=7_000_000, transcendentals=0),
        compiler_params=VMEM,
        name="merge_gated",
    )(scal, meta, rows, hot_rows)


def merge_plain(scal, meta, rows, hot_rows):
    n = rows.shape[1] // CAP

    def kernel(scal, meta, rows, hot_rows, *outs):
        block = rows[...].astype(F32)
        for o in range(n):
            pick, _, hpick, _ = column_parts(meta[o], scal)
            mine = block[:, CAP * o : CAP * o + CAP, :].reshape(16 * CAP, D).astype(BF)
            out = dot(pick.reshape(16 * CAP, T).T.astype(BF), mine)
            out = out + dot(hpick.T.astype(BF), hot_rows[o].astype(BF))
            outs[o][...] = out.astype(BF)

    return pl.pallas_call(
        kernel,
        in_specs=[pl.BlockSpec(memory_space=pltpu.SMEM)]
        + [pl.BlockSpec(memory_space=pltpu.VMEM)] * 3,
        out_shape=[jax.ShapeDtypeStruct((T, D), BF)] * n,
        cost_estimate=pl.CostEstimate(
            flops=75_000_000 * n, bytes_accessed=1_000_000 * n, transcendentals=0
        ),
        compiler_params=VMEM,
        name=f"merge_plain_{n}",
    )(scal, meta, rows, hot_rows)


def silu_slope(pre):
    sig = jax.nn.sigmoid(pre)
    return sig * (1.0 + pre * (1.0 - sig))


def hot_kernel(rows_in, rows_cot, weights, out, back, grads):
    x = rows_in[...].reshape(NZ * HOT, D)
    c = rows_cot[...].reshape(NZ * HOT, D)
    gate_w = weights[0, 0:SLICE, :]
    up_w = weights[0, SLICE : 2 * SLICE, :]
    down_w = weights[0, 2 * SLICE : 3 * SLICE, :]
    pre_gate = dot_t(x, gate_w)
    pre_up = dot_t(x, up_w)
    sig = 1.0 / (1.0 + jnp.exp(-pre_gate))
    active = pre_gate * sig
    hidden = active * pre_up
    out[...] = dot(hidden.astype(BF), down_w).reshape(NZ, HOT, D)
    grad_hidden = dot_t(c, down_w)
    grad_pg = grad_hidden * pre_up * (sig * (1.0 + pre_gate * (1.0 - sig)))
    grad_pu = grad_hidden * active
    back[...] = (dot(grad_pg.astype(BF), gate_w) + dot(grad_pu.astype(BF), up_w)).reshape(NZ, HOT, D)
    grads[0, 0:SLICE, :] = dot(grad_pg.T.astype(BF), x)
    grads[0, SLICE : 2 * SLICE, :] = dot(grad_pu.T.astype(BF), x)
    grads[0, 2 * SLICE : 3 * SLICE, :] = dot(hidden.T.astype(BF), c)


def hot_pass(hot_in, hot_cot, weights):
    rows = jax.ShapeDtypeStruct((NZ, 2 * HOT, D), F32)
    return pl.pallas_call(
        hot_kernel,
        grid=(2,),
        in_specs=[
            pl.BlockSpec((NZ, HOT, D), lambda h: (0, h, 0)),
            pl.BlockSpec((NZ, HOT, D), lambda h: (0, h, 0)),
            pl.BlockSpec((1, 3 * SLICE, D), lambda h: (h, 0, 0)),
        ],
        out_specs=[
            pl.BlockSpec((NZ, HOT, D), lambda h: (0, h, 0)),
            pl.BlockSpec((NZ, HOT, D), lambda h: (0, h, 0)),
            pl.BlockSpec((1, 3 * SLICE, D), lambda h: (h, 0, 0)),
        ],
        out_shape=[rows, rows, jax.ShapeDtypeStruct((2, 3 * SLICE, D), F32)],
        cost_estimate=pl.CostEstimate(flops=600_000_000, bytes_accessed=6_000_000, transcendentals=20_000),
        compiler_params=VMEM,
        name="hot_pass",
    )(hot_in, hot_cot, weights)


def up(v):
    return lax.ppermute(v, "z", [(i, (i + 1) % NZ) for i in range(NZ)])


def down(v):
    return lax.ppermute(v, "z", [((i + 1) % NZ, i) for i in range(NZ)])


def tie(v, *others):
    return lax.optimization_barrier((v, *others))[0]


def ring_gather(v, *others):
    below, above = [v], [v]
    for step in range(4):
        last = tie(below[-1], *others) if step == 3 and others else below[-1]
        below.append(up(last))
        if step < 3:
            above.append(down(above[-1]))
    return below[:0:-1] + above


def add(a, b):
    return (a.astype(F32) + b.astype(F32)).astype(BF)


def ring_sum(parts):
    rising, falling = up(parts[0]), down(parts[1])
    for step in range(3):
        rising = up(add(rising, parts[7 - step]))
        if step < 2:
            falling = down(add(falling, parts[2 + step]))
    return (parts[4].astype(F32) + rising.astype(F32) + falling.astype(F32)).astype(BF)


def swap(v):
    return lax.ppermute(v, "dp", [(0, 1), (1, 0)])


def half_sum(v, dp, dim):
    size = v.shape[dim] // 2
    mine = lax.dynamic_slice_in_dim(v, dp * size, size, dim)
    other = lax.dynamic_slice_in_dim(v, (1 - dp) * size, size, dim)
    return mine + swap(other)


def exchange(v, axes):
    return lax.all_to_all(v, axes, split_axis=0, concat_axis=0, tiled=True)


def shards(tokens, cotangent, route, numer, w_gate, w_up, w_down):
    dp = lax.axis_index("dp")
    z = lax.axis_index("z")
    me = z * 16 + lax.axis_index("x") * 4 + lax.axis_index("y")
    gate_w, up_w, down_w = w_gate[0], w_up[0], w_down[0]
    plane = ("x", "y")

    pay, info = pl.pallas_call(
        send_kernel,
        out_shape=[
            jax.ShapeDtypeStruct((PAY, D), BF),
            jax.ShapeDtypeStruct((8, T), jnp.int32),
        ],
        cost_estimate=pl.CostEstimate(flops=10_000_000, bytes_accessed=700_000, transcendentals=0),
        compiler_params=VMEM,
        name="send",
    )(tokens, route.T, numer.T)
    first, second = info[0, 0], info[1, 0]
    places_z = [lax.rem(z + g + 4, NZ) for g in ORDER]
    scal = jnp.stack([first, second, z * 16, *places_z]).astype(jnp.int32)

    wcat = jnp.concatenate(
        [w.reshape(NZ, SLICE, D) for w in (gate_w.T, up_w.T, down_w)], axis=1
    )
    wcat = wcat.reshape(NZ, 2, PIECE, 8, T).transpose(1, 3, 0, 2, 4)
    owner = jnp.where(dp == 0, first, second)
    plane_w = exchange(wcat.reshape(16, NZ * PIECE, T), plane)
    plane_w = lax.dynamic_index_in_dim(plane_w, lax.rem(owner, 16), 0, keepdims=False)
    piece = exchange(plane_w.reshape(NZ, PIECE, T), "z")
    piece = lax.dynamic_index_in_dim(piece, owner // 16, 0, keepdims=False)
    piece = jnp.pad(piece.reshape(9, D), ((0, EXTRA - 9), (0, 0)))

    cots = lax.all_gather(cotangent, "z")
    ring = ring_gather(pay, plane_w)
    sent_in, hot_in, meta = send_part(scal, piece, [ring[g] for g in ORDER])
    recv_in = exchange(sent_in, plane)

    sent_cot, hot_cot = send_cots(scal, meta, cots)
    sent_cot, recv_in = lax.optimization_barrier((sent_cot, recv_in))
    recv_cot = exchange(sent_cot, plane)

    hot_w = recv_in[:, 64:73].reshape(2, 8, PIECE, T).transpose(0, 2, 1, 3)
    hot_w = hot_w.reshape(3 * SLICE, D)
    other_w = swap(hot_w)
    hot_w = jnp.where(dp == 0, jnp.stack([hot_w, other_w]), jnp.stack([other_w, hot_w]))
    hot_out, hot_back, hot_grads = hot_pass(hot_in, hot_cot, hot_w)
    hot_g = half_sum(hot_grads.reshape(2 * 3 * SLICE, D), dp, 1).astype(BF)
    hot_g = hot_g.reshape(4, PIECE, 4, T).transpose(0, 2, 1, 3).reshape(16, 9, D)
    hot_g = jnp.pad(hot_g, ((0, 0), (0, EXTRA - 9), (0, 0)))

    rows_in = recv_in[:, :64].reshape(T * CAP, D)
    pre_gate = dot(rows_in, gate_w)
    pre_up = dot(rows_in, up_w)
    active = jax.nn.silu(pre_gate)
    hidden = (active * pre_up).astype(BF)
    result = dot(hidden, down_w).astype(BF)
    sent_out = jnp.concatenate([result.reshape(16, 64, D), hot_g], axis=1)
    sent_out, recv_cot = lax.optimization_barrier((sent_out, recv_cot))
    back_out = exchange(sent_out, plane)

    rows_cot = recv_cot.reshape(T * CAP, D)
    grad_hidden = dot_t(rows_cot, down_w)
    grad_pg = (grad_hidden * pre_up * silu_slope(pre_gate)).astype(BF)
    grad_pu = (grad_hidden * active).astype(BF)
    back = (dot_t(grad_pg, gate_w) + dot_t(grad_pu, up_w)).astype(BF)
    back, back_out = lax.optimization_barrier((back, back_out))
    back_grad = exchange(back.reshape(16, 64, D), plane)

    total = merge_gated(scal, meta, back_out, hot_out)
    output = lax.psum_scatter(
        total.reshape(NZ * T, D), "z", scatter_dimension=0, tiled=True
    )
    merged = merge_plain(scal, meta, back_grad, hot_back)
    grad_tokens = ring_sum([merged[ORDER.index(g)] for g in range(NZ)])

    hot_g = jnp.sum(back_out[:, 64:73].astype(F32), axis=0).astype(BF)
    hot_g = jnp.stack(ring_gather(hot_g.reshape(PIECE, T)))
    hot_g = jnp.roll(hot_g, z - 4, axis=0).reshape(1, NZ * PIECE, T)
    hot_g = jnp.broadcast_to(tie(hot_g, back_grad), (16, NZ * PIECE, T))
    hot_g = exchange(hot_g, plane)
    hot_g = lax.dynamic_slice_in_dim(hot_g, jnp.where(me == first, 0, 8), 8, 0)
    hot_g = hot_g.reshape(2, 4, NZ, PIECE, T).transpose(2, 0, 3, 1, 4)
    hot_g = hot_g.reshape(NZ, 3, SLICE, D // 2).astype(F32)
    is_hot = (me == first) | (me == second)

    def pieces(i):
        return hot_g[:, i].reshape(FF, D // 2)

    def grad(a, b):
        return lax.dot_general(a, b, (((0,), (0,)), ((), ())), preferred_element_type=F32)

    cold_gate = half_sum(grad(rows_in, grad_pg), dp, 0)
    cold_up = half_sum(grad(rows_in, grad_pu), dp, 0)
    cold_down = half_sum(grad(hidden, rows_cot), dp, 1)
    grad_gate = jnp.where(is_hot, pieces(0).T, cold_gate)
    grad_up = jnp.where(is_hot, pieces(1).T, cold_up)
    grad_down = jnp.where(is_hot, pieces(2), cold_down)
    return (output, grad_tokens, grad_gate[None], grad_up[None], grad_down[None])


def solution(mesh):
    cube = Mesh(mesh.devices.reshape(2, 8, 4, 4), ("dp", "z", "x", "y"))
    owner = ("z", "x", "y")
    rows = P(("dp", "z", "x", "y"), None)
    weights = P(owner, None, None)
    return jax.shard_map(
        shards,
        mesh=cube,
        in_specs=(rows, rows, rows, rows, weights, weights, weights),
        out_specs=(
            rows,
            rows,
            P(owner, "dp", None),
            P(owner, "dp", None),
            P(owner, None, "dp"),
        ),
        check_vma=False,
    )
```

```python
import jax
import jax.numpy as jnp
from jax import lax
from jax.experimental import pallas as pl
from jax.experimental.pallas import tpu as pltpu
from jax.sharding import Mesh, PartitionSpec as P

BF = jnp.bfloat16
F32 = jnp.float32
D = 1024
FF = 384
T = 128
CAP = 8
HOT = 16
NZ = 8
SLICE = FF // NZ
PAY = T + 16
ORDER = (3, 4, 5, 2, 6, 0, 1, 7)
EXTRA = 16
PIECE = 72
VMEM = pltpu.CompilerParams(vmem_limit_bytes=48 * 1024 * 1024)


def iota(shape, dim):
    return lax.broadcasted_iota(jnp.int32, shape, dim).astype(F32)


def before():
    return (iota((T, T), 0) < iota((T, T), 1)).astype(BF)


def dot(a, b):
    return jnp.dot(a, b, preferred_element_type=F32)


def dot_t(a, b):
    return lax.dot_general(a, b, (((1,), (1,)), ((), ())), preferred_element_type=F32)


def members(route, gates, expert):
    hit = jnp.zeros(expert.shape, F32)
    gate = jnp.zeros(expert.shape, F32)
    for k in range(8):
        same = route[k : k + 1, :] == expert
        hit = hit + jnp.where(same, 1.0, 0.0)
        if gates is not None:
            gate = gate + jnp.where(same, gates[k : k + 1, :], 0.0)
    return hit, gate


def places(hit):
    return jnp.where(hit > 0.5, dot(hit.astype(BF), before()), -1.0)


def cold_pick(place):
    n = place.shape[0]
    return jnp.where(place[:, None, :] == iota((n, CAP, T), 1), 1.0, 0.0)


def hot_pick(place2):
    want = iota((HOT, T), 0)
    return jnp.concatenate(
        [jnp.where(place2[h : h + 1, :] == want, 1.0, 0.0) for h in range(2)], axis=0
    )


def send_kernel(tok, route, numer, pay, info):
    r = route[...].astype(F32)
    hit, _ = members(r, None, iota((T, T), 0))
    hot = jnp.sum(hit, axis=1, keepdims=True) > CAP + 0.5
    ids = iota((T, 1), 0)
    first = jnp.min(jnp.where(hot, ids, 1000.0), axis=0, keepdims=True)
    second = jnp.max(jnp.where(hot, ids, -1.0), axis=0, keepdims=True)
    info[...] = jnp.where(iota((8, T), 0) == 0.0, first, second).astype(jnp.int32)
    pay[0:T, :] = tok[...]
    pay[T:PAY, :] = jnp.zeros((16, D), BF)
    pay[T:PAY, 0:T] = jnp.concatenate([r, numer[...].astype(F32)], axis=0).astype(BF)


def column_parts(meta, scal):
    meta = meta.astype(F32)
    route, numer = meta[0:8], meta[8:16]
    gates = numer / jnp.sum(numer, axis=0, keepdims=True)
    first = scal[0].astype(F32)
    second = scal[1].astype(F32)
    expert = iota((16, T), 0) + scal[2].astype(F32)
    hit, gate = members(route, gates, expert)
    place = places(hit)
    place = jnp.where((expert == first) | (expert == second), -1.0, place)
    hot_expert = jnp.where(iota((8, T), 0) == 0.0, first, second)
    hot_hit, hot_gate = members(route, gates, hot_expert)
    pick = cold_pick(place)
    weight = pick * gate[:, None, :]
    hpick = hot_pick(places(hot_hit))
    hgate = jnp.concatenate(
        [jnp.broadcast_to(hot_gate[h : h + 1, :], (HOT, T)) for h in range(2)], axis=0
    )
    hweight = hpick * hgate
    return pick, weight, hpick, hweight


def send_part(scal, piece, pays):
    n = len(pays)

    def kernel(scal, piece, *refs):
        slots, hot_in, meta = refs[n:]
        parts = []
        for o in range(n):
            small = refs[o][T:PAY, 0:T]
            meta[o] = small
            pick, _, hpick, _ = column_parts(small, scal)
            tok = refs[o][0:T, :]
            parts.append(dot(pick.reshape(16 * CAP, T).astype(BF), tok).reshape(16, CAP, D))
            hot_in[o] = dot(hpick.astype(BF), tok).astype(BF)
        parts.append(jnp.broadcast_to(piece[...].astype(F32)[None], (16, EXTRA, D)))
        slots[...] = jnp.concatenate(parts, axis=1).astype(BF)

    return pl.pallas_call(
        kernel,
        in_specs=[pl.BlockSpec(memory_space=pltpu.SMEM)]
        + [pl.BlockSpec(memory_space=pltpu.VMEM)] * (n + 1),
        out_shape=[
            jax.ShapeDtypeStruct((16, CAP * n + EXTRA, D), BF),
            jax.ShapeDtypeStruct((n, 2 * HOT, D), BF),
            jax.ShapeDtypeStruct((n, 16, T), BF),
        ],
        cost_estimate=pl.CostEstimate(
            flops=75_000_000 * n, bytes_accessed=800_000 * n, transcendentals=0
        ),
        compiler_params=VMEM,
        name=f"send_part_{n}",
    )(scal, piece, *pays)


def cots_kernel(scal, meta, cot_a, cot_b, slots, hot_cot):
    parts = []
    for o, ref in enumerate((cot_a, cot_b)):
        pick, weight, hpick, hweight = column_parts(meta[o], scal)
        cot = ref[0]
        rows = dot(pick.reshape(16 * CAP, T).astype(BF), cot).reshape(16, CAP, D)
        parts.append(rows * jnp.sum(weight, axis=2, keepdims=True))
        hot_rows = dot(hpick.astype(BF), cot) * jnp.sum(hweight, axis=1, keepdims=True)
        hot_cot[o] = hot_rows.astype(BF)
    slots[...] = jnp.concatenate(parts, axis=1).astype(BF)


def send_cots(scal, meta, cots):
    def at(odd):
        return pl.BlockSpec((1, T, D), lambda g, s: (s[3 + 2 * g + odd], 0, 0))

    return pl.pallas_call(
        cots_kernel,
        grid_spec=pltpu.PrefetchScalarGridSpec(
            num_scalar_prefetch=1,
            grid=(4,),
            in_specs=[pl.BlockSpec((2, 16, T), lambda g, s: (g, 0, 0)), at(0), at(1)],
            out_specs=[
                pl.BlockSpec((16, 16, D), lambda g, s: (0, g, 0)),
                pl.BlockSpec((2, 2 * HOT, D), lambda g, s: (g, 0, 0)),
            ],
        ),
        out_shape=[
            jax.ShapeDtypeStruct((16, 64, D), BF),
            jax.ShapeDtypeStruct((NZ, 2 * HOT, D), BF),
        ],
        cost_estimate=pl.CostEstimate(flops=600_000_000, bytes_accessed=7_000_000, transcendentals=0),
        compiler_params=VMEM,
        name="send_cots",
    )(scal, meta, cots, cots)


def merge_kernel(scal, meta, rows, hot_rows, total):
    odd = lax.rem(pl.program_id(0), 2) == 1
    _, weight, hpick, hweight = column_parts(meta[0], scal)
    block = rows[...].astype(F32)
    mine = jnp.where(odd, block[:, CAP:, :], block[:, :CAP, :])
    mine = mine.reshape(16 * CAP, D).astype(BF)
    hot = hot_rows[0] * jnp.sum(hweight, axis=1, keepdims=True)
    weight = weight.reshape(16 * CAP, T).T
    high = weight.astype(BF)
    low = (weight - high.astype(F32)).astype(BF)
    out = dot(hpick.T.astype(BF), hot.astype(BF)) + dot(high, mine) + dot(low, mine)
    total[0] = out.astype(BF)


def merge_gated(scal, meta, rows, hot_rows):
    return pl.pallas_call(
        merge_kernel,
        grid_spec=pltpu.PrefetchScalarGridSpec(
            num_scalar_prefetch=1,
            grid=(NZ,),
            in_specs=[
                pl.BlockSpec((1, 16, T), lambda g, s: (g, 0, 0)),
                pl.BlockSpec((16, 16, D), lambda g, s: (0, g // 2, 0)),
                pl.BlockSpec((1, 2 * HOT, D), lambda g, s: (g, 0, 0)),
            ],
            out_specs=pl.BlockSpec((1, T, D), lambda g, s: (s[3 + g], 0, 0)),
        ),
        out_shape=jax.ShapeDtypeStruct((NZ, T, D), BF),
        cost_estimate=pl.CostEstimate(flops=900_000_000, bytes_accessed=7_000_000, transcendentals=0),
        compiler_params=VMEM,
        name="merge_gated",
    )(scal, meta, rows, hot_rows)


def merge_plain(scal, meta, rows, hot_rows):
    n = rows.shape[1] // CAP

    def kernel(scal, meta, rows, hot_rows, *outs):
        block = rows[...].astype(F32)
        for o in range(n):
            pick, _, hpick, _ = column_parts(meta[o], scal)
            mine = block[:, CAP * o : CAP * o + CAP, :].reshape(16 * CAP, D).astype(BF)
            out = dot(pick.reshape(16 * CAP, T).T.astype(BF), mine)
            out = out + dot(hpick.T.astype(BF), hot_rows[o].astype(BF))
            outs[o][...] = out.astype(BF)

    return pl.pallas_call(
        kernel,
        in_specs=[pl.BlockSpec(memory_space=pltpu.SMEM)]
        + [pl.BlockSpec(memory_space=pltpu.VMEM)] * 3,
        out_shape=[jax.ShapeDtypeStruct((T, D), BF)] * n,
        cost_estimate=pl.CostEstimate(
            flops=75_000_000 * n, bytes_accessed=1_000_000 * n, transcendentals=0
        ),
        compiler_params=VMEM,
        name=f"merge_plain_{n}",
    )(scal, meta, rows, hot_rows)


def silu_slope(pre):
    sig = jax.nn.sigmoid(pre)
    return sig * (1.0 + pre * (1.0 - sig))


def hot_kernel(rows_in, rows_cot, weights, out, back, grads):
    x = rows_in[...].reshape(NZ * HOT, D)
    c = rows_cot[...].reshape(NZ * HOT, D)
    gate_w = weights[0, 0:SLICE, :]
    up_w = weights[0, SLICE : 2 * SLICE, :]
    down_w = weights[0, 2 * SLICE : 3 * SLICE, :]
    pre_gate = dot_t(x, gate_w)
    pre_up = dot_t(x, up_w)
    sig = 1.0 / (1.0 + jnp.exp(-pre_gate))
    active = pre_gate * sig
    hidden = active * pre_up
    out[...] = dot(hidden.astype(BF), down_w).reshape(NZ, HOT, D)
    grad_hidden = dot_t(c, down_w)
    grad_pg = grad_hidden * pre_up * (sig * (1.0 + pre_gate * (1.0 - sig)))
    grad_pu = grad_hidden * active
    back[...] = (dot(grad_pg.astype(BF), gate_w) + dot(grad_pu.astype(BF), up_w)).reshape(NZ, HOT, D)
    grads[0, 0:SLICE, :] = dot(grad_pg.T.astype(BF), x)
    grads[0, SLICE : 2 * SLICE, :] = dot(grad_pu.T.astype(BF), x)
    grads[0, 2 * SLICE : 3 * SLICE, :] = dot(hidden.T.astype(BF), c)


def hot_pass(hot_in, hot_cot, weights):
    rows = jax.ShapeDtypeStruct((NZ, 2 * HOT, D), F32)
    return pl.pallas_call(
        hot_kernel,
        grid=(2,),
        in_specs=[
            pl.BlockSpec((NZ, HOT, D), lambda h: (0, h, 0)),
            pl.BlockSpec((NZ, HOT, D), lambda h: (0, h, 0)),
            pl.BlockSpec((1, 3 * SLICE, D), lambda h: (h, 0, 0)),
        ],
        out_specs=[
            pl.BlockSpec((NZ, HOT, D), lambda h: (0, h, 0)),
            pl.BlockSpec((NZ, HOT, D), lambda h: (0, h, 0)),
            pl.BlockSpec((1, 3 * SLICE, D), lambda h: (h, 0, 0)),
        ],
        out_shape=[rows, rows, jax.ShapeDtypeStruct((2, 3 * SLICE, D), F32)],
        cost_estimate=pl.CostEstimate(flops=600_000_000, bytes_accessed=6_000_000, transcendentals=20_000),
        compiler_params=VMEM,
        name="hot_pass",
    )(hot_in, hot_cot, weights)


def choose_kernel(is_hot, hot, gate, up, down, out_gate, out_up, out_down):
    @pl.when(is_hot[0] == 0)
    def _():
        out_gate[...] = gate[...]
        out_up[...] = up[...]
        out_down[...] = down[...]

    @pl.when(is_hot[0] == 1)
    def _():
        slices = [hot[i].astype(F32) for i in range(NZ)]

        def whole(k):
            return jnp.concatenate([v[SLICE * k : SLICE * k + SLICE] for v in slices], axis=0)

        out_gate[...] = whole(0).T
        out_up[...] = whole(1).T
        out_down[...] = whole(2)


def choose(is_hot, hot, gate, up, down):
    return pl.pallas_call(
        choose_kernel,
        in_specs=[pl.BlockSpec(memory_space=pltpu.SMEM)]
        + [pl.BlockSpec(memory_space=pltpu.VMEM)] * 4,
        out_shape=[jax.ShapeDtypeStruct(v.shape, F32) for v in (gate, up, down)],
        cost_estimate=pl.CostEstimate(flops=1_000_000, bytes_accessed=6_000_000, transcendentals=0),
        compiler_params=VMEM,
        name="choose",
    )(is_hot, hot, gate, up, down)


def up(v):
    return lax.ppermute(v, "z", [(i, (i + 1) % NZ) for i in range(NZ)])


def down(v):
    return lax.ppermute(v, "z", [((i + 1) % NZ, i) for i in range(NZ)])


def tie(v, *others):
    return lax.optimization_barrier((v, *others))[0]


def ring_gather(v, *others):
    below, above = [v], [v]
    for step in range(4):
        last = tie(below[-1], *others) if step == 3 and others else below[-1]
        below.append(up(last))
        if step < 3:
            above.append(down(above[-1]))
    return below[:0:-1] + above


def add(a, b):
    return (a.astype(F32) + b.astype(F32)).astype(BF)


def ring_sum(parts):
    rising, falling = up(parts[0]), down(parts[1])
    for step in range(3):
        rising = up(add(rising, parts[7 - step]))
        if step < 2:
            falling = down(add(falling, parts[2 + step]))
    return (parts[4].astype(F32) + rising.astype(F32) + falling.astype(F32)).astype(BF)


def swap(v):
    return lax.ppermute(v, "dp", [(0, 1), (1, 0)])


def half_sum(v, dp, dim):
    size = v.shape[dim] // 2
    mine = lax.dynamic_slice_in_dim(v, dp * size, size, dim)
    other = lax.dynamic_slice_in_dim(v, (1 - dp) * size, size, dim)
    return mine + swap(other)


def exchange(v, axes):
    return lax.all_to_all(v, axes, split_axis=0, concat_axis=0, tiled=True)


def shards(tokens, cotangent, route, numer, w_gate, w_up, w_down):
    dp = lax.axis_index("dp")
    z = lax.axis_index("z")
    me = z * 16 + lax.axis_index("x") * 4 + lax.axis_index("y")
    gate_w, up_w, down_w = w_gate[0], w_up[0], w_down[0]
    plane = ("x", "y")

    pay, info = pl.pallas_call(
        send_kernel,
        out_shape=[
            jax.ShapeDtypeStruct((PAY, D), BF),
            jax.ShapeDtypeStruct((8, T), jnp.int32),
        ],
        cost_estimate=pl.CostEstimate(flops=10_000_000, bytes_accessed=700_000, transcendentals=0),
        compiler_params=VMEM,
        name="send",
    )(tokens, route.T, numer.T)
    first, second = info[0, 0], info[1, 0]
    places_z = [lax.rem(z + g + 4, NZ) for g in ORDER]
    scal = jnp.stack([first, second, z * 16, *places_z]).astype(jnp.int32)

    wcat = jnp.concatenate(
        [w.reshape(NZ, SLICE, D) for w in (gate_w.T, up_w.T, down_w)], axis=1
    )
    wcat = wcat.reshape(NZ, 2, PIECE, 8, T).transpose(1, 3, 0, 2, 4)
    owner = jnp.where(dp == 0, first, second)
    plane_w = exchange(wcat.reshape(16, NZ * PIECE, T), plane)
    plane_w = lax.dynamic_index_in_dim(plane_w, lax.rem(owner, 16), 0, keepdims=False)
    piece = exchange(plane_w.reshape(NZ, PIECE, T), "z")
    piece = lax.dynamic_index_in_dim(piece, owner // 16, 0, keepdims=False)
    piece = jnp.pad(piece.reshape(9, D), ((0, EXTRA - 9), (0, 0)))

    cots = lax.all_gather(cotangent, "z")
    ring = ring_gather(pay, plane_w)
    sent_in, hot_in, meta = send_part(scal, piece, [ring[g] for g in ORDER])
    recv_in = exchange(sent_in, plane)

    sent_cot, hot_cot = send_cots(scal, meta, cots)
    sent_cot, recv_in = lax.optimization_barrier((sent_cot, recv_in))
    recv_cot = exchange(sent_cot, plane)

    hot_w = recv_in[:, 64:73].reshape(2, 8, PIECE, T).transpose(0, 2, 1, 3)
    hot_w = hot_w.reshape(3 * SLICE, D)
    other_w = swap(hot_w)
    hot_w = jnp.where(dp == 0, jnp.stack([hot_w, other_w]), jnp.stack([other_w, hot_w]))
    hot_out, hot_back, hot_grads = hot_pass(hot_in, hot_cot, hot_w)
    hot_g = half_sum(hot_grads.reshape(2 * 3 * SLICE, D), dp, 1).astype(BF)
    hot_g = jnp.concatenate([hot_g[: 3 * SLICE], hot_g[3 * SLICE :]], axis=1).reshape(16, 9, D)
    hot_g = jnp.pad(hot_g, ((0, 0), (0, EXTRA - 9), (0, 0)))

    rows_in = recv_in[:, :64].reshape(T * CAP, D)
    pre_gate = dot(rows_in, gate_w)
    pre_up = dot(rows_in, up_w)
    active = jax.nn.silu(pre_gate)
    hidden = (active * pre_up).astype(BF)
    result = dot(hidden, down_w).astype(BF)
    sent_out = jnp.concatenate([result.reshape(16, 64, D), hot_g], axis=1)
    sent_out, recv_cot = lax.optimization_barrier((sent_out, recv_cot))
    back_out = exchange(sent_out, plane)

    rows_cot = recv_cot.reshape(T * CAP, D)
    grad_hidden = dot_t(rows_cot, down_w)
    grad_pg = (grad_hidden * pre_up * silu_slope(pre_gate)).astype(BF)
    grad_pu = (grad_hidden * active).astype(BF)
    back = (dot_t(grad_pg, gate_w) + dot_t(grad_pu, up_w)).astype(BF)
    back, back_out = lax.optimization_barrier((back, back_out))
    back_grad = exchange(back.reshape(16, 64, D), plane)

    total = merge_gated(scal, meta, back_out, hot_out)
    output = lax.psum_scatter(
        total.reshape(NZ * T, D), "z", scatter_dimension=0, tiled=True
    )
    merged = merge_plain(scal, meta, back_grad, hot_back)
    grad_tokens = ring_sum([merged[ORDER.index(g)] for g in range(NZ)])

    hot_g = jnp.sum(back_out[:, 64:73].astype(F32), axis=0).astype(BF)
    hot_g = jnp.stack(ring_gather(tie(hot_g, back_grad)))
    hot_g = jnp.roll(hot_g, z - 4, axis=0)
    for_first = (jnp.arange(16) == lax.rem(first, 16)) & (first // 16 == z)
    hot_g = jnp.where(
        for_first[:, None, None, None], hot_g[None, :, :, : D // 2], hot_g[None, :, :, D // 2 :]
    )
    hot_g = exchange(hot_g.reshape(16, 9 * NZ, D // 2), plane)
    hot_g = hot_g.reshape(16, NZ, 9, D // 2).transpose(1, 0, 2, 3)
    hot_g = hot_g.reshape(NZ, 3 * SLICE, D // 2)
    is_hot = ((me == first) | (me == second)).astype(jnp.int32)

    def grad(a, b):
        return lax.dot_general(a, b, (((0,), (0,)), ((), ())), preferred_element_type=F32)

    cold_gate = half_sum(grad(rows_in, grad_pg), dp, 0)
    cold_up = half_sum(grad(rows_in, grad_pu), dp, 0)
    cold_down = half_sum(grad(hidden, rows_cot), dp, 1)
    grad_gate, grad_up, grad_down = choose(is_hot[None], hot_g, cold_gate, cold_up, cold_down)
    return (output, grad_tokens, grad_gate[None], grad_up[None], grad_down[None])


def solution(mesh):
    cube = Mesh(mesh.devices.reshape(2, 8, 4, 4), ("dp", "z", "x", "y"))
    owner = ("z", "x", "y")
    rows = P(("dp", "z", "x", "y"), None)
    weights = P(owner, None, None)
    return jax.shard_map(
        shards,
        mesh=cube,
        in_specs=(rows, rows, rows, rows, weights, weights, weights),
        out_specs=(
            rows,
            rows,
            P(owner, "dp", None),
            P(owner, "dp", None),
            P(owner, None, "dp"),
        ),
        check_vma=False,
    )
```

```python
import jax
import jax.numpy as jnp
from jax import lax
from jax.experimental import pallas as pl
from jax.experimental.pallas import tpu as pltpu
from jax.sharding import Mesh, PartitionSpec as P

BF = jnp.bfloat16
F32 = jnp.float32
D = 1024
FF = 384
T = 128
CAP = 8
HOT = 16
NZ = 8
SLICE = FF // NZ
PAY = T + 16
ORDER = (3, 4, 5, 2, 6, 0, 1, 7)
EXTRA = 16
PIECE = 72
RIDE = 80
VMEM = pltpu.CompilerParams(vmem_limit_bytes=48 * 1024 * 1024)


def iota(shape, dim):
    return lax.broadcasted_iota(jnp.int32, shape, dim).astype(F32)


def before():
    return (iota((T, T), 0) < iota((T, T), 1)).astype(BF)


def dot(a, b):
    return jnp.dot(a, b, preferred_element_type=F32)


def dot_t(a, b):
    return lax.dot_general(a, b, (((1,), (1,)), ((), ())), preferred_element_type=F32)


def members(route, gates, expert):
    hit = jnp.zeros(expert.shape, F32)
    gate = jnp.zeros(expert.shape, F32)
    for k in range(8):
        same = route[k : k + 1, :] == expert
        hit = hit + jnp.where(same, 1.0, 0.0)
        if gates is not None:
            gate = gate + jnp.where(same, gates[k : k + 1, :], 0.0)
    return hit, gate


def places(hit):
    return jnp.where(hit > 0.5, dot(hit.astype(BF), before()), -1.0)


def cold_pick(place):
    n = place.shape[0]
    return jnp.where(place[:, None, :] == iota((n, CAP, T), 1), 1.0, 0.0)


def hot_pick(place2):
    want = iota((HOT, T), 0)
    return jnp.concatenate(
        [jnp.where(place2[h : h + 1, :] == want, 1.0, 0.0) for h in range(2)], axis=0
    )


def send_kernel(tok, route, numer, pay, info):
    r = route[...].astype(F32)
    hit, _ = members(r, None, iota((T, T), 0))
    hot = jnp.sum(hit, axis=1, keepdims=True) > CAP + 0.5
    ids = iota((T, 1), 0)
    first = jnp.min(jnp.where(hot, ids, 1000.0), axis=0, keepdims=True)
    second = jnp.max(jnp.where(hot, ids, -1.0), axis=0, keepdims=True)
    info[...] = jnp.where(iota((8, T), 0) == 0.0, first, second).astype(jnp.int32)
    pay[0:T, :] = tok[...]
    pay[T:PAY, :] = jnp.zeros((16, D), BF)
    pay[T:PAY, 0:T] = jnp.concatenate([r, numer[...].astype(F32)], axis=0).astype(BF)


def column_parts(meta, scal):
    meta = meta.astype(F32)
    route, numer = meta[0:8], meta[8:16]
    gates = numer / jnp.sum(numer, axis=0, keepdims=True)
    first = scal[0].astype(F32)
    second = scal[1].astype(F32)
    expert = iota((16, T), 0) + scal[2].astype(F32)
    hit, gate = members(route, gates, expert)
    place = places(hit)
    place = jnp.where((expert == first) | (expert == second), -1.0, place)
    hot_expert = jnp.where(iota((8, T), 0) == 0.0, first, second)
    hot_hit, hot_gate = members(route, gates, hot_expert)
    pick = cold_pick(place)
    weight = pick * gate[:, None, :]
    hpick = hot_pick(places(hot_hit))
    hgate = jnp.concatenate(
        [jnp.broadcast_to(hot_gate[h : h + 1, :], (HOT, T)) for h in range(2)], axis=0
    )
    hweight = hpick * hgate
    return pick, weight, hpick, hweight


def send_part(scal, piece, pays):
    n = len(pays)

    def kernel(scal, piece, *refs):
        slots, hot_in, meta = refs[n:]
        parts = []
        for o in range(n):
            small = refs[o][T:PAY, 0:T]
            meta[o] = small
            pick, _, hpick, _ = column_parts(small, scal)
            tok = refs[o][0:T, :]
            parts.append(dot(pick.reshape(16 * CAP, T).astype(BF), tok).reshape(16, CAP, D))
            hot_in[o] = dot(hpick.astype(BF), tok).astype(BF)
        parts.append(jnp.broadcast_to(piece[...].astype(F32)[None], (16, EXTRA, D)))
        slots[...] = jnp.concatenate(parts, axis=1).astype(BF)

    return pl.pallas_call(
        kernel,
        in_specs=[pl.BlockSpec(memory_space=pltpu.SMEM)]
        + [pl.BlockSpec(memory_space=pltpu.VMEM)] * (n + 1),
        out_shape=[
            jax.ShapeDtypeStruct((16, CAP * n + EXTRA, D), BF),
            jax.ShapeDtypeStruct((n, 2 * HOT, D), BF),
            jax.ShapeDtypeStruct((n, 16, T), BF),
        ],
        cost_estimate=pl.CostEstimate(
            flops=75_000_000 * n, bytes_accessed=800_000 * n, transcendentals=0
        ),
        compiler_params=VMEM,
        name=f"send_part_{n}",
    )(scal, piece, *pays)


def cots_kernel(scal, meta, cot_a, cot_b, slots, hot_cot):
    parts = []
    for o, ref in enumerate((cot_a, cot_b)):
        pick, weight, hpick, hweight = column_parts(meta[o], scal)
        cot = ref[0]
        rows = dot(pick.reshape(16 * CAP, T).astype(BF), cot).reshape(16, CAP, D)
        parts.append(rows * jnp.sum(weight, axis=2, keepdims=True))
        hot_rows = dot(hpick.astype(BF), cot) * jnp.sum(hweight, axis=1, keepdims=True)
        hot_cot[o] = hot_rows.astype(BF)
    slots[...] = jnp.concatenate(parts, axis=1).astype(BF)


def send_cots(scal, meta, cots):
    def at(odd):
        return pl.BlockSpec((1, T, D), lambda g, s: (s[3 + 2 * g + odd], 0, 0))

    return pl.pallas_call(
        cots_kernel,
        grid_spec=pltpu.PrefetchScalarGridSpec(
            num_scalar_prefetch=1,
            grid=(4,),
            in_specs=[pl.BlockSpec((2, 16, T), lambda g, s: (g, 0, 0)), at(0), at(1)],
            out_specs=[
                pl.BlockSpec((16, 16, D), lambda g, s: (0, g, 0)),
                pl.BlockSpec((2, 2 * HOT, D), lambda g, s: (g, 0, 0)),
            ],
        ),
        out_shape=[
            jax.ShapeDtypeStruct((16, 64, D), BF),
            jax.ShapeDtypeStruct((NZ, 2 * HOT, D), BF),
        ],
        cost_estimate=pl.CostEstimate(flops=600_000_000, bytes_accessed=7_000_000, transcendentals=0),
        compiler_params=VMEM,
        name="send_cots",
    )(scal, meta, cots, cots)


def merge_kernel(scal, meta, rows, hot_rows, extra, total):
    block = rows[...].astype(F32)
    for o in range(NZ):
        to = scal[3 + o]
        _, weight, hpick, hweight = column_parts(meta[o], scal)
        mine = block[:, CAP * o : CAP * o + CAP, :].reshape(16 * CAP, D).astype(BF)
        hot = hot_rows[o] * jnp.sum(hweight, axis=1, keepdims=True)
        weight = weight.reshape(16 * CAP, T).T
        high = weight.astype(BF)
        low = (weight - high.astype(F32)).astype(BF)
        out = dot(hpick.T.astype(BF), hot.astype(BF)) + dot(high, mine) + dot(low, mine)
        total[to, 0:T, :] = out.astype(BF)
        total[to, T : T + RIDE, :] = extra[...]


def merge_gated(scal, meta, rows, hot_rows, extra):
    return pl.pallas_call(
        merge_kernel,
        in_specs=[pl.BlockSpec(memory_space=pltpu.SMEM)]
        + [pl.BlockSpec(memory_space=pltpu.VMEM)] * 4,
        out_shape=jax.ShapeDtypeStruct((NZ, T + RIDE, D), BF),
        cost_estimate=pl.CostEstimate(flops=900_000_000, bytes_accessed=7_000_000, transcendentals=0),
        compiler_params=VMEM,
        name="merge_gated",
    )(scal, meta, rows, hot_rows, extra)


def merge_plain(scal, meta, rows, hot_rows):
    n = rows.shape[1] // CAP

    def kernel(scal, meta, rows, hot_rows, *outs):
        block = rows[...].astype(F32)
        for o in range(n):
            pick, _, hpick, _ = column_parts(meta[o], scal)
            mine = block[:, CAP * o : CAP * o + CAP, :].reshape(16 * CAP, D).astype(BF)
            out = dot(pick.reshape(16 * CAP, T).T.astype(BF), mine)
            out = out + dot(hpick.T.astype(BF), hot_rows[o].astype(BF))
            outs[o][...] = out.astype(BF)

    return pl.pallas_call(
        kernel,
        in_specs=[pl.BlockSpec(memory_space=pltpu.SMEM)]
        + [pl.BlockSpec(memory_space=pltpu.VMEM)] * 3,
        out_shape=[jax.ShapeDtypeStruct((T, D), BF)] * n,
        cost_estimate=pl.CostEstimate(
            flops=75_000_000 * n, bytes_accessed=1_000_000 * n, transcendentals=0
        ),
        compiler_params=VMEM,
        name=f"merge_plain_{n}",
    )(scal, meta, rows, hot_rows)


def silu_slope(pre):
    sig = jax.nn.sigmoid(pre)
    return sig * (1.0 + pre * (1.0 - sig))


def hot_kernel(rows_in, rows_cot, weights, out, back, grads):
    x = rows_in[...].reshape(NZ * HOT, D)
    c = rows_cot[...].reshape(NZ * HOT, D)
    gate_w = weights[0, 0:SLICE, :]
    up_w = weights[0, SLICE : 2 * SLICE, :]
    down_w = weights[0, 2 * SLICE : 3 * SLICE, :]
    pre_gate = dot_t(x, gate_w)
    pre_up = dot_t(x, up_w)
    sig = 1.0 / (1.0 + jnp.exp(-pre_gate))
    active = pre_gate * sig
    hidden = active * pre_up
    out[...] = dot(hidden.astype(BF), down_w).reshape(NZ, HOT, D)
    grad_hidden = dot_t(c, down_w)
    grad_pg = grad_hidden * pre_up * (sig * (1.0 + pre_gate * (1.0 - sig)))
    grad_pu = grad_hidden * active
    back[...] = (dot(grad_pg.astype(BF), gate_w) + dot(grad_pu.astype(BF), up_w)).reshape(NZ, HOT, D)
    grads[0, 0:SLICE, :] = dot(grad_pg.T.astype(BF), x)
    grads[0, SLICE : 2 * SLICE, :] = dot(grad_pu.T.astype(BF), x)
    grads[0, 2 * SLICE : 3 * SLICE, :] = dot(hidden.T.astype(BF), c)


def hot_pass(hot_in, hot_cot, weights):
    rows = jax.ShapeDtypeStruct((NZ, 2 * HOT, D), F32)
    return pl.pallas_call(
        hot_kernel,
        grid=(2,),
        in_specs=[
            pl.BlockSpec((NZ, HOT, D), lambda h: (0, h, 0)),
            pl.BlockSpec((NZ, HOT, D), lambda h: (0, h, 0)),
            pl.BlockSpec((1, 3 * SLICE, D), lambda h: (h, 0, 0)),
        ],
        out_specs=[
            pl.BlockSpec((NZ, HOT, D), lambda h: (0, h, 0)),
            pl.BlockSpec((NZ, HOT, D), lambda h: (0, h, 0)),
            pl.BlockSpec((1, 3 * SLICE, D), lambda h: (h, 0, 0)),
        ],
        out_shape=[rows, rows, jax.ShapeDtypeStruct((2, 3 * SLICE, D), F32)],
        cost_estimate=pl.CostEstimate(flops=600_000_000, bytes_accessed=6_000_000, transcendentals=20_000),
        compiler_params=VMEM,
        name="hot_pass",
    )(hot_in, hot_cot, weights)


def choose_kernel(is_hot, hot, gate, up, down, out_gate, out_up, out_down):
    @pl.when(is_hot[0] == 0)
    def _():
        out_gate[...] = gate[...]
        out_up[...] = up[...]
        out_down[...] = down[...]

    @pl.when(is_hot[0] == 1)
    def _():
        slices = [hot[i].astype(F32) for i in range(NZ)]

        def whole(k):
            return jnp.concatenate([v[SLICE * k : SLICE * k + SLICE] for v in slices], axis=0)

        out_gate[...] = whole(0).T
        out_up[...] = whole(1).T
        out_down[...] = whole(2)


def choose(is_hot, hot, gate, up, down):
    return pl.pallas_call(
        choose_kernel,
        in_specs=[pl.BlockSpec(memory_space=pltpu.SMEM)]
        + [pl.BlockSpec(memory_space=pltpu.VMEM)] * 4,
        out_shape=[jax.ShapeDtypeStruct(v.shape, F32) for v in (gate, up, down)],
        cost_estimate=pl.CostEstimate(flops=1_000_000, bytes_accessed=6_000_000, transcendentals=0),
        compiler_params=VMEM,
        name="choose",
    )(is_hot, hot, gate, up, down)


def up(v):
    return lax.ppermute(v, "z", [(i, (i + 1) % NZ) for i in range(NZ)])


def down(v):
    return lax.ppermute(v, "z", [((i + 1) % NZ, i) for i in range(NZ)])


def tie(v, *others):
    return lax.optimization_barrier((v, *others))[0]


def ring_gather(v, *others):
    below, above = [v], [v]
    for step in range(4):
        last = tie(below[-1], *others) if step == 3 and others else below[-1]
        below.append(up(last))
        if step < 3:
            above.append(down(above[-1]))
    return below[:0:-1] + above


def add(a, b):
    return (a.astype(F32) + b.astype(F32)).astype(BF)


def ring_sum(parts, other):
    rising, falling = up(parts[0]), down(parts[1])
    for step in range(3):
        if step == 1:
            rising = tie(rising, other)
        rising = up(add(rising, parts[7 - step]))
        if step < 2:
            falling = down(add(falling, parts[2 + step]))
    return (parts[4].astype(F32) + rising.astype(F32) + falling.astype(F32)).astype(BF)


def swap(v):
    return lax.ppermute(v, "dp", [(0, 1), (1, 0)])


def half_sum(v, dp, dim):
    size = v.shape[dim] // 2
    mine = lax.dynamic_slice_in_dim(v, dp * size, size, dim)
    other = lax.dynamic_slice_in_dim(v, (1 - dp) * size, size, dim)
    return mine + swap(other)


def exchange(v, axes):
    return lax.all_to_all(v, axes, split_axis=0, concat_axis=0, tiled=True)


def shards(tokens, cotangent, route, numer, w_gate, w_up, w_down):
    dp = lax.axis_index("dp")
    z = lax.axis_index("z")
    me = z * 16 + lax.axis_index("x") * 4 + lax.axis_index("y")
    gate_w, up_w, down_w = w_gate[0], w_up[0], w_down[0]
    plane = ("x", "y")

    pay, info = pl.pallas_call(
        send_kernel,
        out_shape=[
            jax.ShapeDtypeStruct((PAY, D), BF),
            jax.ShapeDtypeStruct((8, T), jnp.int32),
        ],
        cost_estimate=pl.CostEstimate(flops=10_000_000, bytes_accessed=700_000, transcendentals=0),
        compiler_params=VMEM,
        name="send",
    )(tokens, route.T, numer.T)
    first, second = info[0, 0], info[1, 0]
    places_z = [lax.rem(z + g + 4, NZ) for g in ORDER]
    scal = jnp.stack([first, second, z * 16, *places_z]).astype(jnp.int32)

    wcat = jnp.concatenate(
        [w.reshape(NZ, SLICE, D) for w in (gate_w.T, up_w.T, down_w)], axis=1
    )
    wcat = wcat.reshape(NZ, 2, PIECE, 8, T).transpose(1, 3, 0, 2, 4)
    owner = jnp.where(dp == 0, first, second)
    plane_w = exchange(wcat.reshape(16, NZ * PIECE, T), plane)
    plane_w = lax.dynamic_index_in_dim(plane_w, lax.rem(owner, 16), 0, keepdims=False)
    piece = exchange(plane_w.reshape(NZ, PIECE, T), "z")
    piece = lax.dynamic_index_in_dim(piece, owner // 16, 0, keepdims=False)
    piece = jnp.pad(piece.reshape(9, D), ((0, EXTRA - 9), (0, 0)))

    cots = lax.all_gather(cotangent, "z")
    ring = ring_gather(pay, plane_w)
    sent_in, hot_in, meta = send_part(scal, piece, [ring[g] for g in ORDER])
    recv_in = exchange(sent_in, plane)

    sent_cot, hot_cot = send_cots(scal, meta, cots)
    sent_cot, recv_in = lax.optimization_barrier((sent_cot, recv_in))
    recv_cot = exchange(sent_cot, plane)

    hot_w = recv_in[:, 64:73].reshape(2, 8, PIECE, T).transpose(0, 2, 1, 3)
    hot_w = hot_w.reshape(3 * SLICE, D)
    other_w = swap(hot_w)
    hot_w = jnp.where(dp == 0, jnp.stack([hot_w, other_w]), jnp.stack([other_w, hot_w]))
    hot_out, hot_back, hot_grads = hot_pass(hot_in, hot_cot, hot_w)
    hot_g = half_sum(hot_grads.reshape(2 * 3 * SLICE, D), dp, 1).astype(BF)
    hot_g = jnp.concatenate([hot_g[: 3 * SLICE], hot_g[3 * SLICE :]], axis=1).reshape(16, 9, D)
    hot_g = jnp.pad(hot_g, ((0, 0), (0, EXTRA - 9), (0, 0)))

    rows_in = recv_in[:, :64].reshape(T * CAP, D)
    pre_gate = dot(rows_in, gate_w)
    pre_up = dot(rows_in, up_w)
    active = jax.nn.silu(pre_gate)
    hidden = (active * pre_up).astype(BF)
    result = dot(hidden, down_w).astype(BF)
    sent_out = jnp.concatenate([result.reshape(16, 64, D), hot_g], axis=1)
    sent_out, recv_cot = lax.optimization_barrier((sent_out, recv_cot))
    back_out = exchange(sent_out, plane)

    rows_cot = recv_cot.reshape(T * CAP, D)
    grad_hidden = dot_t(rows_cot, down_w)
    grad_pg = (grad_hidden * pre_up * silu_slope(pre_gate)).astype(BF)
    grad_pu = (grad_hidden * active).astype(BF)
    back = (dot_t(grad_pg, gate_w) + dot_t(grad_pu, up_w)).astype(BF)
    hot_g = jnp.sum(back_out[:, 64:73].astype(F32), axis=0).astype(BF)
    hot_g = jnp.where((jnp.arange(NZ) == z)[:, None, None], hot_g[None], jnp.zeros((), BF))
    hot_g = jnp.pad(hot_g.reshape(9 * NZ, D), ((0, RIDE - 9 * NZ), (0, 0)))
    total = merge_gated(scal, meta, back_out, hot_out, hot_g)
    back, total = lax.optimization_barrier((back, total))
    back_grad = exchange(back.reshape(16, 64, D), plane)

    summed = lax.psum_scatter(
        total.reshape(NZ * (T + RIDE), D), "z", scatter_dimension=0, tiled=True
    )
    output = summed[:T]
    merged = merge_plain(scal, meta, back_grad, hot_back)
    grad_tokens = ring_sum([merged[ORDER.index(g)] for g in range(NZ)], summed)

    hot_g = summed[T : T + 9 * NZ].reshape(NZ, 9, D)
    for_first = (jnp.arange(16) == lax.rem(first, 16)) & (first // 16 == z)
    hot_g = jnp.where(
        for_first[:, None, None, None], hot_g[None, :, :, : D // 2], hot_g[None, :, :, D // 2 :]
    )
    hot_g = exchange(hot_g.reshape(16, 9 * NZ, D // 2), plane)
    hot_g = hot_g.reshape(16, NZ, 9, D // 2).transpose(1, 0, 2, 3)
    hot_g = hot_g.reshape(NZ, 3 * SLICE, D // 2)
    is_hot = ((me == first) | (me == second)).astype(jnp.int32)

    def grad(a, b):
        return lax.dot_general(a, b, (((0,), (0,)), ((), ())), preferred_element_type=F32)

    cold_gate = half_sum(grad(rows_in, grad_pg), dp, 0)
    cold_up = half_sum(grad(rows_in, grad_pu), dp, 0)
    cold_down = half_sum(grad(hidden, rows_cot), dp, 1)
    grad_gate, grad_up, grad_down = choose(is_hot[None], hot_g, cold_gate, cold_up, cold_down)
    return (output, grad_tokens, grad_gate[None], grad_up[None], grad_down[None])


def solution(mesh):
    cube = Mesh(mesh.devices.reshape(2, 8, 4, 4), ("dp", "z", "x", "y"))
    owner = ("z", "x", "y")
    rows = P(("dp", "z", "x", "y"), None)
    weights = P(owner, None, None)
    return jax.shard_map(
        shards,
        mesh=cube,
        in_specs=(rows, rows, rows, rows, weights, weights, weights),
        out_specs=(
            rows,
            rows,
            P(owner, "dp", None),
            P(owner, "dp", None),
            P(owner, None, "dp"),
        ),
        check_vma=False,
    )
```

```python
import jax
import jax.numpy as jnp
from jax import lax
from jax.experimental import pallas as pl
from jax.experimental.pallas import tpu as pltpu
from jax.sharding import Mesh, PartitionSpec as P

BF = jnp.bfloat16
F32 = jnp.float32
D = 1024
FF = 384
T = 128
CAP = 8
HOT = 16
NZ = 8
SLICE = FF // NZ
PAY = T + 16
ORDER = (3, 4, 5, 2, 6, 0, 1, 7)
EXTRA = 16
PIECE = 72
RIDE = 80
VMEM = pltpu.CompilerParams(vmem_limit_bytes=48 * 1024 * 1024)


def iota(shape, dim):
    return lax.broadcasted_iota(jnp.int32, shape, dim).astype(F32)


def before():
    return (iota((T, T), 0) < iota((T, T), 1)).astype(BF)


def dot(a, b):
    return jnp.dot(a, b, preferred_element_type=F32)


def dot_t(a, b):
    return lax.dot_general(a, b, (((1,), (1,)), ((), ())), preferred_element_type=F32)


def members(route, gates, expert):
    hit = jnp.zeros(expert.shape, F32)
    gate = jnp.zeros(expert.shape, F32)
    for k in range(8):
        same = route[k : k + 1, :] == expert
        hit = hit + jnp.where(same, 1.0, 0.0)
        if gates is not None:
            gate = gate + jnp.where(same, gates[k : k + 1, :], 0.0)
    return hit, gate


def places(hit):
    return jnp.where(hit > 0.5, dot(hit.astype(BF), before()), -1.0)


def cold_pick(place):
    n = place.shape[0]
    return jnp.where(place[:, None, :] == iota((n, CAP, T), 1), 1.0, 0.0)


def hot_pick(place2):
    want = iota((HOT, T), 0)
    return jnp.concatenate(
        [jnp.where(place2[h : h + 1, :] == want, 1.0, 0.0) for h in range(2)], axis=0
    )


def send_kernel(tok, route, numer, pay, info):
    r = route[...].astype(F32)
    hit, _ = members(r, None, iota((T, T), 0))
    hot = jnp.sum(hit, axis=1, keepdims=True) > CAP + 0.5
    ids = iota((T, 1), 0)
    first = jnp.min(jnp.where(hot, ids, 1000.0), axis=0, keepdims=True)
    second = jnp.max(jnp.where(hot, ids, -1.0), axis=0, keepdims=True)
    info[...] = jnp.where(iota((8, T), 0) == 0.0, first, second).astype(jnp.int32)
    pay[0:T, :] = tok[...]
    pay[T:PAY, :] = jnp.zeros((16, D), BF)
    pay[T:PAY, 0:T] = jnp.concatenate([r, numer[...].astype(F32)], axis=0).astype(BF)


def column_parts(meta, scal):
    meta = meta.astype(F32)
    route, numer = meta[0:8], meta[8:16]
    gates = numer / jnp.sum(numer, axis=0, keepdims=True)
    first = scal[0].astype(F32)
    second = scal[1].astype(F32)
    expert = iota((16, T), 0) + scal[2].astype(F32)
    hit, gate = members(route, gates, expert)
    place = places(hit)
    place = jnp.where((expert == first) | (expert == second), -1.0, place)
    hot_expert = jnp.where(iota((8, T), 0) == 0.0, first, second)
    hot_hit, hot_gate = members(route, gates, hot_expert)
    pick = cold_pick(place)
    weight = pick * gate[:, None, :]
    hpick = hot_pick(places(hot_hit))
    hgate = jnp.concatenate(
        [jnp.broadcast_to(hot_gate[h : h + 1, :], (HOT, T)) for h in range(2)], axis=0
    )
    hweight = hpick * hgate
    return pick, weight, hpick, hweight


def send_part(scal, piece, pays):
    n = len(pays)

    def kernel(scal, piece, *refs):
        slots, hot_in, meta = refs[n:]
        parts = []
        for o in range(n):
            small = refs[o][T:PAY, 0:T]
            meta[o] = small
            pick, _, hpick, _ = column_parts(small, scal)
            tok = refs[o][0:T, :]
            parts.append(dot(pick.reshape(16 * CAP, T).astype(BF), tok).reshape(16, CAP, D))
            hot_in[o] = dot(hpick.astype(BF), tok).astype(BF)
        parts.append(jnp.broadcast_to(piece[...].astype(F32)[None], (16, EXTRA, D)))
        slots[...] = jnp.concatenate(parts, axis=1).astype(BF)

    return pl.pallas_call(
        kernel,
        in_specs=[pl.BlockSpec(memory_space=pltpu.SMEM)]
        + [pl.BlockSpec(memory_space=pltpu.VMEM)] * (n + 1),
        out_shape=[
            jax.ShapeDtypeStruct((16, CAP * n + EXTRA, D), BF),
            jax.ShapeDtypeStruct((n, 2 * HOT, D), BF),
            jax.ShapeDtypeStruct((n, 16, T), BF),
        ],
        cost_estimate=pl.CostEstimate(
            flops=75_000_000 * n, bytes_accessed=800_000 * n, transcendentals=0
        ),
        compiler_params=VMEM,
        name=f"send_part_{n}",
    )(scal, piece, *pays)


def cots_kernel(scal, meta, cot_a, cot_b, slots, hot_cot):
    parts = []
    for o, ref in enumerate((cot_a, cot_b)):
        pick, weight, hpick, hweight = column_parts(meta[o], scal)
        cot = ref[0]
        rows = dot(pick.reshape(16 * CAP, T).astype(BF), cot).reshape(16, CAP, D)
        parts.append(rows * jnp.sum(weight, axis=2, keepdims=True))
        hot_rows = dot(hpick.astype(BF), cot) * jnp.sum(hweight, axis=1, keepdims=True)
        hot_cot[o] = hot_rows.astype(BF)
    slots[...] = jnp.concatenate(parts, axis=1).astype(BF)


def send_cots(scal, meta, cots):
    def at(odd):
        return pl.BlockSpec((1, T, D), lambda g, s: (s[3 + 2 * g + odd], 0, 0))

    return pl.pallas_call(
        cots_kernel,
        grid_spec=pltpu.PrefetchScalarGridSpec(
            num_scalar_prefetch=1,
            grid=(4,),
            in_specs=[pl.BlockSpec((2, 16, T), lambda g, s: (g, 0, 0)), at(0), at(1)],
            out_specs=[
                pl.BlockSpec((16, 16, D), lambda g, s: (0, g, 0)),
                pl.BlockSpec((2, 2 * HOT, D), lambda g, s: (g, 0, 0)),
            ],
        ),
        out_shape=[
            jax.ShapeDtypeStruct((16, 64, D), BF),
            jax.ShapeDtypeStruct((NZ, 2 * HOT, D), BF),
        ],
        cost_estimate=pl.CostEstimate(flops=600_000_000, bytes_accessed=7_000_000, transcendentals=0),
        compiler_params=VMEM,
        name="send_cots",
    )(scal, meta, cots, cots)


def merge_kernel(scal, meta, rows, hot_rows, extra, total):
    block = rows[...].astype(F32)
    for o in range(NZ):
        to = scal[3 + o]
        _, weight, hpick, hweight = column_parts(meta[o], scal)
        mine = block[:, CAP * o : CAP * o + CAP, :].reshape(16 * CAP, D).astype(BF)
        hot = hot_rows[o] * jnp.sum(hweight, axis=1, keepdims=True)
        weight = weight.reshape(16 * CAP, T).T
        high = weight.astype(BF)
        low = (weight - high.astype(F32)).astype(BF)
        out = dot(hpick.T.astype(BF), hot.astype(BF)) + dot(high, mine) + dot(low, mine)
        total[to, 0:T, :] = out.astype(BF)
        total[to, T : T + RIDE, :] = extra[...]


def merge_gated(scal, meta, rows, hot_rows, extra):
    return pl.pallas_call(
        merge_kernel,
        in_specs=[pl.BlockSpec(memory_space=pltpu.SMEM)]
        + [pl.BlockSpec(memory_space=pltpu.VMEM)] * 4,
        out_shape=jax.ShapeDtypeStruct((NZ, T + RIDE, D), BF),
        cost_estimate=pl.CostEstimate(flops=900_000_000, bytes_accessed=7_000_000, transcendentals=0),
        compiler_params=VMEM,
        name="merge_gated",
    )(scal, meta, rows, hot_rows, extra)


def merge_plain(scal, meta, rows, hot_rows):
    n = rows.shape[1] // CAP

    def kernel(scal, meta, rows, hot_rows, *outs):
        block = rows[...].astype(F32)
        for o in range(n):
            pick, _, hpick, _ = column_parts(meta[o], scal)
            mine = block[:, CAP * o : CAP * o + CAP, :].reshape(16 * CAP, D).astype(BF)
            out = dot(pick.reshape(16 * CAP, T).T.astype(BF), mine)
            out = out + dot(hpick.T.astype(BF), hot_rows[o].astype(BF))
            outs[o][...] = out.astype(BF)

    return pl.pallas_call(
        kernel,
        in_specs=[pl.BlockSpec(memory_space=pltpu.SMEM)]
        + [pl.BlockSpec(memory_space=pltpu.VMEM)] * 3,
        out_shape=[jax.ShapeDtypeStruct((T, D), BF)] * n,
        cost_estimate=pl.CostEstimate(
            flops=75_000_000 * n, bytes_accessed=1_000_000 * n, transcendentals=0
        ),
        compiler_params=VMEM,
        name=f"merge_plain_{n}",
    )(scal, meta, rows, hot_rows)


def silu_slope(pre):
    sig = jax.nn.sigmoid(pre)
    return sig * (1.0 + pre * (1.0 - sig))


def hot_kernel(rows_in, rows_cot, weights, out, back, grads):
    x = rows_in[...].reshape(NZ * HOT, D)
    c = rows_cot[...].reshape(NZ * HOT, D)
    gate_w = weights[0, 0:SLICE, :]
    up_w = weights[0, SLICE : 2 * SLICE, :]
    down_w = weights[0, 2 * SLICE : 3 * SLICE, :]
    pre_gate = dot_t(x, gate_w)
    pre_up = dot_t(x, up_w)
    sig = 1.0 / (1.0 + jnp.exp(-pre_gate))
    active = pre_gate * sig
    hidden = active * pre_up
    out[...] = dot(hidden.astype(BF), down_w).reshape(NZ, HOT, D)
    grad_hidden = dot_t(c, down_w)
    grad_pg = grad_hidden * pre_up * (sig * (1.0 + pre_gate * (1.0 - sig)))
    grad_pu = grad_hidden * active
    back[...] = (dot(grad_pg.astype(BF), gate_w) + dot(grad_pu.astype(BF), up_w)).reshape(NZ, HOT, D)
    grads[0, 0:SLICE, :] = dot(grad_pg.T.astype(BF), x)
    grads[0, SLICE : 2 * SLICE, :] = dot(grad_pu.T.astype(BF), x)
    grads[0, 2 * SLICE : 3 * SLICE, :] = dot(hidden.T.astype(BF), c)


def hot_pass(hot_in, hot_cot, weights):
    rows = jax.ShapeDtypeStruct((NZ, 2 * HOT, D), F32)
    return pl.pallas_call(
        hot_kernel,
        grid=(2,),
        in_specs=[
            pl.BlockSpec((NZ, HOT, D), lambda h: (0, h, 0)),
            pl.BlockSpec((NZ, HOT, D), lambda h: (0, h, 0)),
            pl.BlockSpec((1, 3 * SLICE, D), lambda h: (h, 0, 0)),
        ],
        out_specs=[
            pl.BlockSpec((NZ, HOT, D), lambda h: (0, h, 0)),
            pl.BlockSpec((NZ, HOT, D), lambda h: (0, h, 0)),
            pl.BlockSpec((1, 3 * SLICE, D), lambda h: (h, 0, 0)),
        ],
        out_shape=[rows, rows, jax.ShapeDtypeStruct((2, 3 * SLICE, D), F32)],
        cost_estimate=pl.CostEstimate(flops=600_000_000, bytes_accessed=6_000_000, transcendentals=20_000),
        compiler_params=VMEM,
        name="hot_pass",
    )(hot_in, hot_cot, weights)


def choose_kernel(is_hot, hot, gate, up, down, out_gate, out_up, out_down):
    @pl.when(is_hot[0] == 0)
    def _():
        out_gate[...] = gate[...]
        out_up[...] = up[...]
        out_down[...] = down[...]

    @pl.when(is_hot[0] == 1)
    def _():
        slices = [hot[i].astype(F32) for i in range(NZ)]

        def whole(k):
            return jnp.concatenate([v[SLICE * k : SLICE * k + SLICE] for v in slices], axis=0)

        out_gate[...] = whole(0).T
        out_up[...] = whole(1).T
        out_down[...] = whole(2)


def choose(is_hot, hot, gate, up, down):
    return pl.pallas_call(
        choose_kernel,
        in_specs=[pl.BlockSpec(memory_space=pltpu.SMEM)]
        + [pl.BlockSpec(memory_space=pltpu.VMEM)] * 4,
        out_shape=[jax.ShapeDtypeStruct(v.shape, F32) for v in (gate, up, down)],
        cost_estimate=pl.CostEstimate(flops=1_000_000, bytes_accessed=6_000_000, transcendentals=0),
        compiler_params=VMEM,
        name="choose",
    )(is_hot, hot, gate, up, down)


def up(v):
    return lax.ppermute(v, "z", [(i, (i + 1) % NZ) for i in range(NZ)])


def down(v):
    return lax.ppermute(v, "z", [((i + 1) % NZ, i) for i in range(NZ)])


def tie(v, *others):
    return lax.optimization_barrier((v, *others))[0]


def ring_gather(v, *others):
    below, above = [v], [v]
    for step in range(4):
        last = tie(below[-1], *others) if step == 3 and others else below[-1]
        below.append(up(last))
        if step < 3:
            above.append(down(above[-1]))
    return below[:0:-1] + above


def add(a, b):
    return (a.astype(F32) + b.astype(F32)).astype(BF)


def ring_sum(parts, other):
    rising, falling = up(parts[0]), down(parts[1])
    for step in range(3):
        if step == 1:
            rising = tie(rising, other)
        rising = up(add(rising, parts[7 - step]))
        if step < 2:
            falling = down(add(falling, parts[2 + step]))
    return (parts[4].astype(F32) + rising.astype(F32) + falling.astype(F32)).astype(BF)


def swap(v):
    return lax.ppermute(v, "dp", [(0, 1), (1, 0)])


def half_sum(v, dp, dim):
    size = v.shape[dim] // 2
    mine = lax.dynamic_slice_in_dim(v, dp * size, size, dim)
    other = lax.dynamic_slice_in_dim(v, (1 - dp) * size, size, dim)
    return mine + swap(other)


def exchange(v, axes):
    return lax.all_to_all(v, axes, split_axis=0, concat_axis=0, tiled=True)


def shards(tokens, cotangent, route, numer, w_gate, w_up, w_down):
    dp = lax.axis_index("dp")
    z = lax.axis_index("z")
    me = z * 16 + lax.axis_index("x") * 4 + lax.axis_index("y")
    gate_w, up_w, down_w = w_gate[0], w_up[0], w_down[0]
    plane = ("x", "y")

    pay, info = pl.pallas_call(
        send_kernel,
        out_shape=[
            jax.ShapeDtypeStruct((PAY, D), BF),
            jax.ShapeDtypeStruct((8, T), jnp.int32),
        ],
        cost_estimate=pl.CostEstimate(flops=10_000_000, bytes_accessed=700_000, transcendentals=0),
        compiler_params=VMEM,
        name="send",
    )(tokens, route.T, numer.T)
    first, second = info[0, 0], info[1, 0]
    places_z = [lax.rem(z + g + 4, NZ) for g in ORDER]
    scal = jnp.stack([first, second, z * 16, *places_z]).astype(jnp.int32)

    wcat = jnp.concatenate(
        [w.reshape(NZ, SLICE, D) for w in (gate_w.T, up_w.T, down_w)], axis=1
    )
    wcat = lax.dynamic_index_in_dim(wcat.reshape(NZ, 2, PIECE, D), dp, 1, keepdims=False)
    wcat = wcat.reshape(NZ, 2, PIECE // 2, 8, T).transpose(1, 3, 0, 2, 4)
    plane_w = exchange(wcat.reshape(16, NZ * PIECE // 2, T), plane)

    def pick(v, i):
        return lax.dynamic_index_in_dim(v, i, 0, keepdims=False)

    pair = [
        pick(plane_w, lax.rem(e, 16)).reshape(NZ, PIECE // 2, T) for e in (first, second)
    ]
    pair = exchange(jnp.concatenate(pair, axis=1), "z")
    piece = jnp.concatenate(
        [pick(pair, first // 16)[: PIECE // 2], pick(pair, second // 16)[PIECE // 2 :]]
    )
    piece = jnp.pad(piece.reshape(9, D), ((0, EXTRA - 9), (0, 0)))

    cots = lax.all_gather(cotangent, "z")
    ring = ring_gather(pay, plane_w)
    sent_in, hot_in, meta = send_part(scal, piece, [ring[g] for g in ORDER])
    recv_in = exchange(sent_in, plane)

    sent_cot, hot_cot = send_cots(scal, meta, cots)
    sent_cot, recv_in = lax.optimization_barrier((sent_cot, recv_in))
    recv_cot = exchange(sent_cot, plane)

    hot_w = recv_in[:, 64:73].reshape(2, 8, 2, PIECE // 2, T).transpose(2, 0, 3, 1, 4)
    hot_w = hot_w.reshape(2, PIECE, D)
    other_w = swap(hot_w)
    hot_w = jnp.where(
        dp == 0,
        jnp.concatenate([hot_w, other_w], axis=1),
        jnp.concatenate([other_w, hot_w], axis=1),
    )
    hot_out, hot_back, hot_grads = hot_pass(hot_in, hot_cot, hot_w)
    hot_g = half_sum(hot_grads.reshape(2 * 3 * SLICE, D), dp, 1).astype(BF)
    hot_g = jnp.concatenate([hot_g[: 3 * SLICE], hot_g[3 * SLICE :]], axis=1).reshape(16, 9, D)
    hot_g = jnp.pad(hot_g, ((0, 0), (0, EXTRA - 9), (0, 0)))

    rows_in = recv_in[:, :64].reshape(T * CAP, D)
    pre_gate = dot(rows_in, gate_w)
    pre_up = dot(rows_in, up_w)
    active = jax.nn.silu(pre_gate)
    hidden = (active * pre_up).astype(BF)
    result = dot(hidden, down_w).astype(BF)
    sent_out = jnp.concatenate([result.reshape(16, 64, D), hot_g], axis=1)
    sent_out, recv_cot = lax.optimization_barrier((sent_out, recv_cot))
    back_out = exchange(sent_out, plane)

    rows_cot = recv_cot.reshape(T * CAP, D)
    grad_hidden = dot_t(rows_cot, down_w)
    grad_pg = (grad_hidden * pre_up * silu_slope(pre_gate)).astype(BF)
    grad_pu = (grad_hidden * active).astype(BF)
    back = (dot_t(grad_pg, gate_w) + dot_t(grad_pu, up_w)).astype(BF)
    hot_g = jnp.sum(back_out[:, 64:73].astype(F32), axis=0).astype(BF)
    hot_g = jnp.where((jnp.arange(NZ) == z)[:, None, None], hot_g[None], jnp.zeros((), BF))
    hot_g = jnp.pad(hot_g.reshape(9 * NZ, D), ((0, RIDE - 9 * NZ), (0, 0)))
    total = merge_gated(scal, meta, back_out, hot_out, hot_g)
    back, total = lax.optimization_barrier((back, total))
    back_grad = exchange(back.reshape(16, 64, D), plane)

    summed = lax.psum_scatter(
        total.reshape(NZ * (T + RIDE), D), "z", scatter_dimension=0, tiled=True
    )
    output = summed[:T]
    merged = merge_plain(scal, meta, back_grad, hot_back)
    grad_tokens = ring_sum([merged[ORDER.index(g)] for g in range(NZ)], summed)

    hot_g = summed[T : T + 9 * NZ].reshape(NZ, 9, D)
    for_first = (jnp.arange(16) == lax.rem(first, 16)) & (first // 16 == z)
    hot_g = jnp.where(
        for_first[:, None, None, None], hot_g[None, :, :, : D // 2], hot_g[None, :, :, D // 2 :]
    )
    hot_g = exchange(hot_g.reshape(16, 9 * NZ, D // 2), plane)
    hot_g = hot_g.reshape(16, NZ, 9, D // 2).transpose(1, 0, 2, 3)
    hot_g = hot_g.reshape(NZ, 3 * SLICE, D // 2)
    is_hot = ((me == first) | (me == second)).astype(jnp.int32)

    def grad(a, b):
        return lax.dot_general(a, b, (((0,), (0,)), ((), ())), preferred_element_type=F32)

    cold_gate = half_sum(grad(rows_in, grad_pg), dp, 0)
    cold_up = half_sum(grad(rows_in, grad_pu), dp, 0)
    cold_down = half_sum(grad(hidden, rows_cot), dp, 1)
    grad_gate, grad_up, grad_down = choose(is_hot[None], hot_g, cold_gate, cold_up, cold_down)
    return (output, grad_tokens, grad_gate[None], grad_up[None], grad_down[None])


def solution(mesh):
    cube = Mesh(mesh.devices.reshape(2, 8, 4, 4), ("dp", "z", "x", "y"))
    owner = ("z", "x", "y")
    rows = P(("dp", "z", "x", "y"), None)
    weights = P(owner, None, None)
    return jax.shard_map(
        shards,
        mesh=cube,
        in_specs=(rows, rows, rows, rows, weights, weights, weights),
        out_specs=(
            rows,
            rows,
            P(owner, "dp", None),
            P(owner, "dp", None),
            P(owner, None, "dp"),
        ),
        check_vma=False,
    )
```

```python
import jax
import jax.numpy as jnp
from jax import lax
from jax.experimental import pallas as pl
from jax.experimental.pallas import tpu as pltpu
from jax.sharding import Mesh, PartitionSpec as P

BF = jnp.bfloat16
F32 = jnp.float32
D = 1024
FF = 384
T = 128
CAP = 8
HOT = 16
NZ = 8
SLICE = FF // NZ
PAY = T + 16
ORDER = (3, 4, 5, 2, 6, 0, 1, 7)
EXTRA = 16
PIECE = 72
RIDE = 80
VMEM = pltpu.CompilerParams(vmem_limit_bytes=48 * 1024 * 1024)


def iota(shape, dim):
    return lax.broadcasted_iota(jnp.int32, shape, dim).astype(F32)


def before():
    return (iota((T, T), 0) < iota((T, T), 1)).astype(BF)


def dot(a, b):
    return jnp.dot(a, b, preferred_element_type=F32)


def dot_t(a, b):
    return lax.dot_general(a, b, (((1,), (1,)), ((), ())), preferred_element_type=F32)


def members(route, gates, expert):
    hit = jnp.zeros(expert.shape, F32)
    gate = jnp.zeros(expert.shape, F32)
    for k in range(8):
        same = route[k : k + 1, :] == expert
        hit = hit + jnp.where(same, 1.0, 0.0)
        if gates is not None:
            gate = gate + jnp.where(same, gates[k : k + 1, :], 0.0)
    return hit, gate


def places(hit):
    return jnp.where(hit > 0.5, dot(hit.astype(BF), before()), -1.0)


def cold_pick(place):
    n = place.shape[0]
    return jnp.where(place[:, None, :] == iota((n, CAP, T), 1), 1.0, 0.0)


def hot_pick(place2):
    want = iota((HOT, T), 0)
    return jnp.concatenate(
        [jnp.where(place2[h : h + 1, :] == want, 1.0, 0.0) for h in range(2)], axis=0
    )


def send_kernel(tok, route, numer, pay, info):
    r = route[...].astype(F32)
    hit, _ = members(r, None, iota((T, T), 0))
    hot = jnp.sum(hit, axis=1, keepdims=True) > CAP + 0.5
    ids = iota((T, 1), 0)
    first = jnp.min(jnp.where(hot, ids, 1000.0), axis=0, keepdims=True)
    second = jnp.max(jnp.where(hot, ids, -1.0), axis=0, keepdims=True)
    info[...] = jnp.where(iota((8, T), 0) == 0.0, first, second).astype(jnp.int32)
    pay[0:T, :] = tok[...]
    pay[T:PAY, :] = jnp.zeros((16, D), BF)
    pay[T:PAY, 0:T] = jnp.concatenate([r, numer[...].astype(F32)], axis=0).astype(BF)


def column_parts(meta, scal):
    meta = meta.astype(F32)
    route, numer = meta[0:8], meta[8:16]
    gates = numer / jnp.sum(numer, axis=0, keepdims=True)
    first = scal[0].astype(F32)
    second = scal[1].astype(F32)
    expert = iota((16, T), 0) + scal[2].astype(F32)
    hit, gate = members(route, gates, expert)
    place = places(hit)
    place = jnp.where((expert == first) | (expert == second), -1.0, place)
    hot_expert = jnp.where(iota((8, T), 0) == 0.0, first, second)
    hot_hit, hot_gate = members(route, gates, hot_expert)
    pick = cold_pick(place)
    weight = pick * gate[:, None, :]
    hpick = hot_pick(places(hot_hit))
    hgate = jnp.concatenate(
        [jnp.broadcast_to(hot_gate[h : h + 1, :], (HOT, T)) for h in range(2)], axis=0
    )
    hweight = hpick * hgate
    return pick, weight, hpick, hweight


def send_part(scal, piece, pays):
    n = len(pays)

    def kernel(scal, piece, *refs):
        slots, hot_in, meta = refs[n:]
        parts = []
        for o in range(n):
            small = refs[o][T:PAY, 0:T]
            meta[o] = small
            pick, _, hpick, _ = column_parts(small, scal)
            tok = refs[o][0:T, :]
            parts.append(dot(pick.reshape(16 * CAP, T).astype(BF), tok).reshape(16, CAP, D))
            hot_in[o] = dot(hpick.astype(BF), tok).astype(BF)
        parts.append(jnp.broadcast_to(piece[...].astype(F32)[None], (16, EXTRA, D)))
        slots[...] = jnp.concatenate(parts, axis=1).astype(BF)

    return pl.pallas_call(
        kernel,
        in_specs=[pl.BlockSpec(memory_space=pltpu.SMEM)]
        + [pl.BlockSpec(memory_space=pltpu.VMEM)] * (n + 1),
        out_shape=[
            jax.ShapeDtypeStruct((16, CAP * n + EXTRA, D), BF),
            jax.ShapeDtypeStruct((n, 2 * HOT, D), BF),
            jax.ShapeDtypeStruct((n, 16, T), BF),
        ],
        cost_estimate=pl.CostEstimate(
            flops=75_000_000 * n, bytes_accessed=800_000 * n, transcendentals=0
        ),
        compiler_params=VMEM,
        name=f"send_part_{n}",
    )(scal, piece, *pays)


def cots_kernel(scal, meta, cot_a, cot_b, slots, hot_cot):
    parts = []
    for o, ref in enumerate((cot_a, cot_b)):
        pick, weight, hpick, hweight = column_parts(meta[o], scal)
        cot = ref[0]
        rows = dot(pick.reshape(16 * CAP, T).astype(BF), cot).reshape(16, CAP, D)
        parts.append(rows * jnp.sum(weight, axis=2, keepdims=True))
        hot_rows = dot(hpick.astype(BF), cot) * jnp.sum(hweight, axis=1, keepdims=True)
        hot_cot[o] = hot_rows.astype(BF)
    slots[...] = jnp.concatenate(parts, axis=1).astype(BF)


def send_cots(scal, meta, cots):
    def at(odd):
        return pl.BlockSpec((1, T, D), lambda g, s: (s[3 + 2 * g + odd], 0, 0))

    return pl.pallas_call(
        cots_kernel,
        grid_spec=pltpu.PrefetchScalarGridSpec(
            num_scalar_prefetch=1,
            grid=(4,),
            in_specs=[pl.BlockSpec((2, 16, T), lambda g, s: (g, 0, 0)), at(0), at(1)],
            out_specs=[
                pl.BlockSpec((16, 16, D), lambda g, s: (0, g, 0)),
                pl.BlockSpec((2, 2 * HOT, D), lambda g, s: (g, 0, 0)),
            ],
        ),
        out_shape=[
            jax.ShapeDtypeStruct((16, 64, D), BF),
            jax.ShapeDtypeStruct((NZ, 2 * HOT, D), BF),
        ],
        cost_estimate=pl.CostEstimate(flops=600_000_000, bytes_accessed=7_000_000, transcendentals=0),
        compiler_params=VMEM,
        name="send_cots",
    )(scal, meta, cots, cots)


def merge_kernel(scal, meta, rows, hot_rows, extra, total):
    block = rows[...].astype(F32)
    for o in range(NZ):
        to = scal[3 + o]
        _, weight, hpick, hweight = column_parts(meta[o], scal)
        mine = block[:, CAP * o : CAP * o + CAP, :].reshape(16 * CAP, D).astype(BF)
        hot = hot_rows[o] * jnp.sum(hweight, axis=1, keepdims=True)
        weight = weight.reshape(16 * CAP, T).T
        high = weight.astype(BF)
        low = (weight - high.astype(F32)).astype(BF)
        out = dot(hpick.T.astype(BF), hot.astype(BF)) + dot(high, mine) + dot(low, mine)
        total[to, 0:T, :] = out.astype(BF)
        total[to, T : T + RIDE, :] = extra[...]


def merge_gated(scal, meta, rows, hot_rows, extra):
    return pl.pallas_call(
        merge_kernel,
        in_specs=[pl.BlockSpec(memory_space=pltpu.SMEM)]
        + [pl.BlockSpec(memory_space=pltpu.VMEM)] * 4,
        out_shape=jax.ShapeDtypeStruct((NZ, T + RIDE, D), BF),
        cost_estimate=pl.CostEstimate(flops=900_000_000, bytes_accessed=7_000_000, transcendentals=0),
        compiler_params=VMEM,
        name="merge_gated",
    )(scal, meta, rows, hot_rows, extra)


def merge_plain(scal, meta, rows, hot_rows):
    n = rows.shape[1] // CAP

    def kernel(scal, meta, rows, hot_rows, *outs):
        block = rows[...].astype(F32)
        for o in range(n):
            pick, _, hpick, _ = column_parts(meta[o], scal)
            mine = block[:, CAP * o : CAP * o + CAP, :].reshape(16 * CAP, D).astype(BF)
            out = dot(pick.reshape(16 * CAP, T).T.astype(BF), mine)
            out = out + dot(hpick.T.astype(BF), hot_rows[o].astype(BF))
            outs[o][...] = out.astype(BF)

    return pl.pallas_call(
        kernel,
        in_specs=[pl.BlockSpec(memory_space=pltpu.SMEM)]
        + [pl.BlockSpec(memory_space=pltpu.VMEM)] * 3,
        out_shape=[jax.ShapeDtypeStruct((T, D), BF)] * n,
        cost_estimate=pl.CostEstimate(
            flops=75_000_000 * n, bytes_accessed=1_000_000 * n, transcendentals=0
        ),
        compiler_params=VMEM,
        name=f"merge_plain_{n}",
    )(scal, meta, rows, hot_rows)


def silu_slope(pre):
    sig = jax.nn.sigmoid(pre)
    return sig * (1.0 + pre * (1.0 - sig))


def hot_kernel(rows_in, rows_cot, weights, out, back, grads):
    x = rows_in[...].reshape(NZ * HOT, D)
    c = rows_cot[...].reshape(NZ * HOT, D)
    gate_w = weights[0, 0:SLICE, :]
    up_w = weights[0, SLICE : 2 * SLICE, :]
    down_w = weights[0, 2 * SLICE : 3 * SLICE, :]
    pre_gate = dot_t(x, gate_w)
    pre_up = dot_t(x, up_w)
    sig = 1.0 / (1.0 + jnp.exp(-pre_gate))
    active = pre_gate * sig
    hidden = active * pre_up
    out[...] = dot(hidden.astype(BF), down_w).reshape(NZ, HOT, D)
    grad_hidden = dot_t(c, down_w)
    grad_pg = grad_hidden * pre_up * (sig * (1.0 + pre_gate * (1.0 - sig)))
    grad_pu = grad_hidden * active
    back[...] = (dot(grad_pg.astype(BF), gate_w) + dot(grad_pu.astype(BF), up_w)).reshape(NZ, HOT, D)
    grads[0, 0:SLICE, :] = dot(grad_pg.T.astype(BF), x)
    grads[0, SLICE : 2 * SLICE, :] = dot(grad_pu.T.astype(BF), x)
    grads[0, 2 * SLICE : 3 * SLICE, :] = dot(hidden.T.astype(BF), c)


def hot_pass(hot_in, hot_cot, weights):
    rows = jax.ShapeDtypeStruct((NZ, 2 * HOT, D), F32)
    return pl.pallas_call(
        hot_kernel,
        grid=(2,),
        in_specs=[
            pl.BlockSpec((NZ, HOT, D), lambda h: (0, h, 0)),
            pl.BlockSpec((NZ, HOT, D), lambda h: (0, h, 0)),
            pl.BlockSpec((1, 3 * SLICE, D), lambda h: (h, 0, 0)),
        ],
        out_specs=[
            pl.BlockSpec((NZ, HOT, D), lambda h: (0, h, 0)),
            pl.BlockSpec((NZ, HOT, D), lambda h: (0, h, 0)),
            pl.BlockSpec((1, 3 * SLICE, D), lambda h: (h, 0, 0)),
        ],
        out_shape=[rows, rows, jax.ShapeDtypeStruct((2, 3 * SLICE, D), F32)],
        cost_estimate=pl.CostEstimate(flops=1_000_000, bytes_accessed=10_000, transcendentals=0),
        compiler_params=VMEM,
        name="hot_pass",
    )(hot_in, hot_cot, weights)


def choose_kernel(is_hot, hot, gate, up, down, out_gate, out_up, out_down):
    @pl.when(is_hot[0] == 0)
    def _():
        out_gate[...] = gate[...]
        out_up[...] = up[...]
        out_down[...] = down[...]

    @pl.when(is_hot[0] == 1)
    def _():
        slices = [hot[i].astype(F32) for i in range(NZ)]

        def whole(k):
            return jnp.concatenate([v[SLICE * k : SLICE * k + SLICE] for v in slices], axis=0)

        out_gate[...] = whole(0).T
        out_up[...] = whole(1).T
        out_down[...] = whole(2)


def choose(is_hot, hot, gate, up, down):
    return pl.pallas_call(
        choose_kernel,
        in_specs=[pl.BlockSpec(memory_space=pltpu.SMEM)]
        + [pl.BlockSpec(memory_space=pltpu.VMEM)] * 4,
        out_shape=[jax.ShapeDtypeStruct(v.shape, F32) for v in (gate, up, down)],
        cost_estimate=pl.CostEstimate(flops=1_000_000, bytes_accessed=6_000_000, transcendentals=0),
        compiler_params=VMEM,
        name="choose",
    )(is_hot, hot, gate, up, down)


def up(v):
    return lax.ppermute(v, "z", [(i, (i + 1) % NZ) for i in range(NZ)])


def down(v):
    return lax.ppermute(v, "z", [((i + 1) % NZ, i) for i in range(NZ)])


def tie(v, *others):
    return lax.optimization_barrier((v, *others))[0]


def ring_gather(v, *others):
    below, above = [v], [v]
    for step in range(4):
        last = tie(below[-1], *others) if step == 3 and others else below[-1]
        below.append(up(last))
        if step < 3:
            above.append(down(above[-1]))
    return below[:0:-1] + above


def add(a, b):
    return (a.astype(F32) + b.astype(F32)).astype(BF)


def ring_sum(parts, other):
    rising, falling = up(parts[0]), down(parts[1])
    for step in range(3):
        if step == 1:
            rising = tie(rising, other)
        rising = up(add(rising, parts[7 - step]))
        if step < 2:
            falling = down(add(falling, parts[2 + step]))
    return (parts[4].astype(F32) + rising.astype(F32) + falling.astype(F32)).astype(BF)


def swap(v):
    return lax.ppermute(v, "dp", [(0, 1), (1, 0)])


def half_sum(v, dp, dim):
    size = v.shape[dim] // 2
    mine = lax.dynamic_slice_in_dim(v, dp * size, size, dim)
    other = lax.dynamic_slice_in_dim(v, (1 - dp) * size, size, dim)
    return mine + swap(other)


def exchange(v, axes):
    return lax.all_to_all(v, axes, split_axis=0, concat_axis=0, tiled=True)


def shards(tokens, cotangent, route, numer, w_gate, w_up, w_down):
    dp = lax.axis_index("dp")
    z = lax.axis_index("z")
    me = z * 16 + lax.axis_index("x") * 4 + lax.axis_index("y")
    gate_w, up_w, down_w = w_gate[0], w_up[0], w_down[0]
    plane = ("x", "y")

    pay, info = pl.pallas_call(
        send_kernel,
        out_shape=[
            jax.ShapeDtypeStruct((PAY, D), BF),
            jax.ShapeDtypeStruct((8, T), jnp.int32),
        ],
        cost_estimate=pl.CostEstimate(flops=10_000_000, bytes_accessed=700_000, transcendentals=0),
        compiler_params=VMEM,
        name="send",
    )(tokens, route.T, numer.T)
    first, second = info[0, 0], info[1, 0]
    places_z = [lax.rem(z + g + 4, NZ) for g in ORDER]
    scal = jnp.stack([first, second, z * 16, *places_z]).astype(jnp.int32)

    wcat = jnp.concatenate(
        [w.reshape(NZ, SLICE, D) for w in (gate_w.T, up_w.T, down_w)], axis=1
    )
    wcat = lax.dynamic_index_in_dim(wcat.reshape(NZ, 2, PIECE, D), dp, 1, keepdims=False)
    wcat = wcat.reshape(NZ, 2, PIECE // 2, 8, T).transpose(1, 3, 0, 2, 4)
    plane_w = exchange(wcat.reshape(16, NZ * PIECE // 2, T), plane)

    def pick(v, i):
        return lax.dynamic_index_in_dim(v, i, 0, keepdims=False)

    pair = [
        pick(plane_w, lax.rem(e, 16)).reshape(NZ, PIECE // 2, T) for e in (first, second)
    ]
    pair = exchange(jnp.concatenate(pair, axis=1), "z")
    piece = jnp.concatenate(
        [pick(pair, first // 16)[: PIECE // 2], pick(pair, second // 16)[PIECE // 2 :]]
    )
    piece = jnp.pad(piece.reshape(9, D), ((0, EXTRA - 9), (0, 0)))

    ring = ring_gather(pay, plane_w)
    cots = lax.all_gather(tie(cotangent, ring[2]), "z")
    sent_in, hot_in, meta = send_part(scal, piece, [ring[g] for g in ORDER])
    recv_in = exchange(sent_in, plane)

    sent_cot, hot_cot = send_cots(scal, meta, cots)
    sent_cot, recv_in = lax.optimization_barrier((sent_cot, recv_in))
    recv_cot = exchange(sent_cot, plane)

    hot_w = recv_in[:, 64:73].reshape(2, 8, 2, PIECE // 2, T).transpose(2, 0, 3, 1, 4)
    hot_w = hot_w.reshape(2, PIECE, D)
    other_w = swap(hot_w)
    hot_w = jnp.where(
        dp == 0,
        jnp.concatenate([hot_w, other_w], axis=1),
        jnp.concatenate([other_w, hot_w], axis=1),
    )
    hot_out, hot_back, hot_grads = hot_pass(hot_in, hot_cot, hot_w)
    hot_g = half_sum(hot_grads.reshape(2 * 3 * SLICE, D), dp, 1).astype(BF)
    hot_g = jnp.concatenate([hot_g[: 3 * SLICE], hot_g[3 * SLICE :]], axis=1).reshape(16, 9, D)
    hot_g = jnp.pad(hot_g, ((0, 0), (0, EXTRA - 9), (0, 0)))

    rows_in = recv_in[:, :64].reshape(T * CAP, D)
    pre_gate = dot(rows_in, gate_w)
    pre_up = dot(rows_in, up_w)
    active = jax.nn.silu(pre_gate)
    hidden = (active * pre_up).astype(BF)
    result = dot(hidden, down_w).astype(BF)
    sent_out = jnp.concatenate([result.reshape(16, 64, D), hot_g], axis=1)
    sent_out, recv_cot = lax.optimization_barrier((sent_out, recv_cot))
    back_out = exchange(sent_out, plane)

    rows_cot = recv_cot.reshape(T * CAP, D)
    grad_hidden = dot_t(rows_cot, down_w)
    grad_pg = (grad_hidden * pre_up * silu_slope(pre_gate)).astype(BF)
    grad_pu = (grad_hidden * active).astype(BF)
    back = (dot_t(grad_pg, gate_w) + dot_t(grad_pu, up_w)).astype(BF)
    hot_g = jnp.sum(back_out[:, 64:73].astype(F32), axis=0).astype(BF)
    hot_g = jnp.where((jnp.arange(NZ) == z)[:, None, None], hot_g[None], jnp.zeros((), BF))
    hot_g = jnp.pad(hot_g.reshape(9 * NZ, D), ((0, RIDE - 9 * NZ), (0, 0)))
    total = merge_gated(scal, meta, back_out, hot_out, hot_g)
    back, total = lax.optimization_barrier((back, total))
    back_grad = exchange(back.reshape(16, 64, D), plane)

    summed = lax.psum_scatter(
        total.reshape(NZ * (T + RIDE), D), "z", scatter_dimension=0, tiled=True
    )
    output = summed[:T]
    merged = merge_plain(scal, meta, back_grad, hot_back)
    grad_tokens = ring_sum([merged[ORDER.index(g)] for g in range(NZ)], summed)

    hot_g = summed[T : T + 9 * NZ].reshape(NZ, 9, D)
    for_first = (jnp.arange(16) == lax.rem(first, 16)) & (first // 16 == z)
    hot_g = jnp.where(
        for_first[:, None, None, None], hot_g[None, :, :, : D // 2], hot_g[None, :, :, D // 2 :]
    )
    hot_g = exchange(hot_g.reshape(16, 9 * NZ, D // 2), plane)
    hot_g = hot_g.reshape(16, NZ, 9, D // 2).transpose(1, 0, 2, 3)
    hot_g = hot_g.reshape(NZ, 3 * SLICE, D // 2)
    is_hot = ((me == first) | (me == second)).astype(jnp.int32)

    def grad(a, b):
        return lax.dot_general(a, b, (((0,), (0,)), ((), ())), preferred_element_type=F32)

    cold_gate = half_sum(grad(rows_in, grad_pg), dp, 0)
    cold_up = half_sum(grad(rows_in, grad_pu), dp, 0)
    cold_down = half_sum(grad(hidden, rows_cot), dp, 1)
    grad_gate, grad_up, grad_down = choose(is_hot[None], hot_g, cold_gate, cold_up, cold_down)
    return (output, grad_tokens, grad_gate[None], grad_up[None], grad_down[None])


def solution(mesh):
    cube = Mesh(mesh.devices.reshape(2, 8, 4, 4), ("dp", "z", "x", "y"))
    owner = ("z", "x", "y")
    rows = P(("dp", "z", "x", "y"), None)
    weights = P(owner, None, None)
    return jax.shard_map(
        shards,
        mesh=cube,
        in_specs=(rows, rows, rows, rows, weights, weights, weights),
        out_specs=(
            rows,
            rows,
            P(owner, "dp", None),
            P(owner, "dp", None),
            P(owner, None, "dp"),
        ),
        check_vma=False,
    )
```

```python
import jax
import jax.numpy as jnp
from jax import lax
from jax.experimental import pallas as pl
from jax.experimental.pallas import tpu as pltpu
from jax.sharding import Mesh, PartitionSpec as P

BF = jnp.bfloat16
F32 = jnp.float32
D = 1024
FF = 384
T = 128
CAP = 8
HOT = 16
NZ = 8
SLICE = FF // NZ
PAY = T + 16
ORDER = (3, 4, 5, 2, 6, 0, 1, 7)
EXTRA = 16
PIECE = 72
RIDE = 80
VMEM = pltpu.CompilerParams(vmem_limit_bytes=48 * 1024 * 1024)


def iota(shape, dim):
    return lax.broadcasted_iota(jnp.int32, shape, dim).astype(F32)


def before():
    return (iota((T, T), 0) < iota((T, T), 1)).astype(BF)


def dot(a, b):
    return jnp.dot(a, b, preferred_element_type=F32)


def dot_t(a, b):
    return lax.dot_general(a, b, (((1,), (1,)), ((), ())), preferred_element_type=F32)


def members(route, gates, expert):
    hit = jnp.zeros(expert.shape, F32)
    gate = jnp.zeros(expert.shape, F32)
    for k in range(8):
        same = route[k : k + 1, :] == expert
        hit = hit + jnp.where(same, 1.0, 0.0)
        if gates is not None:
            gate = gate + jnp.where(same, gates[k : k + 1, :], 0.0)
    return hit, gate


def places(hit):
    return jnp.where(hit > 0.5, dot(hit.astype(BF), before()), -1.0)


def cold_pick(place):
    n = place.shape[0]
    return jnp.where(place[:, None, :] == iota((n, CAP, T), 1), 1.0, 0.0)


def hot_pick(place2):
    want = iota((HOT, T), 0)
    return jnp.concatenate(
        [jnp.where(place2[h : h + 1, :] == want, 1.0, 0.0) for h in range(2)], axis=0
    )


def send_kernel(tok, route, numer, pay, info):
    r = route[...].astype(F32)
    hit, _ = members(r, None, iota((T, T), 0))
    hot = jnp.sum(hit, axis=1, keepdims=True) > CAP + 0.5
    ids = iota((T, 1), 0)
    first = jnp.min(jnp.where(hot, ids, 1000.0), axis=0, keepdims=True)
    second = jnp.max(jnp.where(hot, ids, -1.0), axis=0, keepdims=True)
    info[...] = jnp.where(iota((8, T), 0) == 0.0, first, second).astype(jnp.int32)
    pay[0:T, :] = tok[...]
    pay[T:PAY, :] = jnp.zeros((16, D), BF)
    pay[T:PAY, 0:T] = jnp.concatenate([r, numer[...].astype(F32)], axis=0).astype(BF)


def column_parts(meta, scal):
    meta = meta.astype(F32)
    route, numer = meta[0:8], meta[8:16]
    gates = numer / jnp.sum(numer, axis=0, keepdims=True)
    first = scal[0].astype(F32)
    second = scal[1].astype(F32)
    expert = iota((16, T), 0) + scal[2].astype(F32)
    hit, gate = members(route, gates, expert)
    place = places(hit)
    place = jnp.where((expert == first) | (expert == second), -1.0, place)
    hot_expert = jnp.where(iota((8, T), 0) == 0.0, first, second)
    hot_hit, hot_gate = members(route, gates, hot_expert)
    pick = cold_pick(place)
    weight = pick * gate[:, None, :]
    hpick = hot_pick(places(hot_hit))
    hgate = jnp.concatenate(
        [jnp.broadcast_to(hot_gate[h : h + 1, :], (HOT, T)) for h in range(2)], axis=0
    )
    hweight = hpick * hgate
    return pick, weight, hpick, hweight


def send_part(scal, piece, pays):
    n = len(pays)

    def kernel(scal, piece, *refs):
        slots, hot_in, meta = refs[n:]
        parts = []
        for o in range(n):
            small = refs[o][T:PAY, 0:T]
            meta[o] = small
            pick, _, hpick, _ = column_parts(small, scal)
            tok = refs[o][0:T, :]
            parts.append(dot(pick.reshape(16 * CAP, T).astype(BF), tok).reshape(16, CAP, D))
            hot_in[o] = dot(hpick.astype(BF), tok).astype(BF)
        parts.append(jnp.broadcast_to(piece[...].astype(F32)[None], (16, EXTRA, D)))
        slots[...] = jnp.concatenate(parts, axis=1).astype(BF)

    return pl.pallas_call(
        kernel,
        in_specs=[pl.BlockSpec(memory_space=pltpu.SMEM)]
        + [pl.BlockSpec(memory_space=pltpu.VMEM)] * (n + 1),
        out_shape=[
            jax.ShapeDtypeStruct((16, CAP * n + EXTRA, D), BF),
            jax.ShapeDtypeStruct((n, 2 * HOT, D), BF),
            jax.ShapeDtypeStruct((n, 16, T), BF),
        ],
        cost_estimate=pl.CostEstimate(
            flops=75_000_000 * n, bytes_accessed=800_000 * n, transcendentals=0
        ),
        compiler_params=VMEM,
        name=f"send_part_{n}",
    )(scal, piece, *pays)


def cots_kernel(scal, meta, cot_a, cot_b, slots, hot_cot):
    parts = []
    for o, ref in enumerate((cot_a, cot_b)):
        pick, weight, hpick, hweight = column_parts(meta[o], scal)
        cot = ref[0]
        rows = dot(pick.reshape(16 * CAP, T).astype(BF), cot).reshape(16, CAP, D)
        parts.append(rows * jnp.sum(weight, axis=2, keepdims=True))
        hot_rows = dot(hpick.astype(BF), cot) * jnp.sum(hweight, axis=1, keepdims=True)
        hot_cot[o] = hot_rows.astype(BF)
    slots[...] = jnp.concatenate(parts, axis=1).astype(BF)


def send_cots(scal, meta, cots):
    def at(odd):
        return pl.BlockSpec((1, T, D), lambda g, s: (s[3 + 2 * g + odd], 0, 0))

    return pl.pallas_call(
        cots_kernel,
        grid_spec=pltpu.PrefetchScalarGridSpec(
            num_scalar_prefetch=1,
            grid=(4,),
            in_specs=[pl.BlockSpec((2, 16, T), lambda g, s: (g, 0, 0)), at(0), at(1)],
            out_specs=[
                pl.BlockSpec((16, 16, D), lambda g, s: (0, g, 0)),
                pl.BlockSpec((2, 2 * HOT, D), lambda g, s: (g, 0, 0)),
            ],
        ),
        out_shape=[
            jax.ShapeDtypeStruct((16, 64, D), BF),
            jax.ShapeDtypeStruct((NZ, 2 * HOT, D), BF),
        ],
        cost_estimate=pl.CostEstimate(flops=600_000_000, bytes_accessed=7_000_000, transcendentals=0),
        compiler_params=VMEM,
        name="send_cots",
    )(scal, meta, cots, cots)


def merge_kernel(scal, meta, rows, hot_rows, extra, total):
    block = rows[...].astype(F32)
    for o in range(NZ):
        to = scal[3 + o]
        _, weight, hpick, hweight = column_parts(meta[o], scal)
        mine = block[:, CAP * o : CAP * o + CAP, :].reshape(16 * CAP, D).astype(BF)
        hot = hot_rows[o] * jnp.sum(hweight, axis=1, keepdims=True)
        weight = weight.reshape(16 * CAP, T).T
        high = weight.astype(BF)
        low = (weight - high.astype(F32)).astype(BF)
        out = dot(hpick.T.astype(BF), hot.astype(BF)) + dot(high, mine) + dot(low, mine)
        total[to, 0:T, :] = out.astype(BF)
        total[to, T : T + RIDE, :] = extra[...]


def merge_gated(scal, meta, rows, hot_rows, extra):
    return pl.pallas_call(
        merge_kernel,
        in_specs=[pl.BlockSpec(memory_space=pltpu.SMEM)]
        + [pl.BlockSpec(memory_space=pltpu.VMEM)] * 4,
        out_shape=jax.ShapeDtypeStruct((NZ, T + RIDE, D), BF),
        cost_estimate=pl.CostEstimate(flops=900_000_000, bytes_accessed=7_000_000, transcendentals=0),
        compiler_params=VMEM,
        name="merge_gated",
    )(scal, meta, rows, hot_rows, extra)


def merge_plain(scal, meta, rows, hot_rows):
    n = rows.shape[1] // CAP

    def kernel(scal, meta, rows, hot_rows, *outs):
        block = rows[...].astype(F32)
        for o in range(n):
            pick, _, hpick, _ = column_parts(meta[o], scal)
            mine = block[:, CAP * o : CAP * o + CAP, :].reshape(16 * CAP, D).astype(BF)
            out = dot(pick.reshape(16 * CAP, T).T.astype(BF), mine)
            out = out + dot(hpick.T.astype(BF), hot_rows[o].astype(BF))
            outs[o][...] = out.astype(BF)

    return pl.pallas_call(
        kernel,
        in_specs=[pl.BlockSpec(memory_space=pltpu.SMEM)]
        + [pl.BlockSpec(memory_space=pltpu.VMEM)] * 3,
        out_shape=[jax.ShapeDtypeStruct((T, D), BF)] * n,
        cost_estimate=pl.CostEstimate(
            flops=75_000_000 * n, bytes_accessed=1_000_000 * n, transcendentals=0
        ),
        compiler_params=VMEM,
        name=f"merge_plain_{n}",
    )(scal, meta, rows, hot_rows)


def silu_slope(pre):
    sig = jax.nn.sigmoid(pre)
    return sig * (1.0 + pre * (1.0 - sig))


def hot_kernel(rows_in, rows_cot, weights, out, back, grads):
    x = rows_in[...].reshape(NZ * HOT, D)
    c = rows_cot[...].reshape(NZ * HOT, D)
    gate_w = weights[0, 0:SLICE, :]
    up_w = weights[0, SLICE : 2 * SLICE, :]
    down_w = weights[0, 2 * SLICE : 3 * SLICE, :]
    pre_gate = dot_t(x, gate_w)
    pre_up = dot_t(x, up_w)
    sig = 1.0 / (1.0 + jnp.exp(-pre_gate))
    active = pre_gate * sig
    hidden = active * pre_up
    out[...] = dot(hidden.astype(BF), down_w).reshape(NZ, HOT, D)
    grad_hidden = dot_t(c, down_w)
    grad_pg = grad_hidden * pre_up * (sig * (1.0 + pre_gate * (1.0 - sig)))
    grad_pu = grad_hidden * active
    back[...] = (dot(grad_pg.astype(BF), gate_w) + dot(grad_pu.astype(BF), up_w)).reshape(NZ, HOT, D)
    grads[0, 0:SLICE, :] = dot(grad_pg.T.astype(BF), x)
    grads[0, SLICE : 2 * SLICE, :] = dot(grad_pu.T.astype(BF), x)
    grads[0, 2 * SLICE : 3 * SLICE, :] = dot(hidden.T.astype(BF), c)


def hot_pass(hot_in, hot_cot, weights):
    rows = jax.ShapeDtypeStruct((NZ, 2 * HOT, D), F32)
    return pl.pallas_call(
        hot_kernel,
        grid=(2,),
        in_specs=[
            pl.BlockSpec((NZ, HOT, D), lambda h: (0, h, 0)),
            pl.BlockSpec((NZ, HOT, D), lambda h: (0, h, 0)),
            pl.BlockSpec((1, 3 * SLICE, D), lambda h: (h, 0, 0)),
        ],
        out_specs=[
            pl.BlockSpec((NZ, HOT, D), lambda h: (0, h, 0)),
            pl.BlockSpec((NZ, HOT, D), lambda h: (0, h, 0)),
            pl.BlockSpec((1, 3 * SLICE, D), lambda h: (h, 0, 0)),
        ],
        out_shape=[rows, rows, jax.ShapeDtypeStruct((2, 3 * SLICE, D), F32)],
        cost_estimate=pl.CostEstimate(flops=600_000_000, bytes_accessed=6_000_000, transcendentals=20_000),
        compiler_params=VMEM,
        name="hot_pass",
    )(hot_in, hot_cot, weights)


def choose_kernel(is_hot, hot, gate, up, down, out_gate, out_up, out_down):
    @pl.when(is_hot[0] == 0)
    def _():
        out_gate[...] = gate[...]
        out_up[...] = up[...]
        out_down[...] = down[...]

    @pl.when(is_hot[0] == 1)
    def _():
        slices = [hot[i].astype(F32) for i in range(NZ)]

        def whole(k):
            return jnp.concatenate([v[SLICE * k : SLICE * k + SLICE] for v in slices], axis=0)

        out_gate[...] = whole(0).T
        out_up[...] = whole(1).T
        out_down[...] = whole(2)


def choose(is_hot, hot, gate, up, down):
    return pl.pallas_call(
        choose_kernel,
        in_specs=[pl.BlockSpec(memory_space=pltpu.SMEM)]
        + [pl.BlockSpec(memory_space=pltpu.VMEM)] * 4,
        out_shape=[jax.ShapeDtypeStruct(v.shape, F32) for v in (gate, up, down)],
        cost_estimate=pl.CostEstimate(flops=1_000_000, bytes_accessed=6_000_000, transcendentals=0),
        compiler_params=VMEM,
        name="choose",
    )(is_hot, hot, gate, up, down)


def up(v):
    return lax.ppermute(v, "z", [(i, (i + 1) % NZ) for i in range(NZ)])


def down(v):
    return lax.ppermute(v, "z", [((i + 1) % NZ, i) for i in range(NZ)])


def tie(v, *others):
    return lax.optimization_barrier((v, *others))[0]


def ring_gather(v, *others):
    below, above = [v], [v]
    for step in range(4):
        last = tie(below[-1], *others) if step == 3 and others else below[-1]
        below.append(up(last))
        if step < 3:
            above.append(down(above[-1]))
    return below[:0:-1] + above


def add(a, b):
    return (a.astype(F32) + b.astype(F32)).astype(BF)


def ring_sum(parts, other):
    rising, falling = up(parts[0]), down(parts[1])
    for step in range(3):
        if step == 1:
            rising = tie(rising, other)
        rising = up(add(rising, parts[7 - step]))
        if step < 2:
            falling = down(add(falling, parts[2 + step]))
    return (parts[4].astype(F32) + rising.astype(F32) + falling.astype(F32)).astype(BF)


def swap(v):
    return lax.ppermute(v, "dp", [(0, 1), (1, 0)])


def half_sum(v, dp, dim):
    size = v.shape[dim] // 2
    mine = lax.dynamic_slice_in_dim(v, dp * size, size, dim)
    other = lax.dynamic_slice_in_dim(v, (1 - dp) * size, size, dim)
    return mine + swap(other)


def exchange(v, axes):
    return lax.all_to_all(v, axes, split_axis=0, concat_axis=0, tiled=True)


def shards(tokens, cotangent, route, numer, w_gate, w_up, w_down):
    dp = lax.axis_index("dp")
    z = lax.axis_index("z")
    me = z * 16 + lax.axis_index("x") * 4 + lax.axis_index("y")
    gate_w, up_w, down_w = w_gate[0], w_up[0], w_down[0]
    plane = ("x", "y")

    pay, info = pl.pallas_call(
        send_kernel,
        out_shape=[
            jax.ShapeDtypeStruct((PAY, D), BF),
            jax.ShapeDtypeStruct((8, T), jnp.int32),
        ],
        cost_estimate=pl.CostEstimate(flops=10_000_000, bytes_accessed=700_000, transcendentals=0),
        compiler_params=VMEM,
        name="send",
    )(tokens, route.T, numer.T)
    first, second = info[0, 0], info[1, 0]
    places_z = [lax.rem(z + g + 4, NZ) for g in ORDER]
    scal = jnp.stack([first, second, z * 16, *places_z]).astype(jnp.int32)

    wcat = jnp.concatenate(
        [w.reshape(NZ, SLICE, D) for w in (gate_w.T, up_w.T, down_w)], axis=1
    )
    wcat = lax.dynamic_index_in_dim(wcat.reshape(NZ, 2, PIECE, D), dp, 1, keepdims=False)
    wcat = wcat.reshape(NZ, 2, PIECE // 2, 8, T).transpose(1, 3, 0, 2, 4)
    plane_w = exchange(wcat.reshape(16, NZ * PIECE // 2, T), plane)

    def pick(v, i):
        return lax.dynamic_index_in_dim(v, i, 0, keepdims=False)

    pair = [
        pick(plane_w, lax.rem(e, 16)).reshape(NZ, PIECE // 2, T) for e in (first, second)
    ]
    pair = exchange(jnp.concatenate(pair, axis=1), "z")
    piece = jnp.concatenate(
        [pick(pair, first // 16)[: PIECE // 2], pick(pair, second // 16)[PIECE // 2 :]]
    )
    piece = jnp.pad(piece.reshape(9, D), ((0, EXTRA - 9), (0, 0)))

    cots = lax.all_gather(cotangent, "z")
    ring = ring_gather(pay, plane_w)
    sent_in, hot_in, meta = send_part(scal, piece, [ring[g] for g in ORDER])
    recv_in = exchange(sent_in, plane)

    sent_cot, hot_cot = send_cots(scal, meta, cots)
    sent_cot, recv_in = lax.optimization_barrier((sent_cot, recv_in))
    recv_cot = exchange(sent_cot, plane)

    hot_w = recv_in[:, 64:73].reshape(2, 8, 2, PIECE // 2, T).transpose(2, 0, 3, 1, 4)
    hot_w = hot_w.reshape(2, PIECE, D)
    other_w = swap(hot_w)
    hot_w = jnp.where(
        dp == 0,
        jnp.concatenate([hot_w, other_w], axis=1),
        jnp.concatenate([other_w, hot_w], axis=1),
    )
    hot_out, hot_back, hot_grads = hot_pass(hot_in, hot_cot, hot_w)
    hot_g = half_sum(hot_grads.reshape(2 * 3 * SLICE, D), dp, 1).astype(BF)
    hot_g = jnp.concatenate([hot_g[: 3 * SLICE], hot_g[3 * SLICE :]], axis=1).reshape(16, 9, D)
    hot_g = jnp.pad(hot_g, ((0, 0), (0, EXTRA - 9), (0, 0)))

    rows_in = tie(recv_in, other_w)[:, :64].reshape(T * CAP, D)
    pre_gate = dot(rows_in, gate_w)
    pre_up = dot(rows_in, up_w)
    active = jax.nn.silu(pre_gate)
    hidden = (active * pre_up).astype(BF)
    result = dot(hidden, down_w).astype(BF)
    sent_out = jnp.concatenate([result.reshape(16, 64, D), hot_g], axis=1)
    sent_out, recv_cot = lax.optimization_barrier((sent_out, recv_cot))
    back_out = exchange(sent_out, plane)

    rows_cot = recv_cot.reshape(T * CAP, D)
    grad_hidden = dot_t(rows_cot, down_w)
    grad_pg = (grad_hidden * pre_up * silu_slope(pre_gate)).astype(BF)
    grad_pu = (grad_hidden * active).astype(BF)
    back = (dot_t(grad_pg, gate_w) + dot_t(grad_pu, up_w)).astype(BF)
    hot_g = jnp.sum(back_out[:, 64:73].astype(F32), axis=0).astype(BF)
    hot_g = jnp.where((jnp.arange(NZ) == z)[:, None, None], hot_g[None], jnp.zeros((), BF))
    hot_g = jnp.pad(hot_g.reshape(9 * NZ, D), ((0, RIDE - 9 * NZ), (0, 0)))
    total = merge_gated(scal, meta, back_out, hot_out, hot_g)
    back, total = lax.optimization_barrier((back, total))
    back_grad = exchange(back.reshape(16, 64, D), plane)

    summed = lax.psum_scatter(
        total.reshape(NZ * (T + RIDE), D), "z", scatter_dimension=0, tiled=True
    )
    output = summed[:T]
    merged = merge_plain(scal, meta, back_grad, hot_back)
    grad_tokens = ring_sum([merged[ORDER.index(g)] for g in range(NZ)], summed)

    hot_g = summed[T : T + 9 * NZ].reshape(NZ, 9, D)
    for_first = (jnp.arange(16) == lax.rem(first, 16)) & (first // 16 == z)
    hot_g = jnp.where(
        for_first[:, None, None, None], hot_g[None, :, :, : D // 2], hot_g[None, :, :, D // 2 :]
    )
    hot_g = exchange(hot_g.reshape(16, 9 * NZ, D // 2), plane)
    hot_g = hot_g.reshape(16, NZ, 9, D // 2).transpose(1, 0, 2, 3)
    hot_g = hot_g.reshape(NZ, 3 * SLICE, D // 2)
    is_hot = ((me == first) | (me == second)).astype(jnp.int32)

    def grad(a, b):
        return lax.dot_general(a, b, (((0,), (0,)), ((), ())), preferred_element_type=F32)

    cold_gate = half_sum(grad(rows_in, grad_pg), dp, 0)
    cold_up = half_sum(grad(rows_in, grad_pu), dp, 0)
    cold_down = half_sum(grad(hidden, rows_cot), dp, 1)
    grad_gate, grad_up, grad_down = choose(is_hot[None], hot_g, cold_gate, cold_up, cold_down)
    return (output, grad_tokens, grad_gate[None], grad_up[None], grad_down[None])


def solution(mesh):
    cube = Mesh(mesh.devices.reshape(2, 8, 4, 4), ("dp", "z", "x", "y"))
    owner = ("z", "x", "y")
    rows = P(("dp", "z", "x", "y"), None)
    weights = P(owner, None, None)
    return jax.shard_map(
        shards,
        mesh=cube,
        in_specs=(rows, rows, rows, rows, weights, weights, weights),
        out_specs=(
            rows,
            rows,
            P(owner, "dp", None),
            P(owner, "dp", None),
            P(owner, None, "dp"),
        ),
        check_vma=False,
    )
```
